32 devices in a mesh: ctx: 8 (over z, y), wa: 4 (over x, core).
Axes of the slice: x: 2, y: 2, z: 4, core: 2. Of those that a mesh axis runs over, the one named last changes fastest.
Arguments:
- inputs: bfloat16 [4096, 1152], P('ctx'), may hold values from -6 to 6
- cotangent: bfloat16 [4096, 1152], P('ctx'), may hold values from -6 to 6
- segments: int32 [4096], replicated, may hold values from 0 to 16, as said below
- pair_order: int32 [8], replicated, may hold values from 0 to 7, as said below
- gain_attn: bfloat16 [1152], P(('ctx', 'wa')), may hold values from 0.099609375 to 1.8984375
- w_query: bfloat16 [1152, 1152], P(('ctx', 'wa')), may hold values from -0.1875 to 0.1875
- w_key: bfloat16 [1152, 384], P(('ctx', 'wa')), may hold values from -0.1875 to 0.1875
- w_value: bfloat16 [1152, 384], P(('ctx', 'wa')), may hold values from -0.1875 to 0.1875
- w_out: bfloat16 [1152, 1152], P(None, ('ctx', 'wa')), may hold values from -1 to 1
- gain_mlp: bfloat16 [1152], P('ctx'), may hold values from 0.099609375 to 1.8984375
- w_gate: bfloat16 [1152, 3072], P('ctx', 'wa'), may hold values from -0.1875 to 0.1875
- w_up: bfloat16 [1152, 3072], P('ctx', 'wa'), may hold values from -0.1875 to 0.1875
- w_down: bfloat16 [3072, 1152], P('wa', 'ctx'), may hold values from -0.21875 to 0.21875
Outputs:
- output: bfloat16 [4096, 1152], P('ctx')
- grad_inputs: bfloat16 [4096, 1152], P('ctx')
- grad_gain_attn: float32 [1152], P(('ctx', 'wa'))
- grad_w_query: float32 [1152, 1152], P(('ctx', 'wa'))
- grad_w_key: float32 [1152, 384], P(('ctx', 'wa'))
- grad_w_value: float32 [1152, 384], P(('ctx', 'wa'))
- grad_w_out: float32 [1152, 1152], P(None, ('ctx', 'wa'))
- grad_gain_mlp: float32 [1152], P('ctx')
- grad_w_gate: float32 [1152, 3072], P('ctx', 'wa')
- grad_w_up: float32 [1152, 3072], P('ctx', 'wa')
- grad_w_down: float32 [3072, 1152], P('wa', 'ctx')
The draws below stay inside these ranges and needn't reach their ends.
Inputs may be any that keep to these rules, and one draw needn't show every extreme that they name: A permutation: index j of ctx holds blocks pair_order[j] and 2 N - 1 - pair_order[j] of the sequence's 2 N blocks of 256 tokens, N = 8. `segments`: taken in order of positions, document numbers start at 1, never fall and each of 1 to 16 is present; then a final run of one or more padding tokens has 0.
All inputs are finite; a program needn't handle non-finite values.
Results may differ from the reference program's by a relative error of at most 0.015.
Values may be sent and summed in bfloat16 or wider, within the bound.
No kernel may reach another device: no remote copies, remote signals or barrier semaphores. Data moves between devices by JAX's collectives and lax.ppermute only.
A program may use at most 256 MiB of HBM per device.

```python
import math
import jax
import jax.numpy as jnp
from jax import lax

D = 1152
HEADS = 18
KV_HEADS = 6
HEAD = 64
FF = 3072
TOK_DEV = 512
DOCS = 16
TOKENS = 4096
N_WA = 4


def pair_table(key):
    return jax.random.permutation(jax.random.fold_in(key, 11), TOKENS // TOK_DEV).astype(jnp.int32)


def draw_pair_order(key, part):
    return pair_table(key)


def draw_segments(key, part):
    total_rows = TOKENS
    half_rows = TOK_DEV // 2
    piece_rows = half_rows // N_WA
    pair_count = TOKENS // TOK_DEV
    padding = jax.random.randint(jax.random.fold_in(key, 41), (), 1, half_rows + 1).astype(jnp.int32)
    live_rows = total_rows - padding
    mantissa = jax.random.randint(jax.random.fold_in(key, 23), (DOCS,), 1, 4).astype(jnp.int32)
    exponent = jax.random.randint(jax.random.fold_in(key, 29), (DOCS,), 0, 2).astype(jnp.int32)
    heaviest = jax.random.randint(jax.random.fold_in(key, 31), (), 0, DOCS).astype(jnp.int32)
    small_weight = (mantissa * jnp.left_shift(jnp.ones_like(exponent), exponent)).astype(jnp.int32)
    doc_index = jnp.arange(DOCS, dtype=jnp.int32)
    doc_weight = jnp.where(doc_index == heaviest, 448, small_weight).astype(jnp.int32)
    before = (jnp.cumsum(doc_weight) - doc_weight).astype(jnp.int32)
    weight_total = jnp.sum(doc_weight).astype(jnp.int32)
    doc_starts = (doc_index + before * (live_rows - DOCS) // weight_total).astype(jnp.int32)
    places = jnp.arange(total_rows, dtype=jnp.int32)
    in_order = jnp.sum((doc_starts[None, :] <= places[:, None]).astype(jnp.int32), 1)
    in_order = jnp.where(places >= live_rows, 0, in_order)
    order_table = pair_table(key)
    device = places // TOK_DEV
    within = places % TOK_DEV
    slot_index = within // (2 * piece_rows)
    inner = within % (2 * piece_rows)
    lower_block = order_table[device]
    block_index = jnp.where(inner < piece_rows, lower_block, 2 * pair_count - 1 - lower_block)
    dealt = block_index * half_rows + slot_index * piece_rows + inner % piece_rows
    return in_order[dealt].astype(jnp.int32)


def block_levels(key, shape, pieces, smallest, largest):
    level = 1.0
    for dim, blocks in pieces:
        draws = jax.random.uniform(jax.random.fold_in(jax.random.fold_in(key, 6), dim), (blocks,), jnp.float32, smallest / len(pieces), largest / len(pieces))
        level = level * jnp.repeat(jnp.exp(draws), shape[dim] // blocks).reshape((-1,) + (1,) * (len(shape) - 1 - dim))
    return level


def gaussian(stream_key, extent, scale, limit, pieces=(), held_as=jnp.bfloat16):
    values = jax.random.normal(stream_key, extent, jnp.float32) * scale
    if len(pieces) > 0:
        values = block_levels(stream_key, extent, pieces, -0.22, 0.18) * values
    return jnp.clip(values, min=-limit, max=limit).astype(held_as)


def setup_inputs(seed: int = 0) -> dict:
    keys = jax.random.split(jax.random.key(seed), 14)
    return {
        "inputs": gaussian(keys[0], (TOKENS, D), 1.0, 6.0, ((0, 8),)),
        "cotangent": gaussian(keys[1], (TOKENS, D), 1.0, 6.0, ((0, 8),)),
        "segments": draw_segments(jax.random.fold_in(keys[13], 71), 0),
        "pair_order": draw_pair_order(jax.random.fold_in(keys[13], 71), 0),
        "gain_attn": jnp.clip(1.0 + 0.18 * jax.random.normal(keys[4], (D,), jnp.float32), 0.099609375, 1.8984375).astype(jnp.bfloat16),
        "w_query": gaussian(keys[5], (D, HEADS * HEAD), D ** -0.5, 0.1875, ((0, 32),)),
        "w_key": gaussian(keys[6], (D, KV_HEADS * HEAD), D ** -0.5, 0.1875, ((0, 32),)),
        "w_value": gaussian(keys[7], (D, KV_HEADS * HEAD), D ** -0.5, 0.1875, ((0, 32),)),
        "w_out": gaussian(keys[8], (HEADS * HEAD, D), (HEADS * HEAD // 32) ** -0.5, 1.0, ((1, 32),)),
        "gain_mlp": jnp.clip(1.0 + 0.18 * jax.random.normal(keys[9], (D,), jnp.float32), 0.099609375, 1.8984375).astype(jnp.bfloat16),
        "w_gate": gaussian(keys[10], (D, FF), D ** -0.5, 0.1875, ((0, 8), (1, 4))),
        "w_up": gaussian(keys[11], (D, FF), D ** -0.5, 0.1875, ((0, 8), (1, 4))),
        "w_down": gaussian(keys[12], (FF, D), (FF // 4) ** -0.5, 0.21875, ((0, 4), (1, 8))),
    }


HIGHEST = lax.Precision.HIGHEST
epsilon = 1e-05
rope_base = 10000.0
masked_score = -1e+30

@jax.custom_vjp
def low(v):
    return lax.optimization_barrier(v.astype(jnp.bfloat16)).astype(jnp.float32)

@jax.custom_vjp
def low_back(v):
    return v

def low_keep(v):
    return (low(v), None)

def low_pass(kept, grad):
    return (grad,)

def back_keep(v):
    return (v, None)

def back_low(kept, grad):
    return (low(grad),)
low.defvjp(low_keep, low_pass)
low_back.defvjp(back_keep, back_low)

def dealt_positions(pair_order, rows_dev, split_count):
    pair_count = pair_order.shape[0]
    row_index = jnp.arange(pair_count * rows_dev, dtype=jnp.int32)
    device = row_index // rows_dev
    within = row_index % rows_dev
    half_rows = rows_dev // 2
    piece_rows = half_rows // split_count
    slot_index = within // (2 * piece_rows)
    inner = within % (2 * piece_rows)
    lower_block = pair_order[device]
    block_index = jnp.where(inner < piece_rows, lower_block, 2 * pair_count - 1 - lower_block)
    return (block_index * half_rows + slot_index * piece_rows + inner % piece_rows).astype(jnp.int32)

def rms_norm(inputs, gain):
    mean_square = lax.optimization_barrier(jnp.mean(inputs * inputs, -1, keepdims=True))
    return inputs * lax.rsqrt(mean_square + epsilon) * gain

def rotary_tables(positions, head_size):
    half_size = head_size // 2
    frequency = jnp.exp(-math.log(rope_base) * 2.0 * jnp.arange(half_size, dtype=jnp.float32) / head_size)
    angles = positions.astype(jnp.float32)[:, None] * frequency[None, :]
    cosine = jnp.concatenate([jnp.cos(angles), jnp.cos(angles)], -1)
    sine_table = jnp.concatenate([jnp.sin(angles), jnp.sin(angles)], -1)
    return (cosine, sine_table)

def rotate(values, cosine, sine_table):
    half_size = values.shape[-1] // 2
    turned = jnp.concatenate([-values[..., half_size:], values[..., :half_size]], -1)
    return values * cosine[:, None, :] + turned * sine_table[:, None, :]

def attend_raw(queries, query_pos, query_seg, key_rows, value_rows, key_pos, key_seg):
    score_scale = queries.shape[-1] ** (-0.5)
    scores = low_back(jnp.einsum('qgd,kd->gqk', queries, key_rows, precision=HIGHEST) * score_scale)
    allowed = (key_pos[None, :] <= query_pos[:, None]) & (key_seg[None, :] == query_seg[:, None])
    allowed = allowed & ((query_seg[:, None] > 0) | (key_pos[None, :] == query_pos[:, None]))
    scores = jnp.where(allowed[None], scores, masked_score)
    log_total = jax.nn.logsumexp(scores, axis=-1, keepdims=True)
    weights_soft = low(jnp.exp(scores - log_total))
    return jnp.einsum('gqk,kd->qgd', weights_soft, value_rows, precision=HIGHEST)

def attend_block(queries, query_pos, query_seg, key_rows, value_rows, key_pos, key_seg):
    return jax.checkpoint(attend_raw)(queries, query_pos, query_seg, key_rows, value_rows, key_pos, key_seg)

def attention(queries, key_rows, value_rows, positions, segments):
    total_rows = queries.shape[0]
    block_rows = min(512, total_rows)
    block_count = total_rows // block_rows
    pos_blocks = positions.reshape(block_count, block_rows)
    seg_blocks = segments.reshape(block_count, block_rows)

    def per_head(head_item):
        head_queries, head_keys, head_values = head_item

        def per_block(block_item):
            return attend_block(block_item[0], block_item[1], block_item[2], head_keys, head_values, positions, segments)
        shaped = head_queries.reshape((block_count, block_rows) + head_queries.shape[1:])
        blocks_out = lax.map(per_block, (shaped, pos_blocks, seg_blocks))
        return blocks_out.reshape(head_queries.shape)
    result = lax.map(per_head, (jnp.transpose(queries, (1, 0, 2, 3)), jnp.transpose(key_rows, (1, 0, 2)), jnp.transpose(value_rows, (1, 0, 2))))
    return jnp.transpose(result, (1, 0, 2, 3))

def block_forward(params, positions, segments):
    inputs, gain_attn, w_query, w_key, w_value, w_out, gain_mlp, w_gate, w_up, w_down = params
    total_rows = inputs.shape[0]
    group_size = HEADS // KV_HEADS
    normed = low(rms_norm(inputs, gain_attn))
    cosine, sine_table = rotary_tables(positions, HEAD)
    query_lin = low_back(jnp.dot(normed, w_query, precision=HIGHEST)).reshape(total_rows, HEADS, HEAD)
    queries = low(rotate(query_lin, cosine, sine_table))
    key_lin = low_back(jnp.dot(normed, w_key, precision=HIGHEST)).reshape(total_rows, KV_HEADS, HEAD)
    key_rows = low(rotate(key_lin, cosine, sine_table))
    value_rows = low_back(low(jnp.dot(normed, w_value, precision=HIGHEST))).reshape(total_rows, KV_HEADS, HEAD)
    mixed_heads = attention(queries.reshape(total_rows, KV_HEADS, group_size, HEAD), key_rows, value_rows, positions, segments)
    mixed_heads = low_back(low(mixed_heads.reshape(total_rows, HEADS * HEAD)))
    hidden = inputs + low_back(jnp.dot(mixed_heads, w_out, precision=HIGHEST))
    normed_mlp = low(rms_norm(hidden, gain_mlp))
    gate_pre = low_back(jnp.dot(normed_mlp, w_gate, precision=HIGHEST))
    upward = low_back(jnp.dot(normed_mlp, w_up, precision=HIGHEST))
    active = low(jax.nn.silu(gate_pre) * upward)
    return hidden + low_back(jnp.dot(active, w_down, precision=HIGHEST))

def reference(inputs, cotangent, segments, pair_order, gain_attn, w_query, w_key, w_value, w_out, gain_mlp, w_gate, w_up, w_down):
    positions = dealt_positions(pair_order, TOK_DEV, N_WA)
    floats = (inputs.astype(jnp.float32), gain_attn.astype(jnp.float32), w_query.astype(jnp.float32), w_key.astype(jnp.float32), w_value.astype(jnp.float32), w_out.astype(jnp.float32), gain_mlp.astype(jnp.float32), w_gate.astype(jnp.float32), w_up.astype(jnp.float32), w_down.astype(jnp.float32))

    def forward(params):
        return block_forward(params, positions, segments)
    output, pull_back = jax.vjp(forward, floats)
    gradients = pull_back(cotangent.astype(jnp.float32))[0]
    return (output.astype(jnp.bfloat16), gradients[0].astype(jnp.bfloat16), gradients[1], gradients[2], gradients[3], gradients[4], gradients[5], gradients[6], gradients[7], gradients[8], gradients[9])
```

```python
import functools
import math

import jax
import jax.numpy as jnp
from jax import lax
from jax.experimental import pallas as pl
from jax.experimental.pallas import tpu as pltpu
from jax.sharding import PartitionSpec as P

HEADS = 18
KV_HEADS = 6
HEAD = 64
GROUP = HEADS // KV_HEADS
HALF_Q = HEADS * HEAD // 2
HALF_KV = KV_HEADS * HEAD // 2
HALF_GROUPS = KV_HEADS // 2
SLAB = 128
PACK = 2 * HALF_KV + HALF_Q + HEAD
Q_WIDE = HALF_Q + HEAD

epsilon = 1e-05
rope_base = 10000.0
masked_score = -1e30
f32 = jnp.float32
bf16 = jnp.bfloat16
VMEM_BYTES = 58 * 1024 * 1024

K_PLACE = [divmod(g, 2) for g in range(HALF_GROUPS)]
V_PLACE = [divmod(HALF_GROUPS + g, 2) for g in range(HALF_GROUPS)]


def vmem():
    return pl.BlockSpec(memory_space=pltpu.VMEM)


def smem():
    return pl.BlockSpec(memory_space=pltpu.SMEM)


def params():
    return pltpu.CompilerParams(vmem_limit_bytes=VMEM_BYTES)


def dot(a, b, ca=1, cb=0):
    return lax.dot_general(a, b, (((ca,), (cb,)), ((), ())), preferred_element_type=f32)


def ctx_parts(n):
    slow = min(4, n)
    return slow, n // slow


def ctx_swap(block, n, k):
    return lax.ppermute(block, "ctx", [(i, i ^ k) for i in range(n)])


def wa_swap(block, k):
    return lax.ppermute(block, "wa", [(i, i ^ k) for i in range(4)])


def core_swap(block):
    return wa_swap(block, 1)


def x_swap(block):
    return wa_swap(block, 2)


def gather_relative(block, n):
    slow, fast = ctx_parts(n)
    found = {0: block}
    for kz in range(1, slow):
        found[kz * fast] = ctx_swap(block, n, kz * fast)
    for kz in range(slow):
        for r in range(1, fast):
            found[kz * fast + r] = ctx_swap(found[kz * fast], n, r)
    return [found[k] for k in range(n)]


def gather_absolute(block, n):
    own = lax.axis_index("ctx")
    blocks = gather_relative(block, n)
    whole = jnp.zeros((n,) + block.shape, block.dtype)
    for k in range(n):
        whole = lax.dynamic_update_index_in_dim(whole, blocks[k], own ^ k, 0)
    return whole


def scatter_sum(terms, n):
    slow, fast = ctx_parts(n)
    sums = [terms(kz * fast) for kz in range(slow)]
    for r in range(1, fast):
        sent = jnp.stack([terms(kz * fast + r) for kz in range(slow)]).astype(bf16)
        came = ctx_swap(sent, n, r)
        sums = [sums[kz] + came[kz].astype(f32) for kz in range(slow)]
    total = sums[0]
    for kz in range(1, slow):
        total = total + ctx_swap(sums[kz].astype(bf16), n, kz * fast).astype(f32)
    return total


def lane_half(shape):
    lane = lax.broadcasted_iota(jnp.int32, shape, 1)
    return lane // HEAD


def turn(z):
    lane = lax.broadcasted_iota(jnp.int32, z.shape, 1)
    return jnp.where(
        lane % HEAD < HEAD // 2,
        pltpu.roll(z, SLAB - HEAD // 2, 1),
        pltpu.roll(z, HEAD // 2, 1),
    )


def project_kernel(x_ref, gain_ref, w_ref, cos_ref, sin_ref, normed_ref, q_ref, kv_ref):
    x = x_ref[...].astype(f32)
    scale_rows = lax.rsqrt(jnp.mean(x * x, -1, keepdims=True) + epsilon)
    normed = (x * scale_rows * gain_ref[...]).astype(bf16)
    normed_ref[...] = normed
    cosine, sine = cos_ref[...], sin_ref[...]
    half = lane_half(cosine.shape)
    for s in range(PACK // SLAB):
        z = dot(normed, w_ref[:, s * SLAB : (s + 1) * SLAB])
        if s == 2:
            kv_ref[:, 2 * SLAB : 3 * SLAB] = z.astype(bf16)
            continue
        turned = z * cosine + turn(z) * sine
        if s == 0:
            kv_ref[:, :SLAB] = turned.astype(bf16)
        elif s == 1:
            kv_ref[:, SLAB : 2 * SLAB] = jnp.where(half == 0, turned, z).astype(bf16)
        else:
            scaled = turned * HEAD ** (-0.5)
            if s == PACK // SLAB - 1:
                scaled = jnp.where(half == 0, scaled, 0.0)
            q_ref[:, (s - 3) * SLAB : (s - 2) * SLAB] = scaled.astype(bf16)


def head_rows(ref, run, rows, g, place):
    parts = []
    for j in range(GROUP):
        slab, half = divmod(GROUP * g + j, 2)
        z = ref[run * rows : (run + 1) * rows, slab * SLAB : (slab + 1) * SLAB].astype(f32)
        if half != place:
            z = pltpu.roll(z, HEAD, 1)
        parts.append(jnp.where(lane_half(z.shape) == place, z, 0.0).astype(bf16))
    return jnp.concatenate(parts, 0)


def put_heads(ref, values, run, rows, g, place):
    flat = values.T
    for j in range(GROUP):
        slab, half = divmod(GROUP * g + j, 2)
        z = flat[j * rows : (j + 1) * rows, :]
        if half != place:
            z = pltpu.roll(z, HEAD, 1)
        where = (slice(run * rows, (run + 1) * rows), slice(slab * SLAB, (slab + 1) * SLAB))
        if half == 0:
            ref[where] = jnp.where(lane_half(z.shape) == 0, z, 0.0)
        else:
            ref[where] = jnp.where(lane_half(z.shape) == 1, z, ref[where])


def key_block(own_ref, other_ref, slot, rows, slab):
    at = pl.ds(pl.multiple_of(slot * rows, rows), rows)
    cols = slice(slab * SLAB, (slab + 1) * SLAB)
    return jnp.concatenate([own_ref[at, cols], other_ref[at, cols]], 0)


def key_places(block, core, rows, width):
    i = lax.broadcasted_iota(jnp.int32, (2 * rows, width), 0)
    mine = i + core * rows
    others = i - core * rows
    return block * (2 * rows) + jnp.where(i < rows, mine, others)


def forward_kernel(blocks, table, q_ref, own_ref, other_ref, rows_ref, mixed_ref, log_ref, s_buf):
    rows = q_ref.shape[0] // 2
    width = GROUP * rows
    core = table[blocks + 4]
    for run in range(2):
        first, last = table[blocks + 2 * run], table[blocks + 2 * run + 1]
        start = rows_ref[2 * run : 2 * run + 1, :]
        stop = rows_ref[2 * run + 1 : 2 * run + 2, :]
        for g in range(HALF_GROUPS):
            k_slab, k_half = K_PLACE[g]
            v_slab, v_half = V_PLACE[g]
            q = head_rows(q_ref, run, rows, g, k_half)

            def score_step(b, high):
                keys = key_block(own_ref, other_ref, table[b], rows, k_slab)
                s = dot(keys, q, 1, 1)
                at = key_places(b, core, rows, width)
                s = jnp.where((at >= start) & (at <= stop), s, masked_score)
                s_buf[pl.ds(pl.multiple_of((b - first) * 2 * rows, 2 * rows), 2 * rows), :] = s
                return jnp.maximum(high, jnp.max(s.reshape(-1, 8, width), 0))

            high = lax.fori_loop(first, last, score_step, jnp.full((8, width), masked_score, f32))
            high = jnp.max(high, 0, keepdims=True)

            def mix_step(b, state):
                total, mixed = state
                s = s_buf[pl.ds(pl.multiple_of((b - first) * 2 * rows, 2 * rows), 2 * rows), :]
                p = jnp.exp(s - high)
                total = total + jnp.sum(p.reshape(-1, 8, width), 0)
                values = key_block(own_ref, other_ref, table[b], rows, v_slab)
                return total, mixed + dot(values, p.astype(bf16), 0, 0)

            total, mixed = lax.fori_loop(
                first, last, mix_step, (jnp.zeros((8, width), f32), jnp.zeros((SLAB, width), f32))
            )
            total = jnp.sum(total, 0, keepdims=True)
            log_ref[run * HALF_GROUPS + g : run * HALF_GROUPS + g + 1, :] = high + jnp.log(total)
            put_heads(mixed_ref, mixed * (1.0 / total), run, rows, g, v_half)


def backward_kernel(
    blocks, table, q_ref, own_ref, other_ref, rows_ref, mixed_ref, log_ref, grad_ref, cos_ref, sin_ref,
    dq_ref, down_ref, dother_ref, dq_buf, raw_buf,
):
    rows = q_ref.shape[0] // 2
    width = GROUP * rows
    core = table[blocks + 4]
    down_ref[...] = jnp.zeros_like(down_ref)
    dother_ref[...] = jnp.zeros_like(dother_ref)
    for run in range(2):
        first, last = table[blocks + 2 * run], table[blocks + 2 * run + 1]
        start = rows_ref[2 * run : 2 * run + 1, :]
        stop = rows_ref[2 * run + 1 : 2 * run + 2, :]
        queries, grads, logs, deltas = [], [], [], []
        for g in range(HALF_GROUPS):
            queries.append(head_rows(q_ref, run, rows, g, K_PLACE[g][1]))
            grads.append(head_rows(grad_ref, run, rows, g, V_PLACE[g][1]))
            logs.append(log_ref[run * HALF_GROUPS + g : run * HALF_GROUPS + g + 1, :])
            parts = []
            for j in range(GROUP):
                slab, half = divmod(GROUP * g + j, 2)
                where = (slice(run * rows, (run + 1) * rows), slice(slab * SLAB, (slab + 1) * SLAB))
                z = grad_ref[where].astype(f32) * mixed_ref[where]
                z = jnp.where(lane_half(z.shape) == half, z, 0.0)
                parts.append(jnp.sum(z.T, 0, keepdims=True))
            deltas.append(jnp.concatenate(parts, 1))
        dq_buf[...] = jnp.zeros_like(dq_buf)

        def step(b, carry):
            slot = table[b]
            slabs = [key_block(own_ref, other_ref, slot, rows, i) for i in range(3)]
            at = key_places(b, core, rows, width)
            ok = (at >= start) & (at <= stop)
            lefts, rights = [[], [], []], [[], [], []]
            for g in range(HALF_GROUPS):
                k_slab, v_slab = K_PLACE[g][0], V_PLACE[g][0]
                s = dot(slabs[k_slab], queries[g], 1, 1)
                p = jnp.where(ok, jnp.exp(s - logs[g]), 0.0)
                dp = dot(slabs[v_slab], grads[g], 1, 1)
                ds = (p * (dp - deltas[g])).astype(bf16)
                dq_buf[g * SLAB : (g + 1) * SLAB, :] += dot(slabs[k_slab], ds, 0, 0)
                lefts[k_slab].append(ds)
                rights[k_slab].append(queries[g])
                lefts[v_slab].append(p.astype(bf16))
                rights[v_slab].append(grads[g])
            at_slot = pl.ds(pl.multiple_of(slot * rows, rows), rows)
            for i in range(3):
                both = dot(jnp.concatenate(lefts[i], 1), jnp.concatenate(rights[i], 0))
                cols = slice(i * SLAB, (i + 1) * SLAB)
                down_ref[at_slot, cols] += both[:rows]
                dother_ref[at_slot, cols] += both[rows:]
            return carry

        lax.fori_loop(first, last, step, 0)
        for g in range(HALF_GROUPS):
            put_heads(raw_buf, dq_buf[g * SLAB : (g + 1) * SLAB, :], run, rows, g, K_PLACE[g][1])
    cosine, sine = cos_ref[...], sin_ref[...]
    for s in range(Q_WIDE // SLAB):
        z = raw_buf[:, s * SLAB : (s + 1) * SLAB] * HEAD ** (-0.5)
        dq_ref[:, s * SLAB : (s + 1) * SLAB] = (z * cosine - turn(z) * sine).astype(bf16)


def lin_grad_kernel(dkv_ref, dq_ref, cos_ref, sin_ref, out_ref):
    cosine, sine = cos_ref[...], sin_ref[...]
    half = lane_half(cosine.shape)
    z = dkv_ref[:, :SLAB]
    out_ref[:, :SLAB] = (z * cosine - turn(z) * sine).astype(bf16)
    z = dkv_ref[:, SLAB : 2 * SLAB]
    out_ref[:, SLAB : 2 * SLAB] = jnp.where(half == 0, z * cosine - turn(z) * sine, z).astype(bf16)
    out_ref[:, 2 * SLAB : 3 * SLAB] = dkv_ref[:, 2 * SLAB :].astype(bf16)
    out_ref[:, 3 * SLAB :] = dq_ref[...]


def by_runs(array, pieces):
    rows = array.shape[0]
    rest = array.shape[1:]
    axes = (0, 2, 1, 3) + tuple(4 + i for i in range(len(rest)))
    split = array.reshape((2, pieces // 2, 2, rows // (2 * pieces)) + rest)
    return jnp.transpose(split, axes).reshape((rows,) + rest)


def as_dealt(array, pieces):
    rows = array.shape[0]
    rest = array.shape[1:]
    axes = (0, 2, 1, 3) + tuple(4 + i for i in range(len(rest)))
    split = array.reshape((2, 2, pieces // 2, rows // (2 * pieces)) + rest)
    return jnp.transpose(split, axes).reshape((rows,) + rest)


def norm_backward(grad_normed, unit_rows, scale_rows, gain):
    grad_unit = grad_normed * gain
    grad_gain = jnp.sum(grad_normed * unit_rows, 0)
    grad_rows = scale_rows * (
        grad_unit - unit_rows * jnp.mean(grad_unit * unit_rows, -1, keepdims=True)
    )
    return grad_rows, grad_gain


def on_device(n, args):
    (inputs, cotangent, segments, pair_order, gain_attn, w_query, w_key, w_value, w_out, gain_mlp,
     w_gate, w_up, w_down) = args
    local_rows, model = inputs.shape
    pieces = 4
    own_rows = local_rows // 2
    run_rows = own_rows // 2
    part_rows = gain_attn.shape[0]
    ctx_rows = gain_mlp.shape[0]
    pair_rows = ctx_rows // 2
    units = w_gate.shape[1]
    blocks = 2 * n
    ctx_index = lax.axis_index("ctx")
    wa_index = lax.axis_index("wa")
    x_index, core_index = wa_index // 2, wa_index % 2

    def both_halves(array, width):
        return array[:, :width], array[:, width:]

    q_halves = both_halves(w_query, HALF_Q)
    k_halves = both_halves(w_key, HALF_KV)
    v_halves = both_halves(w_value, HALF_KV)
    gain_cols = jnp.broadcast_to(gain_attn[:, None], (part_rows, HEAD))
    in_halves = [
        jnp.concatenate([k_halves[i], v_halves[i], q_halves[i], gain_cols], 1) for i in range(2)
    ]
    out_halves = both_halves(w_out.T, HALF_Q)

    def gather_rows(halves):
        mine = jnp.where(x_index == 0, halves[0], halves[1])
        theirs = jnp.where(x_index == 0, halves[1], halves[0])
        came = x_swap(theirs)
        low = jnp.where(x_index == 0, mine, came)
        high = jnp.where(x_index == 0, came, mine)
        pair = jnp.stack([low, high])
        other = core_swap(pair)
        zero = jnp.where(core_index == 0, pair, other)
        one = jnp.where(core_index == 0, other, pair)
        quad = jnp.stack([zero, one], 1).reshape(ctx_rows, -1)
        sent = lax.dynamic_slice_in_dim(quad, core_index * pair_rows, pair_rows, 0)
        held = gather_absolute(sent, n)
        opposite = core_swap(held)
        whole = jnp.where(
            core_index == 0,
            jnp.concatenate([held, opposite], 1),
            jnp.concatenate([opposite, held], 1),
        )
        return whole.reshape(n * ctx_rows, -1)

    w_in = gather_rows(in_halves)
    gain_one = w_in[:, PACK - 1].astype(f32)[None, :]

    gain_rows = jnp.zeros((8, units), bf16).at[0, :ctx_rows].set(gain_mlp)
    mlp_pack = jnp.concatenate([w_gate, w_up, w_down.T, gain_rows], 0)
    mlp_full = lax.all_gather(mlp_pack, "ctx", axis=0, tiled=False)
    full_gate = mlp_full[:, :ctx_rows].reshape(model, units)
    full_up = mlp_full[:, ctx_rows : 2 * ctx_rows].reshape(model, units)
    full_down_t = mlp_full[:, 2 * ctx_rows : 3 * ctx_rows].reshape(model, units)
    gain_two = mlp_full[:, 3 * ctx_rows, :ctx_rows].reshape(1, model).astype(f32)

    run_inputs = by_runs(inputs, pieces)
    run_cotangent = by_runs(cotangent, pieces)
    own_start = core_index * own_rows
    x_own = lax.dynamic_slice_in_dim(run_inputs, own_start, own_rows)
    lower = pair_order[ctx_index]
    offsets = core_index * run_rows + jnp.arange(run_rows, dtype=jnp.int32)
    pos_runs = jnp.stack([lower * 2 * run_rows + offsets, (blocks - 1 - lower) * 2 * run_rows + offsets])
    positions = pos_runs.reshape(own_rows)
    seg_local = lax.dynamic_slice_in_dim(segments, ctx_index * local_rows, local_rows)
    seg_own = lax.dynamic_slice_in_dim(by_runs(seg_local, pieces), own_start, own_rows)
    earlier = (segments[None, :] > 0) & (segments[None, :] < seg_own[:, None])
    starts = jnp.sum(earlier.astype(jnp.int32), 1)
    starts = jnp.where(seg_own > 0, starts, positions)
    start_runs = starts.reshape(2, run_rows)
    rows_info = jnp.tile(
        jnp.stack([start_runs[0], pos_runs[0], start_runs[1], pos_runs[1]]), (1, GROUP)
    )
    ctx_ids = jnp.arange(n, dtype=jnp.int32)
    relative = ctx_ids ^ ctx_index
    block_ids = jnp.arange(blocks, dtype=jnp.int32)[:, None]
    slots = jnp.sum(
        jnp.where(pair_order[None, :] == block_ids, 2 * relative[None, :], 0)
        + jnp.where(blocks - 1 - pair_order[None, :] == block_ids, 2 * relative[None, :] + 1, 0),
        1,
    )
    bounds = jnp.stack(
        [
            start_runs[0, 0] // (2 * run_rows),
            lower + 1,
            start_runs[1, 0] // (2 * run_rows),
            blocks - lower,
            core_index,
        ]
    )
    table = jnp.concatenate([slots, bounds]).astype(jnp.int32)

    frequency = jnp.exp(
        -math.log(rope_base) * 2.0 * jnp.arange(HEAD // 2, dtype=f32) / HEAD
    )
    angles = positions.astype(f32)[:, None] * frequency[None, :]
    cos_half, sin_half = jnp.cos(angles), jnp.sin(angles)
    cosine = jnp.concatenate([cos_half] * 4, 1)
    sine = jnp.concatenate([-sin_half, sin_half] * 2, 1)

    normed, queries, kv_own = pl.pallas_call(
        project_kernel,
        out_shape=(
            jax.ShapeDtypeStruct((own_rows, model), bf16),
            jax.ShapeDtypeStruct((own_rows, Q_WIDE), bf16),
            jax.ShapeDtypeStruct((own_rows, 2 * HALF_KV), bf16),
        ),
        in_specs=[vmem()] * 5,
        out_specs=(vmem(),) * 3,
        compiler_params=params(),
    )(x_own, gain_one, w_in, cosine, sine)

    kv_core = jnp.concatenate(gather_relative(kv_own, n), 0)
    kv_other = core_swap(kv_core)

    mixed, log_total = pl.pallas_call(
        functools.partial(forward_kernel, blocks),
        out_shape=(
            jax.ShapeDtypeStruct((own_rows, Q_WIDE), f32),
            jax.ShapeDtypeStruct((8, GROUP * run_rows), f32),
        ),
        in_specs=[smem()] + [vmem()] * 4,
        out_specs=(vmem(),) * 2,
        scratch_shapes=[pltpu.VMEM((blocks * 2 * run_rows, GROUP * run_rows), f32)],
        compiler_params=params(),
    )(table, queries, kv_core, kv_other, rows_info)

    out_halves = lax.optimization_barrier((out_halves, kv_own))[0]
    w_out_t = gather_rows(out_halves)
    mixed_b = mixed[:, :HALF_Q].astype(bf16)
    attn_part = dot(mixed_b, w_out_t, 1, 1).astype(bf16)
    attn_came = x_swap(attn_part)
    x_f = x_own.astype(f32)
    hidden_own = x_f + (attn_part.astype(f32) + attn_came.astype(f32))
    hidden_other = core_swap(hidden_own)

    def join(own, other):
        return jnp.where(
            core_index == 0, jnp.concatenate([own, other], 0), jnp.concatenate([other, own], 0)
        )

    hidden = join(hidden_own, hidden_other)
    scale_two = lax.rsqrt(jnp.mean(hidden * hidden, -1, keepdims=True) + epsilon)
    normed_two = (hidden * scale_two * gain_two).astype(bf16)
    gate_pre = dot(normed_two, full_gate)
    upward = dot(normed_two, full_up)
    sigmoid_gate = jax.nn.sigmoid(gate_pre)
    silu_gate = gate_pre * sigmoid_gate
    active = (silu_gate * upward).astype(bf16)
    grad_active = dot(run_cotangent, full_down_t)
    grad_gate = (
        grad_active * upward * (sigmoid_gate * (1.0 + gate_pre * (1.0 - sigmoid_gate)))
    ).astype(bf16)
    grad_up = (grad_active * silu_gate).astype(bf16)
    grad_two_part = dot(grad_gate, full_gate, 1, 1) + dot(grad_up, full_up, 1, 1)

    def own_part(array):
        return lax.dynamic_slice_in_dim(array, own_start, own_rows)

    def other_part(array):
        return lax.dynamic_slice_in_dim(array, own_rows - own_start, own_rows)

    def sum_wa(part):
        chip = own_part(part) + core_swap(other_part(part).astype(bf16)).astype(f32)
        chip_b = chip.astype(bf16)
        return chip_b.astype(f32) + x_swap(chip_b).astype(f32)

    grad_normed_two = sum_wa(grad_two_part)
    mlp_part = dot(active, full_down_t, 1, 1)
    output_own = (hidden_own + sum_wa(mlp_part)).astype(bf16)
    output = as_dealt(join(output_own, core_swap(output_own)), pieces)

    d_gate = dot(normed_two, grad_gate, 0, 0).astype(bf16)
    d_up = dot(normed_two, grad_up, 0, 0).astype(bf16)
    d_down_t = dot(run_cotangent, active, 0, 0).astype(bf16)
    d_pack = jnp.concatenate(
        [a.reshape(n, ctx_rows, units) for a in (d_gate, d_up, d_down_t)], 1
    )
    d_mlp = lax.psum_scatter(d_pack, "ctx", scatter_dimension=0, tiled=False).astype(f32)
    grad_w_gate = d_mlp[:ctx_rows]
    grad_w_up = d_mlp[ctx_rows : 2 * ctx_rows]
    grad_w_down = d_mlp[2 * ctx_rows :].T

    scale_own = lax.rsqrt(jnp.mean(hidden_own * hidden_own, -1, keepdims=True) + epsilon)
    grad_rows, grad_gain_two = norm_backward(
        grad_normed_two, hidden_own * scale_own, scale_own, gain_two
    )
    grad_hidden = own_part(run_cotangent).astype(f32) + grad_rows
    grad_attn = grad_hidden.astype(bf16)
    grad_mixed = dot(grad_attn, w_out_t)
    grad_mixed = jnp.pad(grad_mixed.astype(bf16), ((0, 0), (0, HEAD)))

    dq_lin, dkv_core, dkv_other = pl.pallas_call(
        functools.partial(backward_kernel, blocks),
        out_shape=(
            jax.ShapeDtypeStruct((own_rows, Q_WIDE), bf16),
            jax.ShapeDtypeStruct(kv_core.shape, f32),
            jax.ShapeDtypeStruct(kv_core.shape, f32),
        ),
        in_specs=[smem()] + [vmem()] * 9,
        out_specs=(vmem(),) * 3,
        scratch_shapes=[
            pltpu.VMEM((HALF_GROUPS * SLAB, GROUP * run_rows), f32),
            pltpu.VMEM((own_rows, Q_WIDE), f32),
        ],
        compiler_params=params(),
    )(table, queries, kv_core, kv_other, rows_info, mixed, log_total, grad_mixed, cosine, sine)

    def scatter_rows(part):
        cols = part.shape[1]
        split = part.reshape(n, 2, pair_rows, cols)
        mine = lax.dynamic_index_in_dim(split, core_index, 1, keepdims=False)
        theirs = lax.dynamic_index_in_dim(split, 1 - core_index, 1, keepdims=False)
        chip = mine + core_swap(theirs.astype(bf16)).astype(f32)
        total = scatter_sum(
            lambda k: lax.dynamic_index_in_dim(chip, ctx_index ^ k, 0, keepdims=False), n
        )
        total_b = total.astype(bf16)
        opposite = core_swap(total_b)
        rows = jnp.where(
            core_index == 0,
            jnp.concatenate([total_b, opposite], 0),
            jnp.concatenate([opposite, total_b], 0),
        )
        quad = rows.reshape(2, 2, part_rows, cols)
        kept = lax.dynamic_index_in_dim(
            lax.dynamic_index_in_dim(quad, x_index, 0, keepdims=False), core_index, 0, keepdims=False
        )
        sent = lax.dynamic_index_in_dim(
            lax.dynamic_index_in_dim(quad, 1 - x_index, 0, keepdims=False), core_index, 0, keepdims=False
        )
        came = x_swap(sent)
        low = jnp.where(x_index == 0, kept, came).astype(f32)
        high = jnp.where(x_index == 0, came, kept).astype(f32)
        return rows, low, high

    unused_rows, out_low, out_high = scatter_rows(dot(grad_attn, mixed_b, 0, 0))
    grad_w_out = jnp.concatenate([out_low, out_high], 1).T

    dkv = dkv_core + core_swap(dkv_other.astype(bf16)).astype(f32)
    dkv = dkv.reshape(n, own_rows, 2 * HALF_KV)
    dkv_own = scatter_sum(lambda k: dkv[k], n)
    lin_grad = pl.pallas_call(
        lin_grad_kernel,
        out_shape=jax.ShapeDtypeStruct((own_rows, PACK), bf16),
        in_specs=[vmem()] * 4,
        out_specs=vmem(),
        compiler_params=params(),
    )(dkv_own, dq_lin, cosine, sine)
    lin_used = lin_grad[:, : PACK - HEAD]
    normed_part = dot(lin_used, w_in[:, : PACK - HEAD], 1, 1).astype(bf16)
    grad_normed = normed_part.astype(f32) + x_swap(normed_part).astype(f32)
    scale_one = lax.rsqrt(jnp.mean(x_f * x_f, -1, keepdims=True) + epsilon)
    input_rows, grad_gain_one = norm_backward(grad_normed, x_f * scale_one, scale_one, gain_one)
    grad_inputs_own = (grad_hidden + input_rows).astype(bf16)
    grad_inputs = as_dealt(join(grad_inputs_own, core_swap(grad_inputs_own)), pieces)

    d_in = dot(normed, lin_used, 0, 0)
    gain_pair = jnp.stack([grad_gain_one, grad_gain_two], 1)
    d_in = jnp.concatenate([d_in, jnp.pad(gain_pair, ((0, 0), (0, HEAD - 2)))], 1)
    in_rows, in_low, in_high = scatter_rows(d_in)
    k_end, v_end, q_end = HALF_KV, 2 * HALF_KV, 2 * HALF_KV + HALF_Q
    grad_w_key = jnp.concatenate([in_low[:, :k_end], in_high[:, :k_end]], 1)
    grad_w_value = jnp.concatenate([in_low[:, k_end:v_end], in_high[:, k_end:v_end]], 1)
    grad_w_query = jnp.concatenate([in_low[:, v_end:q_end], in_high[:, v_end:q_end]], 1)
    grad_gain_attn = in_low[:, q_end]
    grad_gain_mlp = in_rows[:, q_end + 1].astype(f32)
    return (
        output,
        grad_inputs,
        grad_gain_attn,
        grad_w_query,
        grad_w_key,
        grad_w_value,
        grad_w_out,
        grad_gain_mlp,
        grad_w_gate,
        grad_w_up,
        grad_w_down,
    )


def solution(mesh):
    n = mesh.shape["ctx"]

    def body(*args):
        return on_device(n, args)

    return jax.shard_map(
        body,
        mesh=mesh,
        in_specs=(
            P("ctx", None),
            P("ctx", None),
            P(),
            P(),
            P(("ctx", "wa")),
            P(("ctx", "wa"), None),
            P(("ctx", "wa"), None),
            P(("ctx", "wa"), None),
            P(None, ("ctx", "wa")),
            P("ctx"),
            P("ctx", "wa"),
            P("ctx", "wa"),
            P("wa", "ctx"),
        ),
        out_specs=(
            P("ctx", None),
            P("ctx", None),
            P(("ctx", "wa")),
            P(("ctx", "wa"), None),
            P(("ctx", "wa"), None),
            P(("ctx", "wa"), None),
            P(None, ("ctx", "wa")),
            P("ctx"),
            P("ctx", "wa"),
            P("ctx", "wa"),
            P("wa", "ctx"),
        ),
        check_vma=False,
    )
```

```python
import functools
import math

import jax
import jax.numpy as jnp
from jax import lax
from jax.experimental import pallas as pl
from jax.experimental.pallas import tpu as pltpu
from jax.sharding import PartitionSpec as P

HEADS = 18
KV_HEADS = 6
HEAD = 64
GROUP = HEADS // KV_HEADS
HALF_Q = HEADS * HEAD // 2
HALF_KV = KV_HEADS * HEAD // 2
HALF_GROUPS = KV_HEADS // 2
SLAB = 128
PACK = 2 * HALF_KV + HALF_Q + HEAD
Q_WIDE = HALF_Q + HEAD

epsilon = 1e-05
rope_base = 10000.0
masked_score = -1e30
DOCS = 16
PIECES = 4
f32 = jnp.float32
bf16 = jnp.bfloat16
VMEM_BYTES = 58 * 1024 * 1024

K_PLACE = [divmod(g, 2) for g in range(HALF_GROUPS)]
V_PLACE = [divmod(HALF_GROUPS + g, 2) for g in range(HALF_GROUPS)]


def vmem():
    return pl.BlockSpec(memory_space=pltpu.VMEM)


def smem():
    return pl.BlockSpec(memory_space=pltpu.SMEM)


def params():
    return pltpu.CompilerParams(vmem_limit_bytes=VMEM_BYTES)


def cost(micros):
    return pl.CostEstimate(flops=int(micros * 1e9), bytes_accessed=0, transcendentals=0)


def dot(a, b, ca=1, cb=0):
    return lax.dot_general(a, b, (((ca,), (cb,)), ((), ())), preferred_element_type=f32)


def ctx_parts(n):
    slow = min(4, n)
    return slow, n // slow


def ctx_swap(block, n, k):
    return lax.ppermute(block, "ctx", [(i, i ^ k) for i in range(n)])


def wa_swap(block, k):
    return lax.ppermute(block, "wa", [(i, i ^ k) for i in range(4)])


def core_swap(block):
    return wa_swap(block, 1)


def x_swap(block):
    return wa_swap(block, 2)


def gather_slow(block, n):
    slow, fast = ctx_parts(n)
    return [block] + [ctx_swap(block, n, kz * fast) for kz in range(1, slow)]


def gather_fast(blocks, n):
    slow, fast = ctx_parts(n)
    return [
        blocks[kz] if r == 0 else ctx_swap(blocks[kz], n, r) for kz in range(slow) for r in range(fast)
    ]


def in_order(blocks, n):
    own = lax.axis_index("ctx")
    whole = jnp.zeros((n,) + blocks[0].shape, blocks[0].dtype)
    for k in range(n):
        whole = lax.dynamic_update_index_in_dim(whole, blocks[k], own ^ k, 0)
    return whole


def ring_order(n):
    slow, fast = ctx_parts(n)
    order = []
    for r in range(fast):
        line = [z * fast + r for z in range(slow)]
        order += line if r % 2 == 0 else line[::-1]
    return order


def ring_id(ctx, offset, n):
    slow, fast = ctx_parts(n)

    def along(r, z):
        return jnp.where(r % 2 == 0, z, slow - 1 - z)

    place = (ctx % fast) * slow + along(ctx % fast, ctx // fast)
    place = (place + offset) % n
    r = place // slow
    return along(r, place % slow) * fast + r


def ring_send(forward, backward, n):
    order = ring_order(n)
    pairs = [(order[p], order[(p + 1) % n]) for p in range(n)]
    return (
        lax.ppermute(forward, "ctx", pairs),
        lax.ppermute(backward, "ctx", [(b, a) for a, b in pairs]),
    )


def ring_gather_step(found, step, n):
    half_ring = n // 2
    f, b = found[(1 - step) % n], found[step - 1]
    if step == half_ring:
        half = f.shape[0] // 2
        parts = ring_send(f[:half], b[half:], n)
        return found | {half_ring: jnp.concatenate(parts, 0)}
    f, b = ring_send(f, b, n)
    return found | {n - step: f, step: b}


def ring_scatter_step(terms, came, step, n):
    half_ring = n // 2
    far = terms[half_ring]
    half = far.shape[0] // 2
    if step == 1:
        return ring_send(far[:half], far[half:], n)
    d = half_ring - step + 1
    f, b = terms[d].astype(f32), terms[n - d].astype(f32)
    came_f, came_b = came[0].astype(f32), came[1].astype(f32)
    if step == 2:
        rest = jnp.zeros_like(far[half:], f32)
        came_f = jnp.concatenate([came_f, rest], 0)
        came_b = jnp.concatenate([jnp.zeros_like(far[:half], f32), came_b], 0)
    return ring_send((f + came_f).astype(bf16), (b + came_b).astype(bf16), n)


def scatter_terms(terms, n, crossing=None):
    slow, fast = ctx_parts(n)
    came = []
    for kz in reversed(range(slow)):
        total = terms(kz * fast).astype(f32)
        for r in range(1, fast):
            block = ctx_swap(terms(kz * fast + r).astype(bf16), n, r)
            if crossing is not None and kz == 1 and r == 1:
                block, crossing = lax.optimization_barrier((block, crossing))
            total = total + block.astype(f32)
        if kz > 0:
            came.append(ctx_swap(total.astype(bf16), n, kz * fast))
    return (total, came) if crossing is None else (total, came, crossing)


def scatter_sum(terms, n, crossing):
    total, came, crossing = scatter_terms(terms, n, crossing)
    for c in came:
        total = total + c.astype(f32)
    return total, crossing


def rounded(array):
    return lax.optimization_barrier(array.astype(bf16))


def lane_half(shape):
    lane = lax.broadcasted_iota(jnp.int32, shape, 1)
    return lane // HEAD


def turn(z):
    lane = lax.broadcasted_iota(jnp.int32, z.shape, 1)
    return jnp.where(
        lane % HEAD < HEAD // 2,
        pltpu.roll(z, SLAB - HEAD // 2, 1),
        pltpu.roll(z, HEAD // 2, 1),
    )


def prepare_kernel(
    n, at_ref, pairs_ref, segments_ref, x_ref, cot_ref, table_ref, ring_ref, rows_ref, cos_ref, sin_ref, own_ref, cots_ref
):
    ctx, core = at_ref[0], at_ref[1]
    own_rows = own_ref.shape[0]
    run_rows = own_rows // 2
    piece = run_rows // 2
    blocks = 2 * n
    lower = pairs_ref[ctx]
    for c in range(2):
        for run in range(2):
            for p in range(2):
                to = c * own_rows + run * run_rows + p * piece
                source = (2 * c + p) * 2 * piece + run * piece
                cots_ref[to : to + piece, :] = cot_ref[source : source + piece, :]
    for run in range(2):
        for p in range(2):
            to = run * run_rows + p * piece
            source = pl.multiple_of((2 * core + p) * 2 * piece + run * piece, piece)
            own_ref[to : to + piece, :] = x_ref[pl.ds(source, piece), :]
    ring_ref[0] = core
    for k in range(n):
        ring_ref[1 + k] = ring_id(ctx, k, n)
    for j in range(n):
        low = pairs_ref[j]
        table_ref[low] = 2 * (ctx ^ j)
        table_ref[blocks - 1 - low] = 2 * (ctx ^ j) + 1
    counts = []
    every = segments_ref[...]
    for d in range(DOCS):
        here = (every == d + 1).astype(f32)
        counts.append(jnp.sum(here, 0, keepdims=True))
    count = jnp.sum(jnp.concatenate(counts, 0), 1, keepdims=True)
    docs = lax.broadcasted_iota(jnp.int32, (DOCS, run_rows), 0) + 1
    lane = lax.broadcasted_iota(jnp.int32, (1, run_rows), 1)
    first_piece = segments_ref[pl.ds(ctx * PIECES + 2 * core, 1), :]
    second_piece = segments_ref[pl.ds(ctx * PIECES + 2 * core + 1, 1), :]
    runs = (
        jnp.where(lane < piece, first_piece, pltpu.roll(second_piece, piece, 1)),
        jnp.where(lane < piece, pltpu.roll(first_piece, piece, 1), second_piece),
    )
    table_ref[blocks] = core
    for run in range(2):
        block = lower if run == 0 else blocks - 1 - lower
        position = block * (2 * run_rows) + core * run_rows + lane
        earlier = jnp.where(docs < runs[run], count, 0.0)
        start = jnp.sum(earlier, 0, keepdims=True)
        start = jnp.where(runs[run] > 0, start, position.astype(f32))
        first = jnp.min(start).astype(jnp.int32) // (2 * run_rows)
        latest = (jnp.max(start).astype(jnp.int32) + 2 * run_rows - 1) // (2 * run_rows)
        whole_from = jnp.minimum(jnp.maximum(latest, first), block + 1)
        whole_to = jnp.maximum(block, whole_from)
        for i, value in enumerate((first, whole_from, whole_to, block + 1)):
            table_ref[blocks + 1 + 4 * run + i] = value
        start = start.astype(jnp.int32)
        rows_ref[2 * run : 2 * run + 1, :] = jnp.concatenate([start] * GROUP, 1)
        rows_ref[2 * run + 1 : 2 * run + 2, :] = jnp.concatenate([position] * GROUP, 1)
    lanes = lax.broadcasted_iota(jnp.int32, (run_rows, SLAB), 1)
    row = lax.broadcasted_iota(jnp.int32, (run_rows, SLAB), 0)
    frequency = jnp.exp(-math.log(rope_base) * 2.0 * (lanes % (HEAD // 2)).astype(f32) / HEAD)
    for run in range(2):
        block = lower if run == 0 else blocks - 1 - lower
        angle = (block * (2 * run_rows) + core * run_rows + row).astype(f32) * frequency
        at = slice(run * run_rows, (run + 1) * run_rows)
        cos_ref[at, :] = jnp.cos(angle)
        sine = jnp.sin(angle)
        sin_ref[at, :] = jnp.where(lanes % HEAD < HEAD // 2, -sine, sine)


def project_kernel(x_ref, w_ref, cos_ref, sin_ref, normed_ref, q_ref, kv_ref, gains_ref):
    tail = w_ref[:, PACK - SLAB : PACK].astype(f32).T
    gains_ref[0:1, :] = tail[SLAB - HEAD : SLAB - HEAD + 1, :]
    gains_ref[1:2, :] = tail[SLAB - 1 :, :]
    gain_ref = gains_ref.at[0:1, :]
    x = x_ref[...].astype(f32)
    scale_rows = lax.rsqrt(jnp.mean(x * x, -1, keepdims=True) + epsilon)
    normed = (x * scale_rows * gain_ref[...]).astype(bf16)
    normed_ref[...] = normed
    cosine, sine = cos_ref[...], sin_ref[...]
    half = lane_half(cosine.shape)
    for s in range(PACK // SLAB):
        z = dot(normed, w_ref[:, s * SLAB : (s + 1) * SLAB])
        if s == 2:
            kv_ref[:, 2 * SLAB : 3 * SLAB] = z.astype(bf16)
            continue
        turned = z * cosine + turn(z) * sine
        if s == 0:
            kv_ref[:, :SLAB] = turned.astype(bf16)
        elif s == 1:
            kv_ref[:, SLAB : 2 * SLAB] = jnp.where(half == 0, turned, z).astype(bf16)
        else:
            scaled = turned * HEAD ** (-0.5)
            if s == PACK // SLAB - 1:
                scaled = jnp.where(half == 0, scaled, 0.0)
            q_ref[:, (s - 3) * SLAB : (s - 2) * SLAB] = scaled.astype(bf16)


def head_rows(ref, run, rows, g, place):
    parts = []
    for j in range(GROUP):
        slab, half = divmod(GROUP * g + j, 2)
        z = ref[run * rows : (run + 1) * rows, slab * SLAB : (slab + 1) * SLAB].astype(f32)
        if half != place:
            z = pltpu.roll(z, HEAD, 1)
        parts.append(jnp.where(lane_half(z.shape) == place, z, 0.0).astype(bf16))
    return jnp.concatenate(parts, 0)


def put_heads(ref, values, run, rows, g, place):
    flat = values.T
    for j in range(GROUP):
        slab, half = divmod(GROUP * g + j, 2)
        z = flat[j * rows : (j + 1) * rows, :]
        if half != place:
            z = pltpu.roll(z, HEAD, 1)
        where = (slice(run * rows, (run + 1) * rows), slice(slab * SLAB, (slab + 1) * SLAB))
        if half == 0:
            ref[where] = jnp.where(lane_half(z.shape) == 0, z, 0.0)
        else:
            ref[where] = jnp.where(lane_half(z.shape) == 1, z, ref[where])


def key_block(own_ref, other_ref, slot, rows, slab):
    at = pl.ds(pl.multiple_of(slot * rows, rows), rows)
    cols = slice(slab * SLAB, (slab + 1) * SLAB)
    return jnp.concatenate([own_ref[at, cols], other_ref[at, cols]], 0)


def key_places(block, core, rows, width):
    i = lax.broadcasted_iota(jnp.int32, (2 * rows, width), 0)
    mine = i + core * rows
    others = i - core * rows
    return block * (2 * rows) + jnp.where(i < rows, mine, others)


def forward_kernel(
    blocks, table, q_ref, own_ref, other_ref, rows_ref, mixed_ref, mixed_b_ref, log_ref, acc_ref, sum_ref, max_ref
):
    rows = q_ref.shape[0] // 2
    width = GROUP * rows
    core = table[blocks]
    for run in range(2):
        first, mid0, mid1, last = [table[blocks + 1 + 4 * run + i] for i in range(4)]
        start = rows_ref[2 * run : 2 * run + 1, :]
        stop = rows_ref[2 * run + 1 : 2 * run + 2, :]
        queries = [head_rows(q_ref, run, rows, g, K_PLACE[g][1]) for g in range(HALF_GROUPS)]
        acc_ref[...] = jnp.zeros_like(acc_ref)
        sum_ref[...] = jnp.zeros_like(sum_ref)
        max_ref[...] = jnp.full_like(max_ref, masked_score)

        def step(b, carry, masked):
            at_rows = pl.ds(pl.multiple_of(table[b] * rows, rows), rows)
            if masked:
                at = key_places(b, core, rows, width)
                ok = (at >= start) & (at <= stop)
            scores = []
            for g in range(HALF_GROUPS):
                cols = slice(K_PLACE[g][0] * SLAB, (K_PLACE[g][0] + 1) * SLAB)
                keys = jnp.concatenate([own_ref[at_rows, cols], other_ref[at_rows, cols]], 0)
                s = dot(keys, queries[g], 1, 1)
                if masked:
                    s = jnp.where(ok, s, masked_score)
                scores.append(s)
            for g in range(HALF_GROUPS):
                s = scores[g]
                cols = slice(V_PLACE[g][0] * SLAB, (V_PLACE[g][0] + 1) * SLAB)
                values = jnp.concatenate([own_ref[at_rows, cols], other_ref[at_rows, cols]], 0)
                before = max_ref[8 * g : 8 * g + 1, :]
                high = jnp.maximum(before, jnp.max(s, 0, keepdims=True))
                keep = jnp.exp(before - high)
                p = jnp.exp(s - high)
                max_ref[8 * g : 8 * g + 1, :] = high
                sum_ref[8 * g : 8 * g + 1, :] = sum_ref[8 * g : 8 * g + 1, :] * keep + jnp.sum(p, 0, keepdims=True)
                rows_g = slice(g * SLAB, (g + 1) * SLAB)
                acc_ref[rows_g, :] = acc_ref[rows_g, :] * keep + dot(values, p.astype(bf16), 0, 0)
            return carry

        lax.fori_loop(first, mid0, functools.partial(step, masked=True), 0)
        lax.fori_loop(mid0, mid1, functools.partial(step, masked=False), 0)
        lax.fori_loop(mid1, last, functools.partial(step, masked=True), 0)
        for g in range(HALF_GROUPS):
            total = sum_ref[8 * g : 8 * g + 1, :]
            log_ref[run * HALF_GROUPS + g : run * HALF_GROUPS + g + 1, :] = max_ref[8 * g : 8 * g + 1, :] + jnp.log(total)
            put_heads(mixed_ref, acc_ref[g * SLAB : (g + 1) * SLAB, :] * (1.0 / total), run, rows, g, V_PLACE[g][1])
    mixed_b_ref[...] = mixed_ref[...].astype(bf16)


def wide_rows(ref, run, rows, places, base):
    parts = []
    for g in range(HALF_GROUPS):
        slab, half = places[g]
        z = head_rows(ref, run, rows, g, half)
        zero = jnp.zeros_like(z)
        parts.append(jnp.concatenate([z, zero] if slab == base else [zero, z], 1))
    return jnp.concatenate(parts, 0)


def backward_kernel(blocks,
    table, q_ref, own_ref, other_ref, rows_ref, mixed_ref, log_ref, grad_ref, cos_ref, sin_ref,
    dq_ref, down_ref, dother_out, dq_buf, raw_buf, dother_ref, q_buf, g_buf):
    rows = q_ref.shape[0] // 2
    width = GROUP * rows
    core = table[blocks]
    down_ref[...] = jnp.zeros_like(down_ref)
    dother_ref[...] = jnp.zeros_like(dother_ref)
    for run in range(2):
        first, mid0, mid1, last = [table[blocks + 1 + 4 * run + i] for i in range(4)]
        start = rows_ref[2 * run : 2 * run + 1, :]
        stop = rows_ref[2 * run + 1 : 2 * run + 2, :]
        q_buf[...] = wide_rows(q_ref, run, rows, K_PLACE, 0)
        g_buf[...] = wide_rows(grad_ref, run, rows, V_PLACE, 1)
        logs, deltas = [], []
        for g in range(HALF_GROUPS):
            logs.append(log_ref[run * HALF_GROUPS + g : run * HALF_GROUPS + g + 1, :])
            parts = []
            for j in range(GROUP):
                slab, half = divmod(GROUP * g + j, 2)
                where = (slice(run * rows, (run + 1) * rows), slice(slab * SLAB, (slab + 1) * SLAB))
                z = grad_ref[where].astype(f32) * mixed_ref[where]
                z = jnp.where(lane_half(z.shape) == half, z, 0.0)
                parts.append(jnp.sum(z.T, 0, keepdims=True))
            deltas.append(jnp.concatenate(parts, 1))
        log_all = jnp.concatenate(logs, 1)
        delta_all = jnp.concatenate(deltas, 1)
        dq_buf[...] = jnp.zeros_like(dq_buf)

        def step(b, carry, masked):
            at_rows = pl.ds(pl.multiple_of(table[b] * rows, rows), rows)
            keys = jnp.concatenate([own_ref[at_rows, : 2 * SLAB], other_ref[at_rows, : 2 * SLAB]], 0)
            vals = jnp.concatenate([own_ref[at_rows, SLAB:], other_ref[at_rows, SLAB:]], 0)
            if masked:
                at = key_places(b, core, rows, width)
                ok = (at >= start) & (at <= stop)
            ps, dss = [], []
            for g in range(HALF_GROUPS):
                rg = slice(g * width, (g + 1) * width)
                s = dot(keys, q_buf[rg, :], 1, 1)
                p = jnp.exp(s - log_all[:, rg])
                if masked:
                    p = jnp.where(ok, p, 0.0)
                dp = dot(vals, g_buf[rg, :], 1, 1)
                ps.append(p.astype(bf16))
                dss.append((p * (dp - delta_all[:, rg])).astype(bf16))
            ds = jnp.concatenate(dss, 1)
            p = jnp.concatenate(ps, 1)
            dq_buf[...] += dot(keys, ds, 0, 0)
            dk = dot(ds, q_buf[...])
            dv = dot(p, g_buf[...])
            for i, val in ((0, dk[:, :SLAB]), (1, dk[:, SLAB:] + dv[:, :SLAB]), (2, dv[:, SLAB:])):
                cols = slice(i * SLAB, (i + 1) * SLAB)
                down_ref[at_rows, cols] += val[:rows]
                dother_ref[at_rows, cols] += val[rows:]
            return carry

        lax.fori_loop(first, mid0, functools.partial(step, masked=True), 0)
        lax.fori_loop(mid0, mid1, functools.partial(step, masked=False), 0)
        lax.fori_loop(mid1, last, functools.partial(step, masked=True), 0)
        for g in range(HALF_GROUPS):
            slab, half = K_PLACE[g]
            put_heads(raw_buf, dq_buf[slab * SLAB : (slab + 1) * SLAB, g * width : (g + 1) * width], run, rows, g, half)
    dother_out[...] = dother_ref[...].astype(bf16)
    cosine, sine = cos_ref[...], sin_ref[...]
    for s in range(Q_WIDE // SLAB):
        z = raw_buf[:, s * SLAB : (s + 1) * SLAB] * HEAD ** (-0.5)
        dq_ref[:, s * SLAB : (s + 1) * SLAB] = (z * cosine - turn(z) * sine).astype(bf16)


def put_weights(ring_ref, block_refs, whole_ref, sems, first, columns):
    copies = []
    for k, ref in enumerate(block_refs):
        block = ref.shape[0]
        at = 0 if len(block_refs) == 1 else pl.multiple_of(ring_ref[1 + k] * block, block)
        copy = pltpu.make_async_copy(
            ref.at[:, pl.ds(first, columns)], whole_ref.at[pl.ds(at, block), :], sems.at[k]
        )
        copy.start()
        copies.append(copy)
    return copies


def feed_kernel(ring_ref, own_ref, other_ref, gain_ref, cot_ref, *rest, unit_tile):
    *block_refs, normed_ref, active_ref, grads_ref, part_ref, part_other_ref, wide_ref, sems = rest
    core_ref = ring_ref
    copies = put_weights(ring_ref, block_refs, wide_ref, sems, 0, wide_ref.shape[1])
    rows = own_ref.shape[0]
    units = active_ref.shape[1]
    gain = gain_ref[1:2, :]
    own_at = pl.multiple_of(core_ref[0] * rows, rows)
    other_at = pl.multiple_of((1 - core_ref[0]) * rows, rows)
    for ref, at in ((own_ref, own_at), (other_ref, other_at)):
        x = ref[...]
        scale_rows = lax.rsqrt(jnp.mean(x * x, -1, keepdims=True) + epsilon)
        normed_ref[pl.ds(at, rows), :] = (x * scale_rows * gain).astype(bf16)
    for copy in copies:
        copy.wait()

    @pl.loop(0, units // unit_tile)
    def unit_step(t):
        at = pl.multiple_of(t * unit_tile, unit_tile)
        cols = pl.ds(at, unit_tile)
        up_cols = pl.ds(pl.multiple_of(units + at, unit_tile), unit_tile)
        gate = dot(normed_ref[...], wide_ref[:, cols])
        up = dot(normed_ref[...], wide_ref[:, up_cols])
        grad_active = dot(cot_ref[...], wide_ref[:, pl.ds(pl.multiple_of(2 * units + at, unit_tile), unit_tile)])
        sig = jax.nn.sigmoid(gate)
        silu = gate * sig
        active_ref[:, cols] = (silu * up).astype(bf16)
        grads_ref[:, cols] = (grad_active * up * (sig * (1.0 + gate * (1.0 - sig)))).astype(bf16)
        grads_ref[:, up_cols] = (grad_active * silu).astype(bf16)

    model = normed_ref.shape[1]
    tile = model // 3

    @pl.loop(0, 3)
    def model_step(t):
        at = pl.ds(pl.multiple_of(t * tile, tile), tile)
        wide = wide_ref[at, : 2 * units]
        part_ref[:, at] = dot(grads_ref[pl.ds(own_at, rows), :], wide, 1, 1)
        part_other_ref[:, at] = dot(grads_ref[pl.ds(other_at, rows), :], wide, 1, 1).astype(bf16)


def feed_weights_kernel(n, count, place_ref, normed_ref, active_ref, grads_ref, cot_ref, *outs):
    weight_refs = outs[:count]
    *block_refs, out_ref, out_other_ref, buf, down_ref, sems = outs[count:]
    units = active_ref.shape[1]
    copies = put_weights(place_ref, weight_refs, down_ref, sems, 2 * units, units)
    rows = out_ref.shape[0]
    units = active_ref.shape[1]
    model = normed_ref.shape[1]
    tile = buf.shape[1]
    own_at = pl.multiple_of(place_ref[0] * rows, rows)
    other_at = pl.multiple_of((1 - place_ref[0]) * rows, rows)

    def put(values, at):
        if len(block_refs) == 1:
            block_refs[0][:, at] = values.astype(bf16)
            return
        buf[...] = values.astype(bf16)
        block = model // n
        for k in range(n):
            block_refs[k][:, at] = buf[pl.ds(pl.multiple_of(place_ref[1 + k] * block, block), block), :]

    @pl.loop(0, units // tile)
    def weight_step(t):
        for i in range(3):
            cols = pl.ds(pl.multiple_of(t * tile, tile), tile)
            at = pl.ds(pl.multiple_of(i * units + t * tile, tile), tile)
            if i < 2:
                put(dot(normed_ref[...], grads_ref[:, at], 0, 0), at)
            else:
                put(dot(cot_ref[...], active_ref[:, cols], 0, 0), at)

    wide_tile = model // 3
    for copy in copies:
        copy.wait()

    @pl.loop(0, 3)
    def out_step(t):
        at = pl.ds(pl.multiple_of(t * wide_tile, wide_tile), wide_tile)
        down = down_ref[at, :]
        out_ref[:, at] = dot(active_ref[pl.ds(own_at, rows), :], down, 1, 1)
        out_other_ref[:, at] = dot(active_ref[pl.ds(other_at, rows), :], down, 1, 1).astype(bf16)


def hidden_grad_kernel(
    core_ref, hidden_ref, mine_ref, came_ref, gains_ref, cot_ref, w_ref, grad_ref, attn_ref, mixed_ref, gain_ref
):
    rows = hidden_ref.shape[0]
    hidden = hidden_ref[...]
    grad_normed = mine_ref[...].astype(f32) + came_ref[...].astype(f32)
    scale_rows = lax.rsqrt(jnp.mean(hidden * hidden, -1, keepdims=True) + epsilon)
    unit = hidden * scale_rows
    gain_ref[...] = jnp.sum(grad_normed * unit, 0, keepdims=True)
    grad_unit = grad_normed * gains_ref[1:2, :]
    inner = jnp.mean(grad_unit * unit, -1, keepdims=True)
    cot = cot_ref[pl.ds(pl.multiple_of(core_ref[0] * rows, rows), rows), :].astype(f32)
    grad = cot + scale_rows * (grad_unit - unit * inner)
    grad_ref[...] = grad
    attn_ref[...] = grad.astype(bf16)
    mixed_ref[:, :HALF_Q] = dot(attn_ref[...], w_ref[:, PACK:]).astype(bf16)
    mixed_ref[:, HALF_Q:] = jnp.zeros((rows, HEAD), bf16)


def last_kernel(
    dkv_ref, dq_ref, cos_ref, sin_ref, w_ref, normed_ref, x_ref, grad_attn_ref, mixed_ref, gain_two_ref, *rest
):
    *came_refs, part_ref, dw_ref, lin_ref = rest
    cosine, sine = cos_ref[...], sin_ref[...]
    half = lane_half(cosine.shape)
    for s in range(3):
        cols = slice(s * SLAB, (s + 1) * SLAB)
        z = dkv_ref[:, cols]
        for ref in came_refs:
            z = z + ref[:, cols].astype(f32)
        turned = z * cosine - turn(z) * sine
        lin_ref[:, cols] = (turned if s == 0 else jnp.where(half == 0, turned, z) if s == 1 else z).astype(bf16)
    lin_ref[:, 3 * SLAB :] = dq_ref[...]
    x = x_ref[...].astype(f32)
    scale_rows = lax.rsqrt(jnp.mean(x * x, -1, keepdims=True) + epsilon)
    model = normed_ref.shape[1]
    tile = model // 3
    last = PACK - SLAB

    @pl.loop(0, 3)
    def model_step(t):
        at = pl.ds(pl.multiple_of(t * tile, tile), tile)
        part = dot(lin_ref[...], w_ref[at, :PACK], 1, 1)
        part_ref[:, at] = part.astype(bf16)
        unit = x_ref[:, at].astype(f32) * scale_rows
        gain_one = jnp.sum(part * unit, 0, keepdims=True)
        gain_one = jnp.broadcast_to(gain_one, (SLAB, tile)).T
        gain_two = jnp.broadcast_to(gain_two_ref[:, at], (SLAB, tile)).T
        dw = dot(normed_ref[:, at], lin_ref[...], 0, 0)
        dw_ref[at, :last] = dw[:, :last].astype(bf16)
        lane = lax.broadcasted_iota(jnp.int32, (tile, SLAB), 1)
        gains = jnp.where(lane < HEAD + HEAD // 2, gain_one, gain_two)
        dw_ref[at, last:PACK] = jnp.where(lane < HEAD, dw[:, last:], gains).astype(bf16)
        dw_ref[at, PACK:] = dot(grad_attn_ref[:, at], mixed_ref[:, :HALF_Q], 0, 0).astype(bf16)


def as_dealt(array, pieces):
    rows = array.shape[0]
    rest = array.shape[1:]
    axes = (0, 2, 1, 3) + tuple(4 + i for i in range(len(rest)))
    split = array.reshape((2, 2, pieces // 2, rows // (2 * pieces)) + rest)
    return jnp.transpose(split, axes).reshape((rows,) + rest)


def norm_backward(grad_normed, unit_rows, scale_rows, gain):
    grad_unit = grad_normed * gain
    grad_gain = jnp.sum(grad_normed * unit_rows, 0)
    grad_rows = scale_rows * (
        grad_unit - unit_rows * jnp.mean(grad_unit * unit_rows, -1, keepdims=True)
    )
    return grad_rows, grad_gain


def on_device(n, args):
    (inputs, cotangent, segments, pair_order, gain_attn, w_query, w_key, w_value, w_out, gain_mlp,
     w_gate, w_up, w_down) = args
    local_rows, model = inputs.shape
    pieces = PIECES
    own_rows = local_rows // 2
    run_rows = own_rows // 2
    part_rows = gain_attn.shape[0]
    ctx_rows = gain_mlp.shape[0]
    pair_rows = ctx_rows // 2
    units = w_gate.shape[1]
    blocks = 2 * n
    ctx_index = lax.axis_index("ctx")
    wa_index = lax.axis_index("wa")
    x_index, core_index = wa_index // 2, wa_index % 2

    def both_halves(array, width):
        return array[:, :width], array[:, width:]

    q_halves = both_halves(w_query, HALF_Q)
    k_halves = both_halves(w_key, HALF_KV)
    v_halves = both_halves(w_value, HALF_KV)
    gain_two_part = lax.dynamic_slice_in_dim(gain_mlp, wa_index * part_rows, part_rows)
    gain_cols = jnp.concatenate(
        [jnp.broadcast_to(g[:, None], (part_rows, HEAD // 2)) for g in (gain_attn, gain_two_part)], 1
    )
    out_halves = both_halves(w_out.T, HALF_Q)
    halves = [
        jnp.concatenate([k_halves[i], v_halves[i], q_halves[i], gain_cols, out_halves[i]], 1)
        for i in range(2)
    ]

    def gather_rows(halves, wide_block):
        mine = jnp.where(x_index == 0, halves[0], halves[1])
        theirs = jnp.where(x_index == 0, halves[1], halves[0])
        came = x_swap(theirs)
        low = jnp.where(x_index == 0, mine, came)
        high = jnp.where(x_index == 0, came, mine)
        pair = jnp.stack([low, high])
        pair, wide_block = lax.optimization_barrier((pair, wide_block))
        other = core_swap(pair)
        zero = jnp.where(core_index == 0, pair, other)
        one = jnp.where(core_index == 0, other, pair)
        quad = jnp.stack([zero, one], 1).reshape(ctx_rows, -1)
        sent = lax.dynamic_slice_in_dim(quad, core_index * pair_rows, pair_rows, 0)
        held = in_order(gather_fast(gather_slow(sent, n), n), n)
        opposite = core_swap(held)
        whole = jnp.where(
            core_index == 0,
            jnp.concatenate([held, opposite], 1),
            jnp.concatenate([opposite, held], 1),
        )
        return whole.reshape(n * ctx_rows, -1), wide_block

    at = jnp.stack([ctx_index, core_index]).astype(jnp.int32)
    table, ring, rows_info, cosine, sine, x_own, run_cotangent = pl.pallas_call(
        functools.partial(prepare_kernel, n),
        out_shape=(
            jax.ShapeDtypeStruct((blocks + 9,), jnp.int32),
            jax.ShapeDtypeStruct((n + 1,), jnp.int32),
            jax.ShapeDtypeStruct((4, GROUP * run_rows), jnp.int32),
            jax.ShapeDtypeStruct((own_rows, SLAB), f32),
            jax.ShapeDtypeStruct((own_rows, SLAB), f32),
            jax.ShapeDtypeStruct((own_rows, model), bf16),
            jax.ShapeDtypeStruct((local_rows, model), bf16),
        ),
        in_specs=[smem()] * 2 + [vmem()] * 3,
        out_specs=(smem(),) * 2 + (vmem(),) * 5,
        compiler_params=params(),
        cost_estimate=cost(6),
    )(at, pair_order, segments.reshape(-1, local_rows // PIECES), inputs, cotangent)

    wide_block = jnp.concatenate([w_gate, w_up, w_down.T], 1)
    half_ring = n // 2
    w_all, wide_block = gather_rows(halves, wide_block)
    w_out_t = w_all[:, PACK:]
    wide = {0: wide_block}
    for step in range(1, half_ring - 2):
        wide = ring_gather_step(wide, step, n)
    normed, queries, kv_own, gains = pl.pallas_call(
        project_kernel,
        out_shape=(
            jax.ShapeDtypeStruct((own_rows, model), bf16),
            jax.ShapeDtypeStruct((own_rows, Q_WIDE), bf16),
            jax.ShapeDtypeStruct((own_rows, 2 * HALF_KV), bf16),
            jax.ShapeDtypeStruct((2, model), f32),
        ),
        in_specs=[vmem()] * 4,
        out_specs=(vmem(),) * 4,
        compiler_params=params(),
        cost_estimate=cost(5),
    )(x_own, w_all, cosine, sine)
    wide, kv_own = lax.optimization_barrier((wide, kv_own))

    kv_core = jnp.concatenate(gather_fast(gather_slow(kv_own, n), n), 0)
    kv_other = core_swap(kv_core)
    wide, kv_core, kv_other = lax.optimization_barrier((wide, kv_core, kv_other))
    wide = ring_gather_step(wide, half_ring - 2, n)

    mixed, mixed_b, log_total = pl.pallas_call(
        functools.partial(forward_kernel, blocks),
        out_shape=(
            jax.ShapeDtypeStruct((own_rows, Q_WIDE), f32),
            jax.ShapeDtypeStruct((own_rows, Q_WIDE), bf16),
            jax.ShapeDtypeStruct((8, GROUP * run_rows), f32),
        ),
        in_specs=[smem()] + [vmem()] * 4,
        out_specs=(vmem(),) * 3,
        scratch_shapes=[
            pltpu.VMEM((HALF_GROUPS * SLAB, GROUP * run_rows), f32),
            pltpu.VMEM((8 * HALF_GROUPS, GROUP * run_rows), f32),
            pltpu.VMEM((8 * HALF_GROUPS, GROUP * run_rows), f32),
        ],
        compiler_params=params(),
        cost_estimate=cost(16),
    )(table, queries, kv_core, kv_other, rows_info)

    wide, mixed_b = lax.optimization_barrier((wide, mixed_b))
    wide = ring_gather_step(wide, half_ring - 1, n)
    wide = ring_gather_step(wide, half_ring, n)
    attn_part = rounded(dot(mixed_b[:, :HALF_Q], w_all[:, PACK:], 1, 1))
    attn_came = x_swap(attn_part)
    wide, attn_came = lax.optimization_barrier((wide, attn_came))
    wide = [wide[k] for k in range(n)]
    whole_tiles = ctx_rows % 16 == 0
    if not whole_tiles:
        wide_full = jnp.zeros((n,) + wide_block.shape, bf16)
        for k in range(n):
            wide_full = lax.dynamic_update_index_in_dim(wide_full, wide[k], ring_id(ctx_index, k, n), 0)
        wide = [wide_full.reshape(model, 3 * units)]
    x_f = x_own.astype(f32)
    hidden_own = x_f + (attn_part.astype(f32) + attn_came.astype(f32))
    hidden_other = core_swap(hidden_own)

    def join(own, other):
        return jnp.where(
            core_index == 0, jnp.concatenate([own, other], 0), jnp.concatenate([other, own], 0)
        )

    normed_two, active, grads_wide, grad_two_own, grad_two_other = pl.pallas_call(
        functools.partial(feed_kernel, unit_tile=min(256, units)),
        out_shape=(
            jax.ShapeDtypeStruct((local_rows, model), bf16),
            jax.ShapeDtypeStruct((local_rows, units), bf16),
            jax.ShapeDtypeStruct((local_rows, 2 * units), bf16),
            jax.ShapeDtypeStruct((own_rows, model), f32),
            jax.ShapeDtypeStruct((own_rows, model), bf16),
        ),
        in_specs=[smem()] + [vmem()] * 4 + [pl.BlockSpec(memory_space=pl.ANY)] * len(wide),
        out_specs=(vmem(),) * 5,
        scratch_shapes=[
            pltpu.VMEM((model, 3 * units), bf16),
            pltpu.SemaphoreType.DMA((len(wide),)),
        ],
        compiler_params=params(),
        cost_estimate=cost(12),
    )(ring, hidden_own, hidden_other, gains, run_cotangent, *wide)
    shapes = (
        (jax.ShapeDtypeStruct((ctx_rows, 3 * units), bf16),) * n
        if whole_tiles
        else (jax.ShapeDtypeStruct((model, 3 * units), bf16),)
    )
    unit_tile = min(256, units)
    *d_terms, mlp_own, mlp_other = pl.pallas_call(
        functools.partial(feed_weights_kernel, n, len(wide)),
        out_shape=shapes
        + (
            jax.ShapeDtypeStruct((own_rows, model), f32),
            jax.ShapeDtypeStruct((own_rows, model), bf16),
        ),
        in_specs=[smem()] + [vmem()] * 4 + [pl.BlockSpec(memory_space=pl.ANY)] * len(wide),
        out_specs=(vmem(),) * (len(shapes) + 2),
        scratch_shapes=[
            pltpu.VMEM((model, unit_tile), bf16),
            pltpu.VMEM((model, units), bf16),
            pltpu.SemaphoreType.DMA((len(wide),)),
        ],
        compiler_params=params(),
        cost_estimate=cost(9),
    )(ring, normed_two, active, grads_wide, run_cotangent, *wide)
    if not whole_tiles:
        d_blocks = d_terms[0].reshape(n, ctx_rows, 3 * units)
        d_terms = [
            lax.dynamic_index_in_dim(d_blocks, ring_id(ctx_index, k, n), 0, keepdims=False) for k in range(n)
        ]
    def chip_sum(own, other):
        return rounded(own + core_swap(other).astype(f32))

    grad_two = chip_sum(grad_two_own, grad_two_other)
    grad_two_came, d_terms, mlp_own = lax.optimization_barrier((x_swap(grad_two), d_terms, mlp_own))
    d_came = None
    for step in range(1, half_ring - 2):
        d_came = ring_scatter_step(d_terms, d_came, step, n)
    output_chip = chip_sum(mlp_own, mlp_other)
    grad_hidden, grad_attn, grad_mixed, grad_gain_two = pl.pallas_call(
        hidden_grad_kernel,
        out_shape=(
            jax.ShapeDtypeStruct((own_rows, model), f32),
            jax.ShapeDtypeStruct((own_rows, model), bf16),
            jax.ShapeDtypeStruct((own_rows, Q_WIDE), bf16),
            jax.ShapeDtypeStruct((1, model), f32),
        ),
        in_specs=[smem()] + [vmem()] * 6,
        out_specs=(vmem(),) * 4,
        compiler_params=params(),
        cost_estimate=cost(5),
    )(ring, hidden_own, grad_two, grad_two_came, gains, run_cotangent, w_all)
    d_came, grad_mixed, output_chip = lax.optimization_barrier((d_came, grad_mixed, output_chip))
    d_came = ring_scatter_step(d_terms, d_came, half_ring - 2, n)

    dq_lin, dkv_core, dkv_other = pl.pallas_call(
        functools.partial(backward_kernel, blocks),
        out_shape=(
            jax.ShapeDtypeStruct((own_rows, Q_WIDE), bf16),
            jax.ShapeDtypeStruct(kv_core.shape, f32),
            jax.ShapeDtypeStruct(kv_core.shape, bf16),
        ),
        in_specs=[smem()] + [vmem()] * 9,
        out_specs=(vmem(),) * 3,
        scratch_shapes=[
            pltpu.VMEM((2 * SLAB, HEADS // 2 * run_rows), f32),
            pltpu.VMEM((own_rows, Q_WIDE), f32),
            pltpu.VMEM(kv_core.shape, f32),
            pltpu.VMEM((HEADS // 2 * run_rows, 2 * SLAB), bf16),
            pltpu.VMEM((HEADS // 2 * run_rows, 2 * SLAB), bf16),
        ],
        compiler_params=params(),
        cost_estimate=cost(24),
    )(table, queries, kv_core, kv_other, rows_info, mixed, log_total, grad_mixed, cosine, sine)

    def scatter_rows(part, crossing, beside):
        cols = part.shape[1]
        split = part.reshape(n, 2, pair_rows, cols)
        mine = lax.dynamic_index_in_dim(split, core_index, 1, keepdims=False)
        theirs = lax.dynamic_index_in_dim(split, 1 - core_index, 1, keepdims=False)
        came, beside = lax.optimization_barrier((core_swap(theirs), beside))
        chip = mine.astype(f32) + came.astype(f32)
        total, crossed = scatter_sum(
            lambda k: lax.dynamic_index_in_dim(chip, ctx_index ^ k, 0, keepdims=False), n, x_swap(crossing)
        )
        total_b = total.astype(bf16)
        opposite = core_swap(total_b)
        rows = jnp.where(
            core_index == 0,
            jnp.concatenate([total_b, opposite], 0),
            jnp.concatenate([opposite, total_b], 0),
        )
        quad = rows.reshape(2, 2, part_rows, cols)
        kept = lax.dynamic_index_in_dim(
            lax.dynamic_index_in_dim(quad, x_index, 0, keepdims=False), core_index, 0, keepdims=False
        )
        sent = lax.dynamic_index_in_dim(
            lax.dynamic_index_in_dim(quad, 1 - x_index, 0, keepdims=False), core_index, 0, keepdims=False
        )
        came = x_swap(sent)
        low = jnp.where(x_index == 0, kept, came).astype(f32)
        high = jnp.where(x_index == 0, came, kept).astype(f32)
        return rows, low, high, crossed, beside

    dkv_other, d_came = lax.optimization_barrier((dkv_other, d_came))
    d_came = ring_scatter_step(d_terms, d_came, half_ring - 1, n)
    dkv = dkv_core + core_swap(dkv_other).astype(f32)
    dkv = dkv.reshape(n, own_rows, 2 * HALF_KV)
    dkv_own, dkv_came = scatter_terms(lambda k: dkv[k], n)
    output_came = x_swap(output_chip)
    dkv_came, d_came, output_came = lax.optimization_barrier((dkv_came, d_came, output_came))
    d_came = ring_scatter_step(d_terms, d_came, half_ring, n)
    output_own = (hidden_own + (output_chip.astype(f32) + output_came.astype(f32))).astype(bf16)
    output = as_dealt(join(output_own, core_swap(output_own)), pieces)
    normed_part, d_in = pl.pallas_call(
        last_kernel,
        out_shape=(
            jax.ShapeDtypeStruct((own_rows, model), bf16),
            jax.ShapeDtypeStruct((model, PACK + HALF_Q), bf16),
        ),
        in_specs=[vmem()] * (10 + len(dkv_came)),
        out_specs=(vmem(),) * 2,
        scratch_shapes=[pltpu.VMEM((own_rows, PACK), bf16)],
        compiler_params=params(),
        cost_estimate=cost(5),
    )(dkv_own, dq_lin, cosine, sine, w_all, normed, x_own, grad_attn, mixed_b, grad_gain_two, *dkv_came)
    in_rows, in_low, in_high, normed_came, d_came = scatter_rows(d_in, normed_part, d_came)
    d_mlp = d_terms[0].astype(f32) + d_came[0].astype(f32) + d_came[1].astype(f32)
    grad_w_gate = d_mlp[:, :units]
    grad_w_up = d_mlp[:, units : 2 * units]
    grad_w_down = d_mlp[:, 2 * units :].T

    k_end, v_end, q_end = HALF_KV, 2 * HALF_KV, 2 * HALF_KV + HALF_Q
    grad_w_key = jnp.concatenate([in_low[:, :k_end], in_high[:, :k_end]], 1)
    grad_w_value = jnp.concatenate([in_low[:, k_end:v_end], in_high[:, k_end:v_end]], 1)
    grad_w_query = jnp.concatenate([in_low[:, v_end:q_end], in_high[:, v_end:q_end]], 1)

    grad_normed = normed_part.astype(f32) + normed_came.astype(f32)
    scale_one = lax.rsqrt(jnp.mean(x_f * x_f, -1, keepdims=True) + epsilon)
    input_rows, unused_gain = norm_backward(grad_normed, x_f * scale_one, scale_one, gains[:1])
    grad_inputs_own = (grad_hidden + input_rows).astype(bf16)
    grad_inputs = as_dealt(join(grad_inputs_own, core_swap(grad_inputs_own)), pieces)
    grad_w_out = jnp.concatenate([in_low[:, PACK:], in_high[:, PACK:]], 1).T
    grad_gain_attn = in_low[:, q_end] + in_high[:, q_end]
    grad_gain_mlp = in_rows[:, PACK - 1].astype(f32)
    return (
        output,
        grad_inputs,
        grad_gain_attn,
        grad_w_query,
        grad_w_key,
        grad_w_value,
        grad_w_out,
        grad_gain_mlp,
        grad_w_gate,
        grad_w_up,
        grad_w_down,
    )


def solution(mesh):
    n = mesh.shape["ctx"]

    def body(*args):
        return on_device(n, args)

    return jax.shard_map(
        body,
        mesh=mesh,
        in_specs=(
            P("ctx", None),
            P("ctx", None),
            P(),
            P(),
            P(("ctx", "wa")),
            P(("ctx", "wa"), None),
            P(("ctx", "wa"), None),
            P(("ctx", "wa"), None),
            P(None, ("ctx", "wa")),
            P("ctx"),
            P("ctx", "wa"),
            P("ctx", "wa"),
            P("wa", "ctx"),
        ),
        out_specs=(
            P("ctx", None),
            P("ctx", None),
            P(("ctx", "wa")),
            P(("ctx", "wa"), None),
            P(("ctx", "wa"), None),
            P(("ctx", "wa"), None),
            P(None, ("ctx", "wa")),
            P("ctx"),
            P("ctx", "wa"),
            P("ctx", "wa"),
            P("wa", "ctx"),
        ),
        check_vma=False,
    )
```

```python
import functools
import math

import jax
import jax.numpy as jnp
from jax import lax
from jax.experimental import pallas as pl
from jax.experimental.pallas import tpu as pltpu
from jax.sharding import PartitionSpec as P

HEADS = 18
KV_HEADS = 6
HEAD = 64
GROUP = HEADS // KV_HEADS
HALF_Q = HEADS * HEAD // 2
HALF_KV = KV_HEADS * HEAD // 2
HALF_GROUPS = KV_HEADS // 2
SLAB = 128
PACK = 2 * HALF_KV + HALF_Q + HEAD
Q_WIDE = HALF_Q + HEAD

epsilon = 1e-05
rope_base = 10000.0
masked_score = -1e30
DOCS = 16
PIECES = 4
f32 = jnp.float32
bf16 = jnp.bfloat16
MIB = 1024 * 1024

K_PLACE = [divmod(g, 2) for g in range(HALF_GROUPS)]
V_PLACE = [divmod(HALF_GROUPS + g, 2) for g in range(HALF_GROUPS)]


def vmem():
    return pl.BlockSpec(memory_space=pltpu.VMEM)


def smem():
    return pl.BlockSpec(memory_space=pltpu.SMEM)


def params(mib=26):
    return pltpu.CompilerParams(vmem_limit_bytes=min(mib, 58) * MIB)


def cost(micros):
    return pl.CostEstimate(flops=int(micros * 1e9), bytes_accessed=0, transcendentals=0)


def dot(a, b, ca=1, cb=0):
    return lax.dot_general(a, b, (((ca,), (cb,)), ((), ())), preferred_element_type=f32)


def ctx_parts(n):
    slow = min(4, n)
    return slow, n // slow


def ctx_swap(block, n, k):
    return lax.ppermute(block, "ctx", [(i, i ^ k) for i in range(n)])


def wa_swap(block, k):
    return lax.ppermute(block, "wa", [(i, i ^ k) for i in range(4)])


def core_swap(block):
    return wa_swap(block, 1)


def x_swap(block):
    return wa_swap(block, 2)


def ring_order(n):
    slow, fast = ctx_parts(n)
    order = []
    for r in range(fast):
        line = [z * fast + r for z in range(slow)]
        order += line if r % 2 == 0 else line[::-1]
    return order


def ring_id(ctx, offset, n):
    slow, fast = ctx_parts(n)

    def along(r, z):
        return jnp.where(r % 2 == 0, z, slow - 1 - z)

    place = (ctx % fast) * slow + along(ctx % fast, ctx // fast)
    place = (place + offset) % n
    r = place // slow
    return along(r, place % slow) * fast + r


def ring_send(forward, backward, n):
    order = ring_order(n)
    pairs = [(order[p], order[(p + 1) % n]) for p in range(n)]
    return (
        lax.ppermute(forward, "ctx", pairs),
        lax.ppermute(backward, "ctx", [(b, a) for a, b in pairs]),
    )


def ring_gather_step(found, step, n):
    half_ring = n // 2
    f, b = found[(1 - step) % n], found[step - 1]
    if step == half_ring:
        half = f.shape[0] // 2
        parts = ring_send(f[:half], b[half:], n)
        return found | {half_ring: jnp.concatenate(parts, 0)}
    f, b = ring_send(f, b, n)
    return found | {n - step: f, step: b}


def ring_scatter_step(terms, came, step, n):
    half_ring = n // 2
    far = terms[half_ring]
    half = far.shape[0] // 2
    if step == 1:
        return ring_send(far[:half].astype(bf16), far[half:].astype(bf16), n)
    d = half_ring - step + 1
    f, b = terms[d].astype(f32), terms[n - d].astype(f32)
    came_f, came_b = came[0].astype(f32), came[1].astype(f32)
    if step == 2:
        rest = jnp.zeros_like(far[half:], f32)
        came_f = jnp.concatenate([came_f, rest], 0)
        came_b = jnp.concatenate([jnp.zeros_like(far[:half], f32), came_b], 0)
    return ring_send((f + came_f).astype(bf16), (b + came_b).astype(bf16), n)


def ring_gather(block, n):
    found = {0: block}
    for step in range(1, n // 2 + 1):
        found = ring_gather_step(found, step, n)
    return found


def ring_scatter(terms, n, crossing=None):
    came = None
    for step in range(1, n // 2 + 1):
        came = ring_scatter_step(terms, came, step, n)
        if crossing is not None and step == 2:
            came, crossing = lax.optimization_barrier((came, crossing))
    return came if crossing is None else (came, crossing)


def rounded(array):
    return lax.optimization_barrier(array.astype(bf16))


def lane_half(shape):
    lane = lax.broadcasted_iota(jnp.int32, shape, 1)
    return lane // HEAD


def turn(z):
    lane = lax.broadcasted_iota(jnp.int32, z.shape, 1)
    return jnp.where(
        lane % HEAD < HEAD // 2,
        pltpu.roll(z, SLAB - HEAD // 2, 1),
        pltpu.roll(z, HEAD // 2, 1),
    )


def prepare_kernel(
    n, at_ref, pairs_ref, segments_ref, x_ref, cot_ref, table_ref, ring_ref, rows_ref, cos_ref, sin_ref, own_ref, cots_ref
):
    ctx, core = at_ref[0], at_ref[1]
    own_rows = own_ref.shape[0]
    run_rows = own_rows // 2
    piece = run_rows // 2
    blocks = 2 * n
    lower = pairs_ref[ctx]
    for c in range(2):
        for run in range(2):
            for p in range(2):
                to = c * own_rows + run * run_rows + p * piece
                source = (2 * c + p) * 2 * piece + run * piece
                cots_ref[to : to + piece, :] = cot_ref[source : source + piece, :]
    for run in range(2):
        for p in range(2):
            to = run * run_rows + p * piece
            source = pl.multiple_of((2 * core + p) * 2 * piece + run * piece, piece)
            own_ref[to : to + piece, :] = x_ref[pl.ds(source, piece), :]
    ring_ref[0] = core
    for k in range(n):
        ring_ref[1 + k] = ring_id(ctx, k, n)
    for k in range(n):
        low = pairs_ref[ring_ref[1 + k]]
        table_ref[low] = 2 * k
        table_ref[blocks - 1 - low] = 2 * k + 1
    counts = []
    every = segments_ref[...]
    for d in range(DOCS):
        here = (every == d + 1).astype(f32)
        counts.append(jnp.sum(here, 0, keepdims=True))
    count = jnp.sum(jnp.concatenate(counts, 0), 1, keepdims=True)
    docs = lax.broadcasted_iota(jnp.int32, (DOCS, run_rows), 0) + 1
    lane = lax.broadcasted_iota(jnp.int32, (1, run_rows), 1)
    first_piece = segments_ref[pl.ds(ctx * PIECES + 2 * core, 1), :]
    second_piece = segments_ref[pl.ds(ctx * PIECES + 2 * core + 1, 1), :]
    runs = (
        jnp.where(lane < piece, first_piece, pltpu.roll(second_piece, piece, 1)),
        jnp.where(lane < piece, pltpu.roll(first_piece, piece, 1), second_piece),
    )
    table_ref[blocks] = core
    for run in range(2):
        block = lower if run == 0 else blocks - 1 - lower
        position = block * (2 * run_rows) + core * run_rows + lane
        earlier = jnp.where(docs < runs[run], count, 0.0)
        start = jnp.sum(earlier, 0, keepdims=True)
        start = jnp.where(runs[run] > 0, start, position.astype(f32))
        first = jnp.min(start).astype(jnp.int32) // (2 * run_rows)
        latest = (jnp.max(start).astype(jnp.int32) + 2 * run_rows - 1) // (2 * run_rows)
        whole_from = jnp.minimum(jnp.maximum(latest, first), block + 1)
        whole_to = jnp.maximum(block, whole_from)
        for i, value in enumerate((first, whole_from, whole_to, block + 1)):
            table_ref[blocks + 1 + 4 * run + i] = value
        start = start.astype(jnp.int32)
        rows_ref[2 * run : 2 * run + 1, :] = jnp.concatenate([start] * GROUP, 1)
        rows_ref[2 * run + 1 : 2 * run + 2, :] = jnp.concatenate([position] * GROUP, 1)
    lanes = lax.broadcasted_iota(jnp.int32, (run_rows, SLAB), 1)
    row = lax.broadcasted_iota(jnp.int32, (run_rows, SLAB), 0)
    frequency = jnp.exp(-math.log(rope_base) * 2.0 * (lanes % (HEAD // 2)).astype(f32) / HEAD)
    for run in range(2):
        block = lower if run == 0 else blocks - 1 - lower
        angle = (block * (2 * run_rows) + core * run_rows + row).astype(f32) * frequency
        at = slice(run * run_rows, (run + 1) * run_rows)
        cos_ref[at, :] = jnp.cos(angle)
        sine = jnp.sin(angle)
        sin_ref[at, :] = jnp.where(lanes % HEAD < HEAD // 2, -sine, sine)


def project_kernel(x_ref, w_ref, cos_ref, sin_ref, normed_ref, q_ref, kv_ref, gains_ref):
    tail = w_ref[:, PACK - SLAB : PACK].astype(f32).T
    gains_ref[0:1, :] = tail[SLAB - HEAD : SLAB - HEAD + 1, :]
    gains_ref[1:2, :] = tail[SLAB - 1 :, :]
    gain_ref = gains_ref.at[0:1, :]
    x = x_ref[...].astype(f32)
    scale_rows = lax.rsqrt(jnp.mean(x * x, -1, keepdims=True) + epsilon)
    normed = (x * scale_rows * gain_ref[...]).astype(bf16)
    normed_ref[...] = normed
    cosine, sine = cos_ref[...], sin_ref[...]
    half = lane_half(cosine.shape)
    for s in range(PACK // SLAB):
        z = dot(normed, w_ref[:, s * SLAB : (s + 1) * SLAB])
        if s == 2:
            kv_ref[:, 2 * SLAB : 3 * SLAB] = z.astype(bf16)
            continue
        turned = z * cosine + turn(z) * sine
        if s == 0:
            kv_ref[:, :SLAB] = turned.astype(bf16)
        elif s == 1:
            kv_ref[:, SLAB : 2 * SLAB] = jnp.where(half == 0, turned, z).astype(bf16)
        else:
            scaled = turned * HEAD ** (-0.5)
            if s == PACK // SLAB - 1:
                scaled = jnp.where(half == 0, scaled, 0.0)
            q_ref[:, (s - 3) * SLAB : (s - 2) * SLAB] = scaled.astype(bf16)


def head_rows(ref, run, rows, g, place):
    parts = []
    for j in range(GROUP):
        slab, half = divmod(GROUP * g + j, 2)
        z = ref[run * rows : (run + 1) * rows, slab * SLAB : (slab + 1) * SLAB].astype(f32)
        if half != place:
            z = pltpu.roll(z, HEAD, 1)
        parts.append(jnp.where(lane_half(z.shape) == place, z, 0.0).astype(bf16))
    return jnp.concatenate(parts, 0)


def put_heads(ref, values, run, rows, g, place):
    flat = values.T
    for j in range(GROUP):
        slab, half = divmod(GROUP * g + j, 2)
        z = flat[j * rows : (j + 1) * rows, :]
        if half != place:
            z = pltpu.roll(z, HEAD, 1)
        where = (slice(run * rows, (run + 1) * rows), slice(slab * SLAB, (slab + 1) * SLAB))
        if half == 0:
            ref[where] = jnp.where(lane_half(z.shape) == 0, z, 0.0)
        else:
            ref[where] = jnp.where(lane_half(z.shape) == 1, z, ref[where])


def key_block(own_ref, other_ref, slot, rows, slab):
    at = pl.ds(pl.multiple_of(slot * rows, rows), rows)
    cols = slice(slab * SLAB, (slab + 1) * SLAB)
    return jnp.concatenate([own_ref[at, cols], other_ref[at, cols]], 0)


def key_places(block, core, rows, width):
    i = lax.broadcasted_iota(jnp.int32, (2 * rows, width), 0)
    mine = i + core * rows
    others = i - core * rows
    return block * (2 * rows) + jnp.where(i < rows, mine, others)


def forward_kernel(
    blocks, table, q_ref, own_ref, other_ref, rows_ref, mixed_ref, mixed_b_ref, log_ref, acc_ref, sum_ref, max_ref
):
    rows = q_ref.shape[0] // 2
    width = GROUP * rows
    core = table[blocks]
    for run in range(2):
        first, mid0, mid1, last = [table[blocks + 1 + 4 * run + i] for i in range(4)]
        start = rows_ref[2 * run : 2 * run + 1, :]
        stop = rows_ref[2 * run + 1 : 2 * run + 2, :]
        queries = [head_rows(q_ref, run, rows, g, K_PLACE[g][1]) for g in range(HALF_GROUPS)]
        acc_ref[...] = jnp.zeros_like(acc_ref)
        sum_ref[...] = jnp.zeros_like(sum_ref)
        max_ref[...] = jnp.full_like(max_ref, masked_score)

        def step(b, carry, masked):
            at_rows = pl.ds(pl.multiple_of(table[b] * rows, rows), rows)
            if masked:
                at = key_places(b, core, rows, width)
                ok = (at >= start) & (at <= stop)
            scores = []
            for g in range(HALF_GROUPS):
                cols = slice(K_PLACE[g][0] * SLAB, (K_PLACE[g][0] + 1) * SLAB)
                keys = jnp.concatenate([own_ref[at_rows, cols], other_ref[at_rows, cols]], 0)
                s = dot(keys, queries[g], 1, 1)
                if masked:
                    s = jnp.where(ok, s, masked_score)
                scores.append(s)
            for g in range(HALF_GROUPS):
                s = scores[g]
                cols = slice(V_PLACE[g][0] * SLAB, (V_PLACE[g][0] + 1) * SLAB)
                values = jnp.concatenate([own_ref[at_rows, cols], other_ref[at_rows, cols]], 0)
                before = max_ref[8 * g : 8 * g + 1, :]
                high = jnp.maximum(before, jnp.max(s, 0, keepdims=True))
                keep = jnp.exp(before - high)
                p = jnp.exp(s - high)
                max_ref[8 * g : 8 * g + 1, :] = high
                sum_ref[8 * g : 8 * g + 1, :] = sum_ref[8 * g : 8 * g + 1, :] * keep + jnp.sum(p, 0, keepdims=True)
                rows_g = slice(g * SLAB, (g + 1) * SLAB)
                acc_ref[rows_g, :] = acc_ref[rows_g, :] * keep + dot(values, p.astype(bf16), 0, 0)
            return carry

        lax.fori_loop(first, mid0, functools.partial(step, masked=True), 0)
        lax.fori_loop(mid0, mid1, functools.partial(step, masked=False), 0)
        lax.fori_loop(mid1, last, functools.partial(step, masked=True), 0)
        for g in range(HALF_GROUPS):
            total = sum_ref[8 * g : 8 * g + 1, :]
            log_ref[run * HALF_GROUPS + g : run * HALF_GROUPS + g + 1, :] = max_ref[8 * g : 8 * g + 1, :] + jnp.log(total)
            put_heads(mixed_ref, acc_ref[g * SLAB : (g + 1) * SLAB, :] * (1.0 / total), run, rows, g, V_PLACE[g][1])
    mixed_b_ref[...] = mixed_ref[...].astype(bf16)


def wide_rows(ref, run, rows, places, base):
    parts = []
    for g in range(HALF_GROUPS):
        slab, half = places[g]
        z = head_rows(ref, run, rows, g, half)
        zero = jnp.zeros_like(z)
        parts.append(jnp.concatenate([z, zero] if slab == base else [zero, z], 1))
    return jnp.concatenate(parts, 0)


def backward_kernel(blocks,
    table, q_ref, own_ref, other_ref, rows_ref, mixed_ref, log_ref, grad_ref, cos_ref, sin_ref,
    dq_ref, down_ref, dother_out, dq_buf, raw_buf, dother_ref, q_buf, g_buf):
    rows = q_ref.shape[0] // 2
    width = GROUP * rows
    core = table[blocks]
    down_ref[...] = jnp.zeros_like(down_ref)
    dother_ref[...] = jnp.zeros_like(dother_ref)
    for run in range(2):
        first, mid0, mid1, last = [table[blocks + 1 + 4 * run + i] for i in range(4)]
        start = rows_ref[2 * run : 2 * run + 1, :]
        stop = rows_ref[2 * run + 1 : 2 * run + 2, :]
        q_buf[...] = wide_rows(q_ref, run, rows, K_PLACE, 0)
        g_buf[...] = wide_rows(grad_ref, run, rows, V_PLACE, 1)
        logs, deltas = [], []
        for g in range(HALF_GROUPS):
            logs.append(log_ref[run * HALF_GROUPS + g : run * HALF_GROUPS + g + 1, :])
            parts = []
            for j in range(GROUP):
                slab, half = divmod(GROUP * g + j, 2)
                where = (slice(run * rows, (run + 1) * rows), slice(slab * SLAB, (slab + 1) * SLAB))
                z = grad_ref[where].astype(f32) * mixed_ref[where]
                z = jnp.where(lane_half(z.shape) == half, z, 0.0)
                parts.append(jnp.sum(z.T, 0, keepdims=True))
            deltas.append(jnp.concatenate(parts, 1))
        log_all = jnp.concatenate(logs, 1)
        delta_all = jnp.concatenate(deltas, 1)
        dq_buf[...] = jnp.zeros_like(dq_buf)

        def step(b, carry, masked):
            at_rows = pl.ds(pl.multiple_of(table[b] * rows, rows), rows)
            keys = jnp.concatenate([own_ref[at_rows, : 2 * SLAB], other_ref[at_rows, : 2 * SLAB]], 0)
            vals = jnp.concatenate([own_ref[at_rows, SLAB:], other_ref[at_rows, SLAB:]], 0)
            if masked:
                at = key_places(b, core, rows, width)
                ok = (at >= start) & (at <= stop)
            ps, dss = [], []
            for g in range(HALF_GROUPS):
                rg = slice(g * width, (g + 1) * width)
                s = dot(keys, q_buf[rg, :], 1, 1)
                p = jnp.exp(s - log_all[:, rg])
                if masked:
                    p = jnp.where(ok, p, 0.0)
                dp = dot(vals, g_buf[rg, :], 1, 1)
                ps.append(p.astype(bf16))
                dss.append((p * (dp - delta_all[:, rg])).astype(bf16))
            ds = jnp.concatenate(dss, 1)
            p = jnp.concatenate(ps, 1)
            dq_buf[...] += dot(keys, ds, 0, 0)
            dk = dot(ds, q_buf[...])
            dv = dot(p, g_buf[...])
            for i, val in ((0, dk[:, :SLAB]), (1, dk[:, SLAB:] + dv[:, :SLAB]), (2, dv[:, SLAB:])):
                cols = slice(i * SLAB, (i + 1) * SLAB)
                down_ref[at_rows, cols] += val[:rows]
                dother_ref[at_rows, cols] += val[rows:]
            return carry

        lax.fori_loop(first, mid0, functools.partial(step, masked=True), 0)
        lax.fori_loop(mid0, mid1, functools.partial(step, masked=False), 0)
        lax.fori_loop(mid1, last, functools.partial(step, masked=True), 0)
        for g in range(HALF_GROUPS):
            slab, half = K_PLACE[g]
            put_heads(raw_buf, dq_buf[slab * SLAB : (slab + 1) * SLAB, g * width : (g + 1) * width], run, rows, g, half)
    dother_out[...] = dother_ref[...].astype(bf16)
    cosine, sine = cos_ref[...], sin_ref[...]
    for s in range(Q_WIDE // SLAB):
        z = raw_buf[:, s * SLAB : (s + 1) * SLAB] * HEAD ** (-0.5)
        dq_ref[:, s * SLAB : (s + 1) * SLAB] = (z * cosine - turn(z) * sine).astype(bf16)


def put_weights(ring_ref, block_refs, whole_ref, sems, first, columns):
    copies = []
    for k, ref in enumerate(block_refs):
        block = ref.shape[0]
        at = 0 if len(block_refs) == 1 else pl.multiple_of(ring_ref[1 + k] * block, block)
        copy = pltpu.make_async_copy(
            ref.at[:, pl.ds(first, columns)], whole_ref.at[pl.ds(at, block), :], sems.at[k]
        )
        copy.start()
        copies.append(copy)
    return copies


def feed_kernel(ring_ref, own_ref, other_ref, gain_ref, cot_ref, *rest, unit_tile):
    *block_refs, normed_ref, active_ref, grads_ref, part_ref, part_other_ref, wide_ref, sems = rest
    core_ref = ring_ref
    copies = put_weights(ring_ref, block_refs, wide_ref, sems, 0, wide_ref.shape[1])
    rows = own_ref.shape[0]
    units = active_ref.shape[1]
    gain = gain_ref[1:2, :]
    own_at = pl.multiple_of(core_ref[0] * rows, rows)
    other_at = pl.multiple_of((1 - core_ref[0]) * rows, rows)
    for ref, at in ((own_ref, own_at), (other_ref, other_at)):
        x = ref[...]
        scale_rows = lax.rsqrt(jnp.mean(x * x, -1, keepdims=True) + epsilon)
        normed_ref[pl.ds(at, rows), :] = (x * scale_rows * gain).astype(bf16)
    for copy in copies:
        copy.wait()

    @pl.loop(0, units // unit_tile)
    def unit_step(t):
        at = pl.multiple_of(t * unit_tile, unit_tile)
        cols = pl.ds(at, unit_tile)
        up_cols = pl.ds(pl.multiple_of(units + at, unit_tile), unit_tile)
        gate = dot(normed_ref[...], wide_ref[:, cols])
        up = dot(normed_ref[...], wide_ref[:, up_cols])
        grad_active = dot(cot_ref[...], wide_ref[:, pl.ds(pl.multiple_of(2 * units + at, unit_tile), unit_tile)])
        sig = jax.nn.sigmoid(gate)
        silu = gate * sig
        active_ref[:, cols] = (silu * up).astype(bf16)
        grads_ref[:, cols] = (grad_active * up * (sig * (1.0 + gate * (1.0 - sig)))).astype(bf16)
        grads_ref[:, up_cols] = (grad_active * silu).astype(bf16)

    model = normed_ref.shape[1]
    tile = model // 3

    @pl.loop(0, 3)
    def model_step(t):
        at = pl.ds(pl.multiple_of(t * tile, tile), tile)
        wide = wide_ref[at, : 2 * units]
        part_ref[:, at] = dot(grads_ref[pl.ds(own_at, rows), :], wide, 1, 1)
        part_other_ref[:, at] = dot(grads_ref[pl.ds(other_at, rows), :], wide, 1, 1).astype(bf16)


def feed_weights_kernel(n, count, place_ref, normed_ref, active_ref, grads_ref, cot_ref, *outs):
    weight_refs = outs[:count]
    *block_refs, out_ref, out_other_ref, buf, down_ref, sems = outs[count:]
    units = active_ref.shape[1]
    copies = put_weights(place_ref, weight_refs, down_ref, sems, 2 * units, units)
    rows = out_ref.shape[0]
    units = active_ref.shape[1]
    model = normed_ref.shape[1]
    tile = buf.shape[1]
    own_at = pl.multiple_of(place_ref[0] * rows, rows)
    other_at = pl.multiple_of((1 - place_ref[0]) * rows, rows)

    def put(values, at):
        if len(block_refs) == 1:
            block_refs[0][:, at] = values.astype(bf16)
            return
        buf[...] = values.astype(bf16)
        block = model // n
        for k in range(n):
            block_refs[k][:, at] = buf[pl.ds(pl.multiple_of(place_ref[1 + k] * block, block), block), :]

    @pl.loop(0, units // tile)
    def weight_step(t):
        for i in range(3):
            cols = pl.ds(pl.multiple_of(t * tile, tile), tile)
            at = pl.ds(pl.multiple_of(i * units + t * tile, tile), tile)
            if i < 2:
                put(dot(normed_ref[...], grads_ref[:, at], 0, 0), at)
            else:
                put(dot(cot_ref[...], active_ref[:, cols], 0, 0), at)

    wide_tile = model // 3
    for copy in copies:
        copy.wait()

    @pl.loop(0, 3)
    def out_step(t):
        at = pl.ds(pl.multiple_of(t * wide_tile, wide_tile), wide_tile)
        down = down_ref[at, :]
        out_ref[:, at] = dot(active_ref[pl.ds(own_at, rows), :], down, 1, 1)
        out_other_ref[:, at] = dot(active_ref[pl.ds(other_at, rows), :], down, 1, 1).astype(bf16)


def hidden_grad_kernel(
    core_ref, hidden_ref, mine_ref, came_ref, gains_ref, cot_ref, w_ref, grad_ref, attn_ref, mixed_ref, gain_ref
):
    rows = hidden_ref.shape[0]
    hidden = hidden_ref[...]
    grad_normed = mine_ref[...].astype(f32) + came_ref[...].astype(f32)
    scale_rows = lax.rsqrt(jnp.mean(hidden * hidden, -1, keepdims=True) + epsilon)
    unit = hidden * scale_rows
    gain_ref[...] = jnp.sum(grad_normed * unit, 0, keepdims=True)
    grad_unit = grad_normed * gains_ref[1:2, :]
    inner = jnp.mean(grad_unit * unit, -1, keepdims=True)
    cot = cot_ref[pl.ds(pl.multiple_of(core_ref[0] * rows, rows), rows), :].astype(f32)
    grad = cot + scale_rows * (grad_unit - unit * inner)
    grad_ref[...] = grad
    attn_ref[...] = grad.astype(bf16)
    mixed_ref[:, :HALF_Q] = dot(attn_ref[...], w_ref[:, PACK:]).astype(bf16)
    mixed_ref[:, HALF_Q:] = jnp.zeros((rows, HEAD), bf16)


def last_kernel(
    dkv_ref, dq_ref, cos_ref, sin_ref, w_ref, normed_ref, x_ref, grad_attn_ref, mixed_ref, gain_two_ref, *rest
):
    *came_refs, part_ref, dw_ref, lin_ref = rest
    cosine, sine = cos_ref[...], sin_ref[...]
    half = lane_half(cosine.shape)
    for s in range(3):
        cols = slice(s * SLAB, (s + 1) * SLAB)
        z = dkv_ref[:, cols]
        for ref in came_refs:
            z = z + ref[:, cols].astype(f32)
        turned = z * cosine - turn(z) * sine
        lin_ref[:, cols] = (turned if s == 0 else jnp.where(half == 0, turned, z) if s == 1 else z).astype(bf16)
    lin_ref[:, 3 * SLAB :] = dq_ref[...]
    x = x_ref[...].astype(f32)
    scale_rows = lax.rsqrt(jnp.mean(x * x, -1, keepdims=True) + epsilon)
    model = normed_ref.shape[1]
    tile = model // 3
    last = PACK - SLAB

    @pl.loop(0, 3)
    def model_step(t):
        at = pl.ds(pl.multiple_of(t * tile, tile), tile)
        part = dot(lin_ref[...], w_ref[at, :PACK], 1, 1)
        part_ref[:, at] = part.astype(bf16)
        unit = x_ref[:, at].astype(f32) * scale_rows
        gain_one = jnp.sum(part * unit, 0, keepdims=True)
        gain_one = jnp.broadcast_to(gain_one, (SLAB, tile)).T
        gain_two = jnp.broadcast_to(gain_two_ref[:, at], (SLAB, tile)).T
        dw = dot(normed_ref[:, at], lin_ref[...], 0, 0)
        dw_ref[at, :last] = dw[:, :last].astype(bf16)
        lane = lax.broadcasted_iota(jnp.int32, (tile, SLAB), 1)
        gains = jnp.where(lane < HEAD + HEAD // 2, gain_one, gain_two)
        dw_ref[at, last:PACK] = jnp.where(lane < HEAD, dw[:, last:], gains).astype(bf16)
        dw_ref[at, PACK:] = dot(grad_attn_ref[:, at], mixed_ref[:, :HALF_Q], 0, 0).astype(bf16)


def as_dealt(array, pieces):
    rows = array.shape[0]
    rest = array.shape[1:]
    axes = (0, 2, 1, 3) + tuple(4 + i for i in range(len(rest)))
    split = array.reshape((2, 2, pieces // 2, rows // (2 * pieces)) + rest)
    return jnp.transpose(split, axes).reshape((rows,) + rest)


def norm_backward(grad_normed, unit_rows, scale_rows, gain):
    grad_unit = grad_normed * gain
    grad_gain = jnp.sum(grad_normed * unit_rows, 0)
    grad_rows = scale_rows * (
        grad_unit - unit_rows * jnp.mean(grad_unit * unit_rows, -1, keepdims=True)
    )
    return grad_rows, grad_gain


def on_device(n, args):
    (inputs, cotangent, segments, pair_order, gain_attn, w_query, w_key, w_value, w_out, gain_mlp,
     w_gate, w_up, w_down) = args
    local_rows, model = inputs.shape
    pieces = PIECES
    own_rows = local_rows // 2
    run_rows = own_rows // 2
    part_rows = gain_attn.shape[0]
    ctx_rows = gain_mlp.shape[0]
    pair_rows = ctx_rows // 2
    units = w_gate.shape[1]
    blocks = 2 * n
    ctx_index = lax.axis_index("ctx")
    wa_index = lax.axis_index("wa")
    x_index, core_index = wa_index // 2, wa_index % 2

    def both_halves(array, width):
        return array[:, :width], array[:, width:]

    q_halves = both_halves(w_query, HALF_Q)
    k_halves = both_halves(w_key, HALF_KV)
    v_halves = both_halves(w_value, HALF_KV)
    gain_two_part = lax.dynamic_slice_in_dim(gain_mlp, wa_index * part_rows, part_rows)
    gain_cols = jnp.concatenate(
        [jnp.broadcast_to(g[:, None], (part_rows, HEAD // 2)) for g in (gain_attn, gain_two_part)], 1
    )
    out_halves = both_halves(w_out.T, HALF_Q)
    halves = [
        jnp.concatenate([k_halves[i], v_halves[i], q_halves[i], gain_cols, out_halves[i]], 1)
        for i in range(2)
    ]

    half_ring = n // 2

    def gather_rows(halves, wide_block, prepared):
        mine = jnp.where(x_index == 0, halves[0], halves[1])
        theirs = jnp.where(x_index == 0, halves[1], halves[0])
        came, prepared, wide_block = lax.optimization_barrier((x_swap(theirs), prepared, wide_block))
        low = jnp.where(x_index == 0, mine, came)
        high = jnp.where(x_index == 0, came, mine)
        pair = jnp.stack([low, high])
        other = core_swap(pair)
        zero = jnp.where(core_index == 0, pair, other)
        one = jnp.where(core_index == 0, other, pair)
        quad = jnp.stack([zero, one], 1).reshape(ctx_rows, -1)
        sent = lax.dynamic_slice_in_dim(quad, core_index * pair_rows, pair_rows, 0)
        held = ring_gather(sent, n)
        wide = {0: wide_block}
        for step in range(1, half_ring - 2):
            wide = ring_gather_step(wide, step, n)
        held, wide = lax.optimization_barrier((held, wide))
        ordered = jnp.zeros((n,) + sent.shape, bf16)
        for k in range(n):
            ordered = lax.dynamic_update_index_in_dim(ordered, held[k], ring_id(ctx_index, k, n), 0)
        held = ordered
        opposite = core_swap(held)
        whole = jnp.where(
            core_index == 0,
            jnp.concatenate([held, opposite], 1),
            jnp.concatenate([opposite, held], 1),
        )
        return whole.reshape(n * ctx_rows, -1), wide, prepared

    at = jnp.stack([ctx_index, core_index]).astype(jnp.int32)
    table, ring, rows_info, cosine, sine, x_own, run_cotangent = pl.pallas_call(
        functools.partial(prepare_kernel, n),
        out_shape=(
            jax.ShapeDtypeStruct((blocks + 9,), jnp.int32),
            jax.ShapeDtypeStruct((n + 1,), jnp.int32),
            jax.ShapeDtypeStruct((4, GROUP * run_rows), jnp.int32),
            jax.ShapeDtypeStruct((own_rows, SLAB), f32),
            jax.ShapeDtypeStruct((own_rows, SLAB), f32),
            jax.ShapeDtypeStruct((own_rows, model), bf16),
            jax.ShapeDtypeStruct((local_rows, model), bf16),
        ),
        in_specs=[smem()] * 2 + [vmem()] * 3,
        out_specs=(smem(),) * 2 + (vmem(),) * 5,
        compiler_params=params(),
        cost_estimate=cost(6),
    )(at, pair_order, segments.reshape(-1, local_rows // PIECES), inputs, cotangent)

    wide_block = jnp.concatenate([w_gate, w_up, w_down.T], 1)
    prepared = (table, ring, rows_info, cosine, sine, x_own, run_cotangent)
    w_all, wide, prepared = gather_rows(halves, wide_block, prepared)
    table, ring, rows_info, cosine, sine, x_own, run_cotangent = prepared
    w_out_t = w_all[:, PACK:]
    normed, queries, kv_own, gains = pl.pallas_call(
        project_kernel,
        out_shape=(
            jax.ShapeDtypeStruct((own_rows, model), bf16),
            jax.ShapeDtypeStruct((own_rows, Q_WIDE), bf16),
            jax.ShapeDtypeStruct((own_rows, 2 * HALF_KV), bf16),
            jax.ShapeDtypeStruct((2, model), f32),
        ),
        in_specs=[vmem()] * 4,
        out_specs=(vmem(),) * 4,
        compiler_params=params(),
        cost_estimate=cost(5),
    )(x_own, w_all, cosine, sine)

    kv_found = ring_gather(kv_own, n)
    kv_core = jnp.concatenate([kv_found[k] for k in range(n)], 0)
    kv_other = core_swap(kv_core)
    wide, kv_core, kv_other = lax.optimization_barrier((wide, kv_core, kv_other))
    wide = ring_gather_step(wide, half_ring - 2, n)

    mixed, mixed_b, log_total = pl.pallas_call(
        functools.partial(forward_kernel, blocks),
        out_shape=(
            jax.ShapeDtypeStruct((own_rows, Q_WIDE), f32),
            jax.ShapeDtypeStruct((own_rows, Q_WIDE), bf16),
            jax.ShapeDtypeStruct((8, GROUP * run_rows), f32),
        ),
        in_specs=[smem()] + [vmem()] * 4,
        out_specs=(vmem(),) * 3,
        scratch_shapes=[
            pltpu.VMEM((HALF_GROUPS * SLAB, GROUP * run_rows), f32),
            pltpu.VMEM((8 * HALF_GROUPS, GROUP * run_rows), f32),
            pltpu.VMEM((8 * HALF_GROUPS, GROUP * run_rows), f32),
        ],
        compiler_params=params(14 + n // 2),
        cost_estimate=cost(16),
    )(table, queries, kv_core, kv_other, rows_info)

    wide, mixed_b = lax.optimization_barrier((wide, mixed_b))
    wide = ring_gather_step(wide, half_ring - 1, n)
    attn_part = rounded(dot(mixed_b[:, :HALF_Q], w_all[:, PACK:], 1, 1))
    attn_came = x_swap(attn_part)
    wide, attn_came = lax.optimization_barrier((wide, attn_came))
    wide = ring_gather_step(wide, half_ring, n)
    x_f = x_own.astype(f32)
    hidden_own = x_f + (attn_part.astype(f32) + attn_came.astype(f32))
    hidden_other = core_swap(hidden_own)
    wide, hidden_other = lax.optimization_barrier((wide, hidden_other))
    wide = [wide[k] for k in range(n)]
    whole_tiles = ctx_rows % 16 == 0
    if not whole_tiles:
        wide_full = jnp.zeros((n,) + wide_block.shape, bf16)
        for k in range(n):
            wide_full = lax.dynamic_update_index_in_dim(wide_full, wide[k], ring_id(ctx_index, k, n), 0)
        wide = [wide_full.reshape(model, 3 * units)]

    def join(own, other):
        return jnp.where(
            core_index == 0, jnp.concatenate([own, other], 0), jnp.concatenate([other, own], 0)
        )

    normed_two, active, grads_wide, grad_two_own, grad_two_other = pl.pallas_call(
        functools.partial(feed_kernel, unit_tile=min(256, units)),
        out_shape=(
            jax.ShapeDtypeStruct((local_rows, model), bf16),
            jax.ShapeDtypeStruct((local_rows, units), bf16),
            jax.ShapeDtypeStruct((local_rows, 2 * units), bf16),
            jax.ShapeDtypeStruct((own_rows, model), f32),
            jax.ShapeDtypeStruct((own_rows, model), bf16),
        ),
        in_specs=[smem()] + [vmem()] * 4 + [pl.BlockSpec(memory_space=pl.ANY)] * len(wide),
        out_specs=(vmem(),) * 5,
        scratch_shapes=[
            pltpu.VMEM((model, 3 * units), bf16),
            pltpu.SemaphoreType.DMA((len(wide),)),
        ],
        compiler_params=params(),
        cost_estimate=cost(12),
    )(ring, hidden_own, hidden_other, gains, run_cotangent, *wide)
    shapes = (
        (jax.ShapeDtypeStruct((ctx_rows, 3 * units), bf16),) * n
        if whole_tiles
        else (jax.ShapeDtypeStruct((model, 3 * units), bf16),)
    )
    unit_tile = min(256, units)
    *d_terms, mlp_own, mlp_other = pl.pallas_call(
        functools.partial(feed_weights_kernel, n, len(wide)),
        out_shape=shapes
        + (
            jax.ShapeDtypeStruct((own_rows, model), f32),
            jax.ShapeDtypeStruct((own_rows, model), bf16),
        ),
        in_specs=[smem()] + [vmem()] * 4 + [pl.BlockSpec(memory_space=pl.ANY)] * len(wide),
        out_specs=(vmem(),) * (len(shapes) + 2),
        scratch_shapes=[
            pltpu.VMEM((model, unit_tile), bf16),
            pltpu.VMEM((model, units), bf16),
            pltpu.SemaphoreType.DMA((len(wide),)),
        ],
        compiler_params=params(),
        cost_estimate=cost(9),
    )(ring, normed_two, active, grads_wide, run_cotangent, *wide)
    if not whole_tiles:
        d_blocks = d_terms[0].reshape(n, ctx_rows, 3 * units)
        d_terms = [
            lax.dynamic_index_in_dim(d_blocks, ring_id(ctx_index, k, n), 0, keepdims=False) for k in range(n)
        ]
    def chip_sum(own, other):
        return rounded(own + core_swap(other).astype(f32))

    grad_two = chip_sum(grad_two_own, grad_two_other)
    grad_two_came, d_terms, mlp_own = lax.optimization_barrier((x_swap(grad_two), d_terms, mlp_own))
    d_came = None
    for step in range(1, half_ring - 2):
        d_came = ring_scatter_step(d_terms, d_came, step, n)
    output_chip = chip_sum(mlp_own, mlp_other)
    grad_hidden, grad_attn, grad_mixed, grad_gain_two = pl.pallas_call(
        hidden_grad_kernel,
        out_shape=(
            jax.ShapeDtypeStruct((own_rows, model), f32),
            jax.ShapeDtypeStruct((own_rows, model), bf16),
            jax.ShapeDtypeStruct((own_rows, Q_WIDE), bf16),
            jax.ShapeDtypeStruct((1, model), f32),
        ),
        in_specs=[smem()] + [vmem()] * 6,
        out_specs=(vmem(),) * 4,
        compiler_params=params(),
        cost_estimate=cost(5),
    )(ring, hidden_own, grad_two, grad_two_came, gains, run_cotangent, w_all)
    d_came, grad_mixed, output_chip = lax.optimization_barrier((d_came, grad_mixed, output_chip))
    d_came = ring_scatter_step(d_terms, d_came, half_ring - 2, n)

    dq_lin, dkv_core, dkv_other = pl.pallas_call(
        functools.partial(backward_kernel, blocks),
        out_shape=(
            jax.ShapeDtypeStruct((own_rows, Q_WIDE), bf16),
            jax.ShapeDtypeStruct(kv_core.shape, f32),
            jax.ShapeDtypeStruct(kv_core.shape, bf16),
        ),
        in_specs=[smem()] + [vmem()] * 9,
        out_specs=(vmem(),) * 3,
        scratch_shapes=[
            pltpu.VMEM((2 * SLAB, HEADS // 2 * run_rows), f32),
            pltpu.VMEM((own_rows, Q_WIDE), f32),
            pltpu.VMEM(kv_core.shape, f32),
            pltpu.VMEM((HEADS // 2 * run_rows, 2 * SLAB), bf16),
            pltpu.VMEM((HEADS // 2 * run_rows, 2 * SLAB), bf16),
        ],
        compiler_params=params(12 + 2 * n),
        cost_estimate=cost(24),
    )(table, queries, kv_core, kv_other, rows_info, mixed, log_total, grad_mixed, cosine, sine)

    def scatter_rows(part, crossing):
        cols = part.shape[1]
        split = part.reshape(n, 2, pair_rows, cols)
        mine = lax.dynamic_index_in_dim(split, core_index, 1, keepdims=False)
        theirs = lax.dynamic_index_in_dim(split, 1 - core_index, 1, keepdims=False)
        chip = mine.astype(f32) + core_swap(theirs).astype(f32)
        terms = [lax.dynamic_index_in_dim(chip, ring_id(ctx_index, k, n), 0, keepdims=False) for k in range(n)]
        came, crossed = ring_scatter(terms, n, x_swap(crossing))
        total = terms[0] + came[0].astype(f32) + came[1].astype(f32)
        total_b = total.astype(bf16)
        opposite = core_swap(total_b)
        rows = jnp.where(
            core_index == 0,
            jnp.concatenate([total_b, opposite], 0),
            jnp.concatenate([opposite, total_b], 0),
        )
        quad = rows.reshape(2, 2, part_rows, cols)
        kept = lax.dynamic_index_in_dim(
            lax.dynamic_index_in_dim(quad, x_index, 0, keepdims=False), core_index, 0, keepdims=False
        )
        sent = lax.dynamic_index_in_dim(
            lax.dynamic_index_in_dim(quad, 1 - x_index, 0, keepdims=False), core_index, 0, keepdims=False
        )
        came = x_swap(sent)
        low = jnp.where(x_index == 0, kept, came).astype(f32)
        high = jnp.where(x_index == 0, came, kept).astype(f32)
        return rows, low, high, crossed

    dkv_other, d_came = lax.optimization_barrier((dkv_other, d_came))
    d_came = ring_scatter_step(d_terms, d_came, half_ring - 1, n)
    dkv = dkv_core + core_swap(dkv_other).astype(f32)
    dkv = dkv.reshape(n, own_rows, 2 * HALF_KV)
    dkv_own, dkv_came = dkv[0], ring_scatter(dkv, n)
    output_came = x_swap(output_chip)
    dkv_came, d_came, output_came = lax.optimization_barrier((dkv_came, d_came, output_came))
    d_came = ring_scatter_step(d_terms, d_came, half_ring, n)
    output_own = (hidden_own + (output_chip.astype(f32) + output_came.astype(f32))).astype(bf16)
    output = as_dealt(join(output_own, core_swap(output_own)), pieces)
    normed_part, d_in = pl.pallas_call(
        last_kernel,
        out_shape=(
            jax.ShapeDtypeStruct((own_rows, model), bf16),
            jax.ShapeDtypeStruct((model, PACK + HALF_Q), bf16),
        ),
        in_specs=[vmem()] * (10 + len(dkv_came)),
        out_specs=(vmem(),) * 2,
        scratch_shapes=[pltpu.VMEM((own_rows, PACK), bf16)],
        compiler_params=params(),
        cost_estimate=cost(5),
    )(dkv_own, dq_lin, cosine, sine, w_all, normed, x_own, grad_attn, mixed_b, grad_gain_two, *dkv_came)
    d_in, d_came = lax.optimization_barrier((d_in, d_came))
    in_rows, in_low, in_high, normed_came = scatter_rows(d_in, normed_part)
    d_mlp = d_terms[0].astype(f32) + d_came[0].astype(f32) + d_came[1].astype(f32)
    grad_w_gate = d_mlp[:, :units]
    grad_w_up = d_mlp[:, units : 2 * units]
    grad_w_down = d_mlp[:, 2 * units :].T

    k_end, v_end, q_end = HALF_KV, 2 * HALF_KV, 2 * HALF_KV + HALF_Q
    grad_w_key = jnp.concatenate([in_low[:, :k_end], in_high[:, :k_end]], 1)
    grad_w_value = jnp.concatenate([in_low[:, k_end:v_end], in_high[:, k_end:v_end]], 1)
    grad_w_query = jnp.concatenate([in_low[:, v_end:q_end], in_high[:, v_end:q_end]], 1)

    grad_normed = normed_part.astype(f32) + normed_came.astype(f32)
    scale_one = lax.rsqrt(jnp.mean(x_f * x_f, -1, keepdims=True) + epsilon)
    input_rows, unused_gain = norm_backward(grad_normed, x_f * scale_one, scale_one, gains[:1])
    grad_inputs_own = (grad_hidden + input_rows).astype(bf16)
    grad_inputs = as_dealt(join(grad_inputs_own, core_swap(grad_inputs_own)), pieces)
    grad_w_out = jnp.concatenate([in_low[:, PACK:], in_high[:, PACK:]], 1).T
    grad_gain_attn = in_low[:, q_end] + in_high[:, q_end]
    grad_gain_mlp = in_rows[:, PACK - 1].astype(f32)
    return (
        output,
        grad_inputs,
        grad_gain_attn,
        grad_w_query,
        grad_w_key,
        grad_w_value,
        grad_w_out,
        grad_gain_mlp,
        grad_w_gate,
        grad_w_up,
        grad_w_down,
    )


def solution(mesh):
    n = mesh.shape["ctx"]

    def body(*args):
        return on_device(n, args)

    return jax.shard_map(
        body,
        mesh=mesh,
        in_specs=(
            P("ctx", None),
            P("ctx", None),
            P(),
            P(),
            P(("ctx", "wa")),
            P(("ctx", "wa"), None),
            P(("ctx", "wa"), None),
            P(("ctx", "wa"), None),
            P(None, ("ctx", "wa")),
            P("ctx"),
            P("ctx", "wa"),
            P("ctx", "wa"),
            P("wa", "ctx"),
        ),
        out_specs=(
            P("ctx", None),
            P("ctx", None),
            P(("ctx", "wa")),
            P(("ctx", "wa"), None),
            P(("ctx", "wa"), None),
            P(("ctx", "wa"), None),
            P(None, ("ctx", "wa")),
            P("ctx"),
            P("ctx", "wa"),
            P("ctx", "wa"),
            P("wa", "ctx"),
        ),
        check_vma=False,
    )
```

```python
import functools
import math

import jax
import jax.numpy as jnp
from jax import lax
from jax.experimental import pallas as pl
from jax.experimental.pallas import tpu as pltpu
from jax.sharding import PartitionSpec as P

HEADS = 18
KV_HEADS = 6
HEAD = 64
GROUP = HEADS // KV_HEADS
HALF_Q = HEADS * HEAD // 2
HALF_KV = KV_HEADS * HEAD // 2
HALF_GROUPS = KV_HEADS // 2
SLAB = 128
PACK = 2 * HALF_KV + HALF_Q + HEAD
Q_WIDE = HALF_Q + HEAD

epsilon = 1e-05
rope_base = 10000.0
masked_score = -1e30
DOCS = 16
PIECES = 4
f32 = jnp.float32
bf16 = jnp.bfloat16
MIB = 1024 * 1024

K_PLACE = [divmod(g, 2) for g in range(HALF_GROUPS)]
V_PLACE = [divmod(HALF_GROUPS + g, 2) for g in range(HALF_GROUPS)]


def vmem():
    return pl.BlockSpec(memory_space=pltpu.VMEM)


def smem():
    return pl.BlockSpec(memory_space=pltpu.SMEM)


def params(mib=26):
    return pltpu.CompilerParams(vmem_limit_bytes=min(mib, 58) * MIB)


def cost(micros):
    return pl.CostEstimate(flops=int(micros * 1e9), bytes_accessed=0, transcendentals=0)


def dot(a, b, ca=1, cb=0):
    return lax.dot_general(a, b, (((ca,), (cb,)), ((), ())), preferred_element_type=f32)


def ctx_parts(n):
    slow = min(4, n)
    return slow, n // slow


def ctx_swap(block, n, k):
    return lax.ppermute(block, "ctx", [(i, i ^ k) for i in range(n)])


def wa_swap(block, k):
    return lax.ppermute(block, "wa", [(i, i ^ k) for i in range(4)])


def core_swap(block):
    return wa_swap(block, 1)


def x_swap(block):
    return wa_swap(block, 2)


def ring_order(n):
    slow, fast = ctx_parts(n)
    order = []
    for r in range(fast):
        line = [z * fast + r for z in range(slow)]
        order += line if r % 2 == 0 else line[::-1]
    return order


def ring_id(ctx, offset, n):
    slow, fast = ctx_parts(n)

    def along(r, z):
        return jnp.where(r % 2 == 0, z, slow - 1 - z)

    place = (ctx % fast) * slow + along(ctx % fast, ctx // fast)
    place = (place + offset) % n
    r = place // slow
    return along(r, place % slow) * fast + r


def ring_send(forward, backward, n):
    order = ring_order(n)
    pairs = [(order[p], order[(p + 1) % n]) for p in range(n)]
    return (
        lax.ppermute(forward, "ctx", pairs),
        lax.ppermute(backward, "ctx", [(b, a) for a, b in pairs]),
    )


def ring_gather_step(found, step, n):
    half_ring = n // 2
    f, b = found[(1 - step) % n], found[step - 1]
    if step == half_ring:
        half = f.shape[0] // 2
        parts = ring_send(f[:half], b[half:], n)
        return found | {half_ring: jnp.concatenate(parts, 0)}
    f, b = ring_send(f, b, n)
    return found | {n - step: f, step: b}


def ring_scatter_step(terms, came, step, n):
    half_ring = n // 2
    far = terms[half_ring]
    half = far.shape[0] // 2
    if step == 1:
        return ring_send(far[:half].astype(bf16), far[half:].astype(bf16), n)
    d = half_ring - step + 1
    f, b = terms[d].astype(f32), terms[n - d].astype(f32)
    came_f, came_b = came[0].astype(f32), came[1].astype(f32)
    if step == 2:
        rest = jnp.zeros_like(far[half:], f32)
        came_f = jnp.concatenate([came_f, rest], 0)
        came_b = jnp.concatenate([jnp.zeros_like(far[:half], f32), came_b], 0)
    return ring_send((f + came_f).astype(bf16), (b + came_b).astype(bf16), n)


def ring_gather(block, n):
    found = {0: block}
    for step in range(1, n // 2 + 1):
        found = ring_gather_step(found, step, n)
    return found


def ring_scatter(terms, n, beside=None):
    came = None
    beside = dict(beside or {})
    for step in range(1, n // 2 + 1):
        came = ring_scatter_step(terms, came, step, n)
        if step in beside:
            came, beside[step] = lax.optimization_barrier((came, beside[step]))
    return came, list(beside.values())


def rounded(array):
    return lax.optimization_barrier(array.astype(bf16))


def lane_half(shape):
    lane = lax.broadcasted_iota(jnp.int32, shape, 1)
    return lane // HEAD


def turn(z):
    lane = lax.broadcasted_iota(jnp.int32, z.shape, 1)
    return jnp.where(
        lane % HEAD < HEAD // 2,
        pltpu.roll(z, SLAB - HEAD // 2, 1),
        pltpu.roll(z, HEAD // 2, 1),
    )


def prepare_kernel(
    n, at_ref, pairs_ref, segments_ref, x_ref, cot_ref, table_ref, ring_ref, rows_ref, cos_ref, sin_ref, own_ref, cots_ref
):
    ctx, core = at_ref[0], at_ref[1]
    own_rows = own_ref.shape[0]
    run_rows = own_rows // 2
    piece = run_rows // 2
    blocks = 2 * n
    lower = pairs_ref[ctx]
    for c in range(2):
        for run in range(2):
            for p in range(2):
                to = c * own_rows + run * run_rows + p * piece
                source = (2 * c + p) * 2 * piece + run * piece
                cots_ref[to : to + piece, :] = cot_ref[source : source + piece, :]
    for run in range(2):
        for p in range(2):
            to = run * run_rows + p * piece
            source = pl.multiple_of((2 * core + p) * 2 * piece + run * piece, piece)
            own_ref[to : to + piece, :] = x_ref[pl.ds(source, piece), :]
    ring_ref[0] = core
    for k in range(n):
        ring_ref[1 + k] = ring_id(ctx, k, n)
    for k in range(n):
        low = pairs_ref[ring_ref[1 + k]]
        table_ref[low] = 2 * k
        table_ref[blocks - 1 - low] = 2 * k + 1
    counts = []
    every = segments_ref[...]
    for d in range(DOCS):
        here = (every == d + 1).astype(f32)
        counts.append(jnp.sum(here, 0, keepdims=True))
    count = jnp.sum(jnp.concatenate(counts, 0), 1, keepdims=True)
    docs = lax.broadcasted_iota(jnp.int32, (DOCS, run_rows), 0) + 1
    lane = lax.broadcasted_iota(jnp.int32, (1, run_rows), 1)
    first_piece = segments_ref[pl.ds(ctx * PIECES + 2 * core, 1), :]
    second_piece = segments_ref[pl.ds(ctx * PIECES + 2 * core + 1, 1), :]
    runs = (
        jnp.where(lane < piece, first_piece, pltpu.roll(second_piece, piece, 1)),
        jnp.where(lane < piece, pltpu.roll(first_piece, piece, 1), second_piece),
    )
    table_ref[blocks] = core
    for run in range(2):
        block = lower if run == 0 else blocks - 1 - lower
        position = block * (2 * run_rows) + core * run_rows + lane
        earlier = jnp.where(docs < runs[run], count, 0.0)
        start = jnp.sum(earlier, 0, keepdims=True)
        start = jnp.where(runs[run] > 0, start, position.astype(f32))
        first = jnp.min(start).astype(jnp.int32) // (2 * run_rows)
        latest = (jnp.max(start).astype(jnp.int32) + 2 * run_rows - 1) // (2 * run_rows)
        whole_from = jnp.minimum(jnp.maximum(latest, first), block + 1)
        whole_to = jnp.maximum(block, whole_from)
        for i, value in enumerate((first, whole_from, whole_to, block + 1)):
            table_ref[blocks + 1 + 4 * run + i] = value
        start = start.astype(jnp.int32)
        rows_ref[2 * run : 2 * run + 1, :] = jnp.concatenate([start] * GROUP, 1)
        rows_ref[2 * run + 1 : 2 * run + 2, :] = jnp.concatenate([position] * GROUP, 1)
    lanes = lax.broadcasted_iota(jnp.int32, (run_rows, SLAB), 1)
    row = lax.broadcasted_iota(jnp.int32, (run_rows, SLAB), 0)
    frequency = jnp.exp(-math.log(rope_base) * 2.0 * (lanes % (HEAD // 2)).astype(f32) / HEAD)
    for run in range(2):
        block = lower if run == 0 else blocks - 1 - lower
        angle = (block * (2 * run_rows) + core * run_rows + row).astype(f32) * frequency
        at = slice(run * run_rows, (run + 1) * run_rows)
        cos_ref[at, :] = jnp.cos(angle)
        sine = jnp.sin(angle)
        sin_ref[at, :] = jnp.where(lanes % HEAD < HEAD // 2, -sine, sine)


def project_kernel(x_ref, w_ref, cos_ref, sin_ref, normed_ref, q_ref, kv_ref, gains_ref):
    tail = w_ref[:, PACK - SLAB : PACK].astype(f32).T
    gains_ref[0:1, :] = tail[SLAB - HEAD : SLAB - HEAD + 1, :]
    gains_ref[1:2, :] = tail[SLAB - 1 :, :]
    gain_ref = gains_ref.at[0:1, :]
    x = x_ref[...].astype(f32)
    scale_rows = lax.rsqrt(jnp.mean(x * x, -1, keepdims=True) + epsilon)
    normed = (x * scale_rows * gain_ref[...]).astype(bf16)
    normed_ref[...] = normed
    cosine, sine = cos_ref[...], sin_ref[...]
    half = lane_half(cosine.shape)
    for s in range(PACK // SLAB):
        z = dot(normed, w_ref[:, s * SLAB : (s + 1) * SLAB])
        if s == 2:
            kv_ref[:, 2 * SLAB : 3 * SLAB] = z.astype(bf16)
            continue
        turned = z * cosine + turn(z) * sine
        if s == 0:
            kv_ref[:, :SLAB] = turned.astype(bf16)
        elif s == 1:
            kv_ref[:, SLAB : 2 * SLAB] = jnp.where(half == 0, turned, z).astype(bf16)
        else:
            scaled = turned * HEAD ** (-0.5)
            if s == PACK // SLAB - 1:
                scaled = jnp.where(half == 0, scaled, 0.0)
            q_ref[:, (s - 3) * SLAB : (s - 2) * SLAB] = scaled.astype(bf16)


def head_rows(ref, run, rows, g, place):
    parts = []
    for j in range(GROUP):
        slab, half = divmod(GROUP * g + j, 2)
        z = ref[run * rows : (run + 1) * rows, slab * SLAB : (slab + 1) * SLAB].astype(f32)
        if half != place:
            z = pltpu.roll(z, HEAD, 1)
        parts.append(jnp.where(lane_half(z.shape) == place, z, 0.0).astype(bf16))
    return jnp.concatenate(parts, 0)


def put_heads(ref, values, run, rows, g, place):
    flat = values.T
    for j in range(GROUP):
        slab, half = divmod(GROUP * g + j, 2)
        z = flat[j * rows : (j + 1) * rows, :]
        if half != place:
            z = pltpu.roll(z, HEAD, 1)
        where = (slice(run * rows, (run + 1) * rows), slice(slab * SLAB, (slab + 1) * SLAB))
        if half == 0:
            ref[where] = jnp.where(lane_half(z.shape) == 0, z, 0.0)
        else:
            ref[where] = jnp.where(lane_half(z.shape) == 1, z, ref[where])


def key_block(own_ref, other_ref, slot, rows, slab):
    at = pl.ds(pl.multiple_of(slot * rows, rows), rows)
    cols = slice(slab * SLAB, (slab + 1) * SLAB)
    return jnp.concatenate([own_ref[at, cols], other_ref[at, cols]], 0)


def key_places(block, core, rows, width):
    i = lax.broadcasted_iota(jnp.int32, (2 * rows, width), 0)
    mine = i + core * rows
    others = i - core * rows
    return block * (2 * rows) + jnp.where(i < rows, mine, others)


def forward_kernel(
    blocks, table, q_ref, own_ref, other_ref, rows_ref, mixed_ref, mixed_b_ref, log_ref, acc_ref, sum_ref, max_ref
):
    rows = q_ref.shape[0] // 2
    width = GROUP * rows
    core = table[blocks]
    for run in range(2):
        first, mid0, mid1, last = [table[blocks + 1 + 4 * run + i] for i in range(4)]
        start = rows_ref[2 * run : 2 * run + 1, :]
        stop = rows_ref[2 * run + 1 : 2 * run + 2, :]
        queries = [head_rows(q_ref, run, rows, g, K_PLACE[g][1]) for g in range(HALF_GROUPS)]
        acc_ref[...] = jnp.zeros_like(acc_ref)
        sum_ref[...] = jnp.zeros_like(sum_ref)
        max_ref[...] = jnp.full_like(max_ref, masked_score)

        def step(b, carry, masked):
            at_rows = pl.ds(pl.multiple_of(table[b] * rows, rows), rows)
            if masked:
                at = key_places(b, core, rows, width)
                ok = (at >= start) & (at <= stop)
            scores = []
            for g in range(HALF_GROUPS):
                cols = slice(K_PLACE[g][0] * SLAB, (K_PLACE[g][0] + 1) * SLAB)
                keys = jnp.concatenate([own_ref[at_rows, cols], other_ref[at_rows, cols]], 0)
                s = dot(keys, queries[g], 1, 1)
                if masked:
                    s = jnp.where(ok, s, masked_score)
                scores.append(s)
            for g in range(HALF_GROUPS):
                s = scores[g]
                cols = slice(V_PLACE[g][0] * SLAB, (V_PLACE[g][0] + 1) * SLAB)
                values = jnp.concatenate([own_ref[at_rows, cols], other_ref[at_rows, cols]], 0)
                before = max_ref[8 * g : 8 * g + 1, :]
                high = jnp.maximum(before, jnp.max(s, 0, keepdims=True))
                keep = jnp.exp(before - high)
                p = jnp.exp(s - high)
                max_ref[8 * g : 8 * g + 1, :] = high
                sum_ref[8 * g : 8 * g + 1, :] = sum_ref[8 * g : 8 * g + 1, :] * keep + jnp.sum(p, 0, keepdims=True)
                rows_g = slice(g * SLAB, (g + 1) * SLAB)
                acc_ref[rows_g, :] = acc_ref[rows_g, :] * keep + dot(values, p.astype(bf16), 0, 0)
            return carry

        lax.fori_loop(first, mid0, functools.partial(step, masked=True), 0)
        lax.fori_loop(mid0, mid1, functools.partial(step, masked=False), 0)
        lax.fori_loop(mid1, last, functools.partial(step, masked=True), 0)
        for g in range(HALF_GROUPS):
            total = sum_ref[8 * g : 8 * g + 1, :]
            log_ref[run * HALF_GROUPS + g : run * HALF_GROUPS + g + 1, :] = max_ref[8 * g : 8 * g + 1, :] + jnp.log(total)
            put_heads(mixed_ref, acc_ref[g * SLAB : (g + 1) * SLAB, :] * (1.0 / total), run, rows, g, V_PLACE[g][1])
    mixed_b_ref[...] = mixed_ref[...].astype(bf16)


def wide_rows(ref, run, rows, places, base):
    parts = []
    for g in range(HALF_GROUPS):
        slab, half = places[g]
        z = head_rows(ref, run, rows, g, half)
        zero = jnp.zeros_like(z)
        parts.append(jnp.concatenate([z, zero] if slab == base else [zero, z], 1))
    return jnp.concatenate(parts, 0)


def backward_kernel(blocks,
    table, q_ref, own_ref, other_ref, rows_ref, mixed_ref, log_ref, grad_ref, cos_ref, sin_ref,
    dq_ref, down_ref, dother_out, dq_buf, raw_buf, dother_ref, q_buf, g_buf):
    rows = q_ref.shape[0] // 2
    width = GROUP * rows
    core = table[blocks]
    down_ref[...] = jnp.zeros_like(down_ref)
    dother_ref[...] = jnp.zeros_like(dother_ref)
    for run in range(2):
        first, mid0, mid1, last = [table[blocks + 1 + 4 * run + i] for i in range(4)]
        start = rows_ref[2 * run : 2 * run + 1, :]
        stop = rows_ref[2 * run + 1 : 2 * run + 2, :]
        q_buf[...] = wide_rows(q_ref, run, rows, K_PLACE, 0)
        g_buf[...] = wide_rows(grad_ref, run, rows, V_PLACE, 1)
        logs, deltas = [], []
        for g in range(HALF_GROUPS):
            logs.append(log_ref[run * HALF_GROUPS + g : run * HALF_GROUPS + g + 1, :])
            parts = []
            for j in range(GROUP):
                slab, half = divmod(GROUP * g + j, 2)
                where = (slice(run * rows, (run + 1) * rows), slice(slab * SLAB, (slab + 1) * SLAB))
                z = grad_ref[where].astype(f32) * mixed_ref[where]
                z = jnp.where(lane_half(z.shape) == half, z, 0.0)
                parts.append(jnp.sum(z.T, 0, keepdims=True))
            deltas.append(jnp.concatenate(parts, 1))
        log_all = jnp.concatenate(logs, 1)
        delta_all = jnp.concatenate(deltas, 1)
        dq_buf[...] = jnp.zeros_like(dq_buf)

        def step(b, carry, masked):
            at_rows = pl.ds(pl.multiple_of(table[b] * rows, rows), rows)
            keys = jnp.concatenate([own_ref[at_rows, : 2 * SLAB], other_ref[at_rows, : 2 * SLAB]], 0)
            vals = jnp.concatenate([own_ref[at_rows, SLAB:], other_ref[at_rows, SLAB:]], 0)
            if masked:
                at = key_places(b, core, rows, width)
                ok = (at >= start) & (at <= stop)
            ps, dss = [], []
            for g in range(HALF_GROUPS):
                rg = slice(g * width, (g + 1) * width)
                s = dot(keys, q_buf[rg, :], 1, 1)
                p = jnp.exp(s - log_all[:, rg])
                if masked:
                    p = jnp.where(ok, p, 0.0)
                dp = dot(vals, g_buf[rg, :], 1, 1)
                ps.append(p.astype(bf16))
                dss.append((p * (dp - delta_all[:, rg])).astype(bf16))
            ds = jnp.concatenate(dss, 1)
            p = jnp.concatenate(ps, 1)
            dq_buf[...] += dot(keys, ds, 0, 0)
            dk = dot(ds, q_buf[...])
            dv = dot(p, g_buf[...])
            for i, val in ((0, dk[:, :SLAB]), (1, dk[:, SLAB:] + dv[:, :SLAB]), (2, dv[:, SLAB:])):
                cols = slice(i * SLAB, (i + 1) * SLAB)
                down_ref[at_rows, cols] += val[:rows]
                dother_ref[at_rows, cols] += val[rows:]
            return carry

        lax.fori_loop(first, mid0, functools.partial(step, masked=True), 0)
        lax.fori_loop(mid0, mid1, functools.partial(step, masked=False), 0)
        lax.fori_loop(mid1, last, functools.partial(step, masked=True), 0)
        for g in range(HALF_GROUPS):
            slab, half = K_PLACE[g]
            put_heads(raw_buf, dq_buf[slab * SLAB : (slab + 1) * SLAB, g * width : (g + 1) * width], run, rows, g, half)
    dother_out[...] = dother_ref[...].astype(bf16)
    cosine, sine = cos_ref[...], sin_ref[...]
    for s in range(Q_WIDE // SLAB):
        z = raw_buf[:, s * SLAB : (s + 1) * SLAB] * HEAD ** (-0.5)
        dq_ref[:, s * SLAB : (s + 1) * SLAB] = (z * cosine - turn(z) * sine).astype(bf16)


def put_weights(ring_ref, block_refs, whole_ref, sems, first, columns):
    copies = []
    for k, ref in enumerate(block_refs):
        block = ref.shape[0]
        at = 0 if len(block_refs) == 1 else pl.multiple_of(ring_ref[1 + k] * block, block)
        copy = pltpu.make_async_copy(
            ref.at[:, pl.ds(first, columns)], whole_ref.at[pl.ds(at, block), :], sems.at[k]
        )
        copy.start()
        copies.append(copy)
    return copies


def feed_kernel(ring_ref, own_ref, other_ref, gain_ref, cot_ref, *rest, unit_tile):
    *block_refs, normed_ref, active_ref, grads_ref, part_ref, part_other_ref, wide_ref, sems = rest
    core_ref = ring_ref
    copies = put_weights(ring_ref, block_refs, wide_ref, sems, 0, wide_ref.shape[1])
    rows = own_ref.shape[0]
    units = active_ref.shape[1]
    gain = gain_ref[1:2, :]
    own_at = pl.multiple_of(core_ref[0] * rows, rows)
    other_at = pl.multiple_of((1 - core_ref[0]) * rows, rows)
    for ref, at in ((own_ref, own_at), (other_ref, other_at)):
        x = ref[...]
        scale_rows = lax.rsqrt(jnp.mean(x * x, -1, keepdims=True) + epsilon)
        normed_ref[pl.ds(at, rows), :] = (x * scale_rows * gain).astype(bf16)
    for copy in copies:
        copy.wait()

    @pl.loop(0, units // unit_tile)
    def unit_step(t):
        at = pl.multiple_of(t * unit_tile, unit_tile)
        cols = pl.ds(at, unit_tile)
        up_cols = pl.ds(pl.multiple_of(units + at, unit_tile), unit_tile)
        gate = dot(normed_ref[...], wide_ref[:, cols])
        up = dot(normed_ref[...], wide_ref[:, up_cols])
        grad_active = dot(cot_ref[...], wide_ref[:, pl.ds(pl.multiple_of(2 * units + at, unit_tile), unit_tile)])
        sig = jax.nn.sigmoid(gate)
        silu = gate * sig
        active_ref[:, cols] = (silu * up).astype(bf16)
        grads_ref[:, cols] = (grad_active * up * (sig * (1.0 + gate * (1.0 - sig)))).astype(bf16)
        grads_ref[:, up_cols] = (grad_active * silu).astype(bf16)

    model = normed_ref.shape[1]
    tile = model // 3

    @pl.loop(0, 3)
    def model_step(t):
        at = pl.ds(pl.multiple_of(t * tile, tile), tile)
        wide = wide_ref[at, : 2 * units]
        part_ref[:, at] = dot(grads_ref[pl.ds(own_at, rows), :], wide, 1, 1)
        part_other_ref[:, at] = dot(grads_ref[pl.ds(other_at, rows), :], wide, 1, 1).astype(bf16)


def feed_weights_kernel(n, count, place_ref, normed_ref, active_ref, grads_ref, cot_ref, *outs):
    weight_refs = outs[:count]
    *block_refs, out_ref, out_other_ref, buf, down_ref, sems = outs[count:]
    units = active_ref.shape[1]
    copies = put_weights(place_ref, weight_refs, down_ref, sems, 2 * units, units)
    rows = out_ref.shape[0]
    units = active_ref.shape[1]
    model = normed_ref.shape[1]
    tile = buf.shape[1]
    own_at = pl.multiple_of(place_ref[0] * rows, rows)
    other_at = pl.multiple_of((1 - place_ref[0]) * rows, rows)

    def put(values, at):
        if len(block_refs) == 1:
            block_refs[0][:, at] = values.astype(bf16)
            return
        buf[...] = values.astype(bf16)
        block = model // n
        for k in range(n):
            block_refs[k][:, at] = buf[pl.ds(pl.multiple_of(place_ref[1 + k] * block, block), block), :]

    @pl.loop(0, units // tile)
    def weight_step(t):
        for i in range(3):
            cols = pl.ds(pl.multiple_of(t * tile, tile), tile)
            at = pl.ds(pl.multiple_of(i * units + t * tile, tile), tile)
            if i < 2:
                put(dot(normed_ref[...], grads_ref[:, at], 0, 0), at)
            else:
                put(dot(cot_ref[...], active_ref[:, cols], 0, 0), at)

    wide_tile = model // 3
    for copy in copies:
        copy.wait()

    @pl.loop(0, 3)
    def out_step(t):
        at = pl.ds(pl.multiple_of(t * wide_tile, wide_tile), wide_tile)
        down = down_ref[at, :]
        out_ref[:, at] = dot(active_ref[pl.ds(own_at, rows), :], down, 1, 1)
        out_other_ref[:, at] = dot(active_ref[pl.ds(other_at, rows), :], down, 1, 1).astype(bf16)


def hidden_grad_kernel(
    core_ref, hidden_ref, mine_ref, came_ref, gains_ref, cot_ref, w_ref, grad_ref, attn_ref, mixed_ref, gain_ref
):
    rows = hidden_ref.shape[0]
    hidden = hidden_ref[...]
    grad_normed = mine_ref[...].astype(f32) + came_ref[...].astype(f32)
    scale_rows = lax.rsqrt(jnp.mean(hidden * hidden, -1, keepdims=True) + epsilon)
    unit = hidden * scale_rows
    gain_ref[...] = jnp.sum(grad_normed * unit, 0, keepdims=True)
    grad_unit = grad_normed * gains_ref[1:2, :]
    inner = jnp.mean(grad_unit * unit, -1, keepdims=True)
    cot = cot_ref[pl.ds(pl.multiple_of(core_ref[0] * rows, rows), rows), :].astype(f32)
    grad = cot + scale_rows * (grad_unit - unit * inner)
    grad_ref[...] = grad
    attn_ref[...] = grad.astype(bf16)
    mixed_ref[:, :HALF_Q] = dot(attn_ref[...], w_ref[:, PACK:]).astype(bf16)
    mixed_ref[:, HALF_Q:] = jnp.zeros((rows, HEAD), bf16)


def last_kernel(
    dkv_ref, dq_ref, cos_ref, sin_ref, w_ref, normed_ref, x_ref, grad_attn_ref, mixed_ref, gain_two_ref, *rest
):
    *came_refs, part_ref, dw_ref, lin_ref = rest
    cosine, sine = cos_ref[...], sin_ref[...]
    half = lane_half(cosine.shape)
    for s in range(3):
        cols = slice(s * SLAB, (s + 1) * SLAB)
        z = dkv_ref[:, cols]
        for ref in came_refs:
            z = z + ref[:, cols].astype(f32)
        turned = z * cosine - turn(z) * sine
        lin_ref[:, cols] = (turned if s == 0 else jnp.where(half == 0, turned, z) if s == 1 else z).astype(bf16)
    lin_ref[:, 3 * SLAB :] = dq_ref[...]
    x = x_ref[...].astype(f32)
    scale_rows = lax.rsqrt(jnp.mean(x * x, -1, keepdims=True) + epsilon)
    model = normed_ref.shape[1]
    tile = model // 3
    last = PACK - SLAB

    @pl.loop(0, 3)
    def model_step(t):
        at = pl.ds(pl.multiple_of(t * tile, tile), tile)
        part = dot(lin_ref[...], w_ref[at, :PACK], 1, 1)
        part_ref[:, at] = part.astype(bf16)
        unit = x_ref[:, at].astype(f32) * scale_rows
        gain_one = jnp.sum(part * unit, 0, keepdims=True)
        gain_one = jnp.broadcast_to(gain_one, (SLAB, tile)).T
        gain_two = jnp.broadcast_to(gain_two_ref[:, at], (SLAB, tile)).T
        dw = dot(normed_ref[:, at], lin_ref[...], 0, 0)
        dw_ref[at, :last] = dw[:, :last].astype(bf16)
        lane = lax.broadcasted_iota(jnp.int32, (tile, SLAB), 1)
        gains = jnp.where(lane < HEAD + HEAD // 2, gain_one, gain_two)
        dw_ref[at, last:PACK] = jnp.where(lane < HEAD, dw[:, last:], gains).astype(bf16)
        dw_ref[at, PACK:] = dot(grad_attn_ref[:, at], mixed_ref[:, :HALF_Q], 0, 0).astype(bf16)


def finish_kernel(x_ref, kept_ref, came_ref, query_ref, key_ref, value_ref, out_ref, gain_ref):
    first = x_ref[0] == 0
    kept, came = kept_ref[...].astype(f32), came_ref[...].astype(f32)
    k_end, v_end, q_end = HALF_KV, 2 * HALF_KV, 2 * HALF_KV + HALF_Q
    for half in range(2):
        z = jnp.where(first, kept, came) if half == 0 else jnp.where(first, came, kept)
        key_ref[:, half * HALF_KV : (half + 1) * HALF_KV] = z[:, :k_end]
        value_ref[:, half * HALF_KV : (half + 1) * HALF_KV] = z[:, k_end:v_end]
        query_ref[:, half * HALF_Q : (half + 1) * HALF_Q] = z[:, v_end:q_end]
        out_ref[:, half * HALF_Q : (half + 1) * HALF_Q] = z[:, PACK:]
    gain_ref[...] = kept[:, q_end : q_end + 1] + came[:, q_end : q_end + 1]


def as_dealt(array, pieces):
    rows = array.shape[0]
    rest = array.shape[1:]
    axes = (0, 2, 1, 3) + tuple(4 + i for i in range(len(rest)))
    split = array.reshape((2, 2, pieces // 2, rows // (2 * pieces)) + rest)
    return jnp.transpose(split, axes).reshape((rows,) + rest)


def norm_backward(grad_normed, unit_rows, scale_rows, gain):
    grad_unit = grad_normed * gain
    grad_gain = jnp.sum(grad_normed * unit_rows, 0)
    grad_rows = scale_rows * (
        grad_unit - unit_rows * jnp.mean(grad_unit * unit_rows, -1, keepdims=True)
    )
    return grad_rows, grad_gain


def on_device(n, args):
    (inputs, cotangent, segments, pair_order, gain_attn, w_query, w_key, w_value, w_out, gain_mlp,
     w_gate, w_up, w_down) = args
    local_rows, model = inputs.shape
    pieces = PIECES
    own_rows = local_rows // 2
    run_rows = own_rows // 2
    part_rows = gain_attn.shape[0]
    ctx_rows = gain_mlp.shape[0]
    pair_rows = ctx_rows // 2
    units = w_gate.shape[1]
    blocks = 2 * n
    ctx_index = lax.axis_index("ctx")
    wa_index = lax.axis_index("wa")
    x_index, core_index = wa_index // 2, wa_index % 2

    def both_halves(array, width):
        return array[:, :width], array[:, width:]

    q_halves = both_halves(w_query, HALF_Q)
    k_halves = both_halves(w_key, HALF_KV)
    v_halves = both_halves(w_value, HALF_KV)
    gain_two_part = lax.dynamic_slice_in_dim(gain_mlp, wa_index * part_rows, part_rows)
    gain_cols = jnp.concatenate(
        [jnp.broadcast_to(g[:, None], (part_rows, HEAD // 2)) for g in (gain_attn, gain_two_part)], 1
    )
    out_halves = both_halves(w_out.T, HALF_Q)
    halves = [
        jnp.concatenate([k_halves[i], v_halves[i], q_halves[i], gain_cols, out_halves[i]], 1)
        for i in range(2)
    ]

    half_ring = n // 2

    def gather_rows(halves, wide_block, prepared):
        mine = jnp.where(x_index == 0, halves[0], halves[1])
        theirs = jnp.where(x_index == 0, halves[1], halves[0])
        came, prepared, wide_block = lax.optimization_barrier((x_swap(theirs), prepared, wide_block))
        low = jnp.where(x_index == 0, mine, came)
        high = jnp.where(x_index == 0, came, mine)
        pair = jnp.stack([low, high])
        other = core_swap(pair)
        zero = jnp.where(core_index == 0, pair, other)
        one = jnp.where(core_index == 0, other, pair)
        quad = jnp.stack([zero, one], 1).reshape(ctx_rows, -1)
        sent = lax.dynamic_slice_in_dim(quad, core_index * pair_rows, pair_rows, 0)
        held = ring_gather(sent, n)
        wide = {0: wide_block}
        for step in range(1, half_ring - 2):
            wide = ring_gather_step(wide, step, n)
        held, wide = lax.optimization_barrier((held, wide))
        ordered = jnp.zeros((n,) + sent.shape, bf16)
        for k in range(n):
            ordered = lax.dynamic_update_index_in_dim(ordered, held[k], ring_id(ctx_index, k, n), 0)
        held = ordered
        opposite = core_swap(held)
        whole = jnp.where(
            core_index == 0,
            jnp.concatenate([held, opposite], 1),
            jnp.concatenate([opposite, held], 1),
        )
        return whole.reshape(n * ctx_rows, -1), wide, prepared

    at = jnp.stack([ctx_index, core_index]).astype(jnp.int32)
    table, ring, rows_info, cosine, sine, x_own, run_cotangent = pl.pallas_call(
        functools.partial(prepare_kernel, n),
        out_shape=(
            jax.ShapeDtypeStruct((blocks + 9,), jnp.int32),
            jax.ShapeDtypeStruct((n + 1,), jnp.int32),
            jax.ShapeDtypeStruct((4, GROUP * run_rows), jnp.int32),
            jax.ShapeDtypeStruct((own_rows, SLAB), f32),
            jax.ShapeDtypeStruct((own_rows, SLAB), f32),
            jax.ShapeDtypeStruct((own_rows, model), bf16),
            jax.ShapeDtypeStruct((local_rows, model), bf16),
        ),
        in_specs=[smem()] * 2 + [vmem()] * 3,
        out_specs=(smem(),) * 2 + (vmem(),) * 5,
        compiler_params=params(),
        cost_estimate=cost(6),
    )(at, pair_order, segments.reshape(-1, local_rows // PIECES), inputs, cotangent)

    wide_block = jnp.concatenate([w_gate, w_up, w_down.T], 1)
    prepared = (table, ring, rows_info, cosine, sine, x_own, run_cotangent)
    w_all, wide, prepared = gather_rows(halves, wide_block, prepared)
    table, ring, rows_info, cosine, sine, x_own, run_cotangent = prepared
    w_out_t = w_all[:, PACK:]
    normed, queries, kv_own, gains = pl.pallas_call(
        project_kernel,
        out_shape=(
            jax.ShapeDtypeStruct((own_rows, model), bf16),
            jax.ShapeDtypeStruct((own_rows, Q_WIDE), bf16),
            jax.ShapeDtypeStruct((own_rows, 2 * HALF_KV), bf16),
            jax.ShapeDtypeStruct((2, model), f32),
        ),
        in_specs=[vmem()] * 4,
        out_specs=(vmem(),) * 4,
        compiler_params=params(),
        cost_estimate=cost(5),
    )(x_own, w_all, cosine, sine)

    kv_found = ring_gather(kv_own, n)
    kv_core = jnp.concatenate([kv_found[k] for k in range(n)], 0)
    kv_other = core_swap(kv_core)
    wide, kv_core, kv_other = lax.optimization_barrier((wide, kv_core, kv_other))
    wide = ring_gather_step(wide, half_ring - 2, n)

    mixed, mixed_b, log_total = pl.pallas_call(
        functools.partial(forward_kernel, blocks),
        out_shape=(
            jax.ShapeDtypeStruct((own_rows, Q_WIDE), f32),
            jax.ShapeDtypeStruct((own_rows, Q_WIDE), bf16),
            jax.ShapeDtypeStruct((8, GROUP * run_rows), f32),
        ),
        in_specs=[smem()] + [vmem()] * 4,
        out_specs=(vmem(),) * 3,
        scratch_shapes=[
            pltpu.VMEM((HALF_GROUPS * SLAB, GROUP * run_rows), f32),
            pltpu.VMEM((8 * HALF_GROUPS, GROUP * run_rows), f32),
            pltpu.VMEM((8 * HALF_GROUPS, GROUP * run_rows), f32),
        ],
        compiler_params=params(14 + n // 2),
        cost_estimate=cost(16),
    )(table, queries, kv_core, kv_other, rows_info)

    wide, mixed_b = lax.optimization_barrier((wide, mixed_b))
    wide = ring_gather_step(wide, half_ring - 1, n)
    attn_part = rounded(dot(mixed_b[:, :HALF_Q], w_all[:, PACK:], 1, 1))
    attn_came = x_swap(attn_part)
    wide, attn_came = lax.optimization_barrier((wide, attn_came))
    wide = ring_gather_step(wide, half_ring, n)
    x_f = x_own.astype(f32)
    hidden_own = x_f + (attn_part.astype(f32) + attn_came.astype(f32))
    hidden_other = core_swap(hidden_own)
    wide, hidden_other = lax.optimization_barrier((wide, hidden_other))
    wide = [wide[k] for k in range(n)]
    whole_tiles = ctx_rows % 16 == 0
    if not whole_tiles:
        wide_full = jnp.zeros((n,) + wide_block.shape, bf16)
        for k in range(n):
            wide_full = lax.dynamic_update_index_in_dim(wide_full, wide[k], ring_id(ctx_index, k, n), 0)
        wide = [wide_full.reshape(model, 3 * units)]

    def join(own, other):
        return jnp.where(
            core_index == 0, jnp.concatenate([own, other], 0), jnp.concatenate([other, own], 0)
        )

    normed_two, active, grads_wide, grad_two_own, grad_two_other = pl.pallas_call(
        functools.partial(feed_kernel, unit_tile=min(256, units)),
        out_shape=(
            jax.ShapeDtypeStruct((local_rows, model), bf16),
            jax.ShapeDtypeStruct((local_rows, units), bf16),
            jax.ShapeDtypeStruct((local_rows, 2 * units), bf16),
            jax.ShapeDtypeStruct((own_rows, model), f32),
            jax.ShapeDtypeStruct((own_rows, model), bf16),
        ),
        in_specs=[smem()] + [vmem()] * 4 + [pl.BlockSpec(memory_space=pl.ANY)] * len(wide),
        out_specs=(vmem(),) * 5,
        scratch_shapes=[
            pltpu.VMEM((model, 3 * units), bf16),
            pltpu.SemaphoreType.DMA((len(wide),)),
        ],
        compiler_params=params(),
        cost_estimate=cost(12),
    )(ring, hidden_own, hidden_other, gains, run_cotangent, *wide)
    shapes = (
        (jax.ShapeDtypeStruct((ctx_rows, 3 * units), bf16),) * n
        if whole_tiles
        else (jax.ShapeDtypeStruct((model, 3 * units), bf16),)
    )
    unit_tile = min(256, units)
    *d_terms, mlp_own, mlp_other = pl.pallas_call(
        functools.partial(feed_weights_kernel, n, len(wide)),
        out_shape=shapes
        + (
            jax.ShapeDtypeStruct((own_rows, model), f32),
            jax.ShapeDtypeStruct((own_rows, model), bf16),
        ),
        in_specs=[smem()] + [vmem()] * 4 + [pl.BlockSpec(memory_space=pl.ANY)] * len(wide),
        out_specs=(vmem(),) * (len(shapes) + 2),
        scratch_shapes=[
            pltpu.VMEM((model, unit_tile), bf16),
            pltpu.VMEM((model, units), bf16),
            pltpu.SemaphoreType.DMA((len(wide),)),
        ],
        compiler_params=params(),
        cost_estimate=cost(9),
    )(ring, normed_two, active, grads_wide, run_cotangent, *wide)
    if not whole_tiles:
        d_blocks = d_terms[0].reshape(n, ctx_rows, 3 * units)
        d_terms = [
            lax.dynamic_index_in_dim(d_blocks, ring_id(ctx_index, k, n), 0, keepdims=False) for k in range(n)
        ]
    def chip_sum(own, other):
        return rounded(own + core_swap(other).astype(f32))

    grad_two = chip_sum(grad_two_own, grad_two_other)
    grad_two_came, d_terms, mlp_own = lax.optimization_barrier((x_swap(grad_two), d_terms, mlp_own))
    d_came = None
    for step in range(1, half_ring - 2):
        d_came = ring_scatter_step(d_terms, d_came, step, n)
    output_chip = chip_sum(mlp_own, mlp_other)
    grad_hidden, grad_attn, grad_mixed, grad_gain_two = pl.pallas_call(
        hidden_grad_kernel,
        out_shape=(
            jax.ShapeDtypeStruct((own_rows, model), f32),
            jax.ShapeDtypeStruct((own_rows, model), bf16),
            jax.ShapeDtypeStruct((own_rows, Q_WIDE), bf16),
            jax.ShapeDtypeStruct((1, model), f32),
        ),
        in_specs=[smem()] + [vmem()] * 6,
        out_specs=(vmem(),) * 4,
        compiler_params=params(),
        cost_estimate=cost(5),
    )(ring, hidden_own, grad_two, grad_two_came, gains, run_cotangent, w_all)
    d_came, grad_mixed, output_chip = lax.optimization_barrier((d_came, grad_mixed, output_chip))
    d_came = ring_scatter_step(d_terms, d_came, half_ring - 2, n)

    dq_lin, dkv_core, dkv_other = pl.pallas_call(
        functools.partial(backward_kernel, blocks),
        out_shape=(
            jax.ShapeDtypeStruct((own_rows, Q_WIDE), bf16),
            jax.ShapeDtypeStruct(kv_core.shape, f32),
            jax.ShapeDtypeStruct(kv_core.shape, bf16),
        ),
        in_specs=[smem()] + [vmem()] * 9,
        out_specs=(vmem(),) * 3,
        scratch_shapes=[
            pltpu.VMEM((2 * SLAB, HEADS // 2 * run_rows), f32),
            pltpu.VMEM((own_rows, Q_WIDE), f32),
            pltpu.VMEM(kv_core.shape, f32),
            pltpu.VMEM((HEADS // 2 * run_rows, 2 * SLAB), bf16),
            pltpu.VMEM((HEADS // 2 * run_rows, 2 * SLAB), bf16),
        ],
        compiler_params=params(12 + 2 * n),
        cost_estimate=cost(24),
    )(table, queries, kv_core, kv_other, rows_info, mixed, log_total, grad_mixed, cosine, sine)

    def scatter_rows(part, crossing):
        cols = part.shape[1]
        split = part.reshape(n, 2, pair_rows, cols)
        mine = lax.dynamic_index_in_dim(split, core_index, 1, keepdims=False)
        theirs = lax.dynamic_index_in_dim(split, 1 - core_index, 1, keepdims=False)
        chip = mine.astype(f32) + core_swap(theirs).astype(f32)
        terms = [lax.dynamic_index_in_dim(chip, ring_id(ctx_index, k, n), 0, keepdims=False) for k in range(n)]
        came, (crossed,) = ring_scatter(terms, n, {2: x_swap(crossing)})
        total = terms[0] + came[0].astype(f32) + came[1].astype(f32)
        total_b = total.astype(bf16)
        opposite = core_swap(total_b)
        rows = jnp.where(
            core_index == 0,
            jnp.concatenate([total_b, opposite], 0),
            jnp.concatenate([opposite, total_b], 0),
        )
        quad = rows.reshape(2, 2, part_rows, cols)
        kept = lax.dynamic_index_in_dim(
            lax.dynamic_index_in_dim(quad, x_index, 0, keepdims=False), core_index, 0, keepdims=False
        )
        sent = lax.dynamic_index_in_dim(
            lax.dynamic_index_in_dim(quad, 1 - x_index, 0, keepdims=False), core_index, 0, keepdims=False
        )
        came = x_swap(sent)
        return rows, kept, came, crossed

    dkv_other, d_came, output_came = lax.optimization_barrier((dkv_other, d_came, x_swap(output_chip)))
    d_step = ring_scatter_step(d_terms, d_came, half_ring - 1, n)
    dkv = dkv_core + core_swap(dkv_other).astype(f32)
    dkv = dkv.reshape(n, own_rows, 2 * HALF_KV)
    dkv_own, (dkv_came, (d_came,)) = dkv[0], ring_scatter(dkv, n, {half_ring - 1: d_step})
    d_came = ring_scatter_step(d_terms, d_came, half_ring, n)
    output_own = (hidden_own + (output_chip.astype(f32) + output_came.astype(f32))).astype(bf16)
    output = as_dealt(join(output_own, core_swap(output_own)), pieces)
    normed_part, d_in = pl.pallas_call(
        last_kernel,
        out_shape=(
            jax.ShapeDtypeStruct((own_rows, model), bf16),
            jax.ShapeDtypeStruct((model, PACK + HALF_Q), bf16),
        ),
        in_specs=[vmem()] * (10 + len(dkv_came)),
        out_specs=(vmem(),) * 2,
        scratch_shapes=[pltpu.VMEM((own_rows, PACK), bf16)],
        compiler_params=params(56),
        cost_estimate=cost(5),
    )(dkv_own, dq_lin, cosine, sine, w_all, normed, x_own, grad_attn, mixed_b, grad_gain_two, *dkv_came)
    d_in, d_came = lax.optimization_barrier((d_in, d_came))
    in_rows, kept, came, normed_came = scatter_rows(d_in, normed_part)
    d_mlp = d_terms[0].astype(f32) + d_came[0].astype(f32) + d_came[1].astype(f32)
    grad_w_gate = d_mlp[:, :units]
    grad_w_up = d_mlp[:, units : 2 * units]
    grad_w_down = d_mlp[:, 2 * units :].T

    grad_w_query, grad_w_key, grad_w_value, grad_w_out, grad_gain = pl.pallas_call(
        finish_kernel,
        out_shape=(
            jax.ShapeDtypeStruct((part_rows, 2 * HALF_Q), f32),
            jax.ShapeDtypeStruct((part_rows, 2 * HALF_KV), f32),
            jax.ShapeDtypeStruct((part_rows, 2 * HALF_KV), f32),
            jax.ShapeDtypeStruct((part_rows, 2 * HALF_Q), f32),
            jax.ShapeDtypeStruct((part_rows, 1), f32),
        ),
        in_specs=[smem(), vmem(), vmem()],
        out_specs=(vmem(),) * 5,
        compiler_params=params(),
        cost_estimate=cost(2),
    )(x_index.reshape(1).astype(jnp.int32), kept, came)
    grad_w_out = grad_w_out.T
    grad_gain_attn = grad_gain[:, 0]

    grad_normed = normed_part.astype(f32) + normed_came.astype(f32)
    scale_one = lax.rsqrt(jnp.mean(x_f * x_f, -1, keepdims=True) + epsilon)
    input_rows, unused_gain = norm_backward(grad_normed, x_f * scale_one, scale_one, gains[:1])
    grad_inputs_own = (grad_hidden + input_rows).astype(bf16)
    grad_inputs = as_dealt(join(grad_inputs_own, core_swap(grad_inputs_own)), pieces)
    grad_gain_mlp = in_rows[:, PACK - 1].astype(f32)
    return (
        output,
        grad_inputs,
        grad_gain_attn,
        grad_w_query,
        grad_w_key,
        grad_w_value,
        grad_w_out,
        grad_gain_mlp,
        grad_w_gate,
        grad_w_up,
        grad_w_down,
    )


def solution(mesh):
    n = mesh.shape["ctx"]

    def body(*args):
        return on_device(n, args)

    return jax.shard_map(
        body,
        mesh=mesh,
        in_specs=(
            P("ctx", None),
            P("ctx", None),
            P(),
            P(),
            P(("ctx", "wa")),
            P(("ctx", "wa"), None),
            P(("ctx", "wa"), None),
            P(("ctx", "wa"), None),
            P(None, ("ctx", "wa")),
            P("ctx"),
            P("ctx", "wa"),
            P("ctx", "wa"),
            P("wa", "ctx"),
        ),
        out_specs=(
            P("ctx", None),
            P("ctx", None),
            P(("ctx", "wa")),
            P(("ctx", "wa"), None),
            P(("ctx", "wa"), None),
            P(("ctx", "wa"), None),
            P(None, ("ctx", "wa")),
            P("ctx"),
            P("ctx", "wa"),
            P("ctx", "wa"),
            P("wa", "ctx"),
        ),
        check_vma=False,
    )
```

```python
import functools
import math

import jax
import jax.numpy as jnp
from jax import lax
from jax.experimental import pallas as pl
from jax.experimental.pallas import tpu as pltpu
from jax.sharding import PartitionSpec as P

HEADS = 18
KV_HEADS = 6
HEAD = 64
GROUP = HEADS // KV_HEADS
HALF_Q = HEADS * HEAD // 2
HALF_KV = KV_HEADS * HEAD // 2
HALF_GROUPS = KV_HEADS // 2
SLAB = 128
PACK = 2 * HALF_KV + HALF_Q + HEAD
Q_WIDE = HALF_Q + HEAD

epsilon = 1e-05
rope_base = 10000.0
masked_score = -1e30
DOCS = 16
PIECES = 4
f32 = jnp.float32
bf16 = jnp.bfloat16
MIB = 1024 * 1024

K_PLACE = [divmod(g, 2) for g in range(HALF_GROUPS)]
V_PLACE = [divmod(HALF_GROUPS + g, 2) for g in range(HALF_GROUPS)]


def vmem():
    return pl.BlockSpec(memory_space=pltpu.VMEM)


def smem():
    return pl.BlockSpec(memory_space=pltpu.SMEM)


def params(mib=26):
    return pltpu.CompilerParams(vmem_limit_bytes=min(mib, 58) * MIB)


def cost(micros):
    return pl.CostEstimate(flops=int(micros * 1e9), bytes_accessed=0, transcendentals=0)


def dot(a, b, ca=1, cb=0):
    return lax.dot_general(a, b, (((ca,), (cb,)), ((), ())), preferred_element_type=f32)


def ctx_parts(n):
    slow = min(4, n)
    return slow, n // slow


def ctx_swap(block, n, k):
    return lax.ppermute(block, "ctx", [(i, i ^ k) for i in range(n)])


def wa_swap(block, k):
    return lax.ppermute(block, "wa", [(i, i ^ k) for i in range(4)])


def core_swap(block):
    return wa_swap(block, 1)


def x_swap(block):
    return wa_swap(block, 2)


def ring_order(n):
    slow, fast = ctx_parts(n)
    order = []
    for r in range(fast):
        line = [z * fast + r for z in range(slow)]
        order += line if r % 2 == 0 else line[::-1]
    return order


def ring_id(ctx, offset, n):
    slow, fast = ctx_parts(n)

    def along(r, z):
        return jnp.where(r % 2 == 0, z, slow - 1 - z)

    place = (ctx % fast) * slow + along(ctx % fast, ctx // fast)
    place = (place + offset) % n
    r = place // slow
    return along(r, place % slow) * fast + r


def ring_send(forward, backward, n):
    order = ring_order(n)
    pairs = [(order[p], order[(p + 1) % n]) for p in range(n)]
    return (
        lax.ppermute(forward, "ctx", pairs),
        lax.ppermute(backward, "ctx", [(b, a) for a, b in pairs]),
    )


def ring_gather_step(found, step, n):
    half_ring = n // 2
    f, b = found[(1 - step) % n], found[step - 1]
    if step == half_ring:
        half = f.shape[0] // 2
        parts = ring_send(f[:half], b[half:], n)
        return found | {half_ring: jnp.concatenate(parts, 0)}
    f, b = ring_send(f, b, n)
    return found | {n - step: f, step: b}


def ring_scatter_step(terms, came, step, n):
    half_ring = n // 2
    far = terms[half_ring]
    half = far.shape[0] // 2
    if step == 1:
        return ring_send(far[:half].astype(bf16), far[half:].astype(bf16), n)
    d = half_ring - step + 1
    f, b = terms[d].astype(f32), terms[n - d].astype(f32)
    came_f, came_b = came[0].astype(f32), came[1].astype(f32)
    if step == 2:
        rest = jnp.zeros_like(far[half:], f32)
        came_f = jnp.concatenate([came_f, rest], 0)
        came_b = jnp.concatenate([jnp.zeros_like(far[:half], f32), came_b], 0)
    return ring_send((f + came_f).astype(bf16), (b + came_b).astype(bf16), n)


def ring_gather(block, n):
    found = {0: block}
    for step in range(1, n // 2 + 1):
        found = ring_gather_step(found, step, n)
    return found


def ring_scatter(terms, n, beside=None):
    came = None
    beside = dict(beside or {})
    for step in range(1, n // 2 + 1):
        came = ring_scatter_step(terms, came, step, n)
        if step in beside:
            came, beside[step] = lax.optimization_barrier((came, beside[step]))
    return came, list(beside.values())


def rounded(array):
    return lax.optimization_barrier(array.astype(bf16))


def lane_half(shape):
    lane = lax.broadcasted_iota(jnp.int32, shape, 1)
    return lane // HEAD


def turn(z):
    lane = lax.broadcasted_iota(jnp.int32, z.shape, 1)
    return jnp.where(
        lane % HEAD < HEAD // 2,
        pltpu.roll(z, SLAB - HEAD // 2, 1),
        pltpu.roll(z, HEAD // 2, 1),
    )


def prepare_kernel(
    n, at_ref, pairs_ref, segments_ref, x_ref, cot_ref, table_ref, ring_ref, rows_ref, cos_ref, sin_ref, own_ref, cots_ref
):
    ctx, core = at_ref[0], at_ref[1]
    own_rows = own_ref.shape[0]
    run_rows = own_rows // 2
    piece = run_rows // 2
    blocks = 2 * n
    lower = pairs_ref[ctx]
    for c in range(2):
        for run in range(2):
            for p in range(2):
                to = c * own_rows + run * run_rows + p * piece
                source = (2 * c + p) * 2 * piece + run * piece
                cots_ref[to : to + piece, :] = cot_ref[source : source + piece, :]
    for run in range(2):
        for p in range(2):
            to = run * run_rows + p * piece
            source = pl.multiple_of((2 * core + p) * 2 * piece + run * piece, piece)
            own_ref[to : to + piece, :] = x_ref[pl.ds(source, piece), :]
    ring_ref[0] = core
    for k in range(n):
        ring_ref[1 + k] = ring_id(ctx, k, n)
    for k in range(n):
        low = pairs_ref[ring_ref[1 + k]]
        table_ref[low] = 2 * k
        table_ref[blocks - 1 - low] = 2 * k + 1
    counts = []
    every = segments_ref[...]
    for d in range(DOCS):
        here = (every == d + 1).astype(f32)
        counts.append(jnp.sum(here, 0, keepdims=True))
    count = jnp.sum(jnp.concatenate(counts, 0), 1, keepdims=True)
    docs = lax.broadcasted_iota(jnp.int32, (DOCS, run_rows), 0) + 1
    lane = lax.broadcasted_iota(jnp.int32, (1, run_rows), 1)
    first_piece = segments_ref[pl.ds(ctx * PIECES + 2 * core, 1), :]
    second_piece = segments_ref[pl.ds(ctx * PIECES + 2 * core + 1, 1), :]
    runs = (
        jnp.where(lane < piece, first_piece, pltpu.roll(second_piece, piece, 1)),
        jnp.where(lane < piece, pltpu.roll(first_piece, piece, 1), second_piece),
    )
    table_ref[blocks] = core
    for run in range(2):
        block = lower if run == 0 else blocks - 1 - lower
        position = block * (2 * run_rows) + core * run_rows + lane
        earlier = jnp.where(docs < runs[run], count, 0.0)
        start = jnp.sum(earlier, 0, keepdims=True)
        start = jnp.where(runs[run] > 0, start, position.astype(f32))
        first = jnp.min(start).astype(jnp.int32) // (2 * run_rows)
        latest = (jnp.max(start).astype(jnp.int32) + 2 * run_rows - 1) // (2 * run_rows)
        whole_from = jnp.minimum(jnp.maximum(latest, first), block + 1)
        whole_to = jnp.maximum(block, whole_from)
        for i, value in enumerate((first, whole_from, whole_to, block + 1)):
            table_ref[blocks + 1 + 4 * run + i] = value
        start = start.astype(jnp.int32)
        rows_ref[2 * run : 2 * run + 1, :] = jnp.concatenate([start] * GROUP, 1)
        rows_ref[2 * run + 1 : 2 * run + 2, :] = jnp.concatenate([position] * GROUP, 1)
    lanes = lax.broadcasted_iota(jnp.int32, (run_rows, SLAB), 1)
    row = lax.broadcasted_iota(jnp.int32, (run_rows, SLAB), 0)
    frequency = jnp.exp(-math.log(rope_base) * 2.0 * (lanes % (HEAD // 2)).astype(f32) / HEAD)
    for run in range(2):
        block = lower if run == 0 else blocks - 1 - lower
        angle = (block * (2 * run_rows) + core * run_rows + row).astype(f32) * frequency
        at = slice(run * run_rows, (run + 1) * run_rows)
        cos_ref[at, :] = jnp.cos(angle)
        sine = jnp.sin(angle)
        sin_ref[at, :] = jnp.where(lanes % HEAD < HEAD // 2, -sine, sine)


def project_kernel(x_ref, w_ref, cos_ref, sin_ref, normed_ref, q_ref, kv_ref, gains_ref):
    tail = w_ref[:, PACK - SLAB : PACK].astype(f32).T
    gains_ref[0:1, :] = tail[SLAB - HEAD : SLAB - HEAD + 1, :]
    gains_ref[1:2, :] = tail[SLAB - 1 :, :]
    gain_ref = gains_ref.at[0:1, :]
    x = x_ref[...].astype(f32)
    scale_rows = lax.rsqrt(jnp.mean(x * x, -1, keepdims=True) + epsilon)
    normed = (x * scale_rows * gain_ref[...]).astype(bf16)
    normed_ref[...] = normed
    cosine, sine = cos_ref[...], sin_ref[...]
    half = lane_half(cosine.shape)
    for s in range(PACK // SLAB):
        z = dot(normed, w_ref[:, s * SLAB : (s + 1) * SLAB])
        if s == 2:
            kv_ref[:, 2 * SLAB : 3 * SLAB] = z.astype(bf16)
            continue
        turned = z * cosine + turn(z) * sine
        if s == 0:
            kv_ref[:, :SLAB] = turned.astype(bf16)
        elif s == 1:
            kv_ref[:, SLAB : 2 * SLAB] = jnp.where(half == 0, turned, z).astype(bf16)
        else:
            scaled = turned * HEAD ** (-0.5)
            if s == PACK // SLAB - 1:
                scaled = jnp.where(half == 0, scaled, 0.0)
            q_ref[:, (s - 3) * SLAB : (s - 2) * SLAB] = scaled.astype(bf16)


def head_rows(ref, run, rows, g, place):
    parts = []
    for j in range(GROUP):
        slab, half = divmod(GROUP * g + j, 2)
        z = ref[run * rows : (run + 1) * rows, slab * SLAB : (slab + 1) * SLAB].astype(f32)
        if half != place:
            z = pltpu.roll(z, HEAD, 1)
        parts.append(jnp.where(lane_half(z.shape) == place, z, 0.0).astype(bf16))
    return jnp.concatenate(parts, 0)


def put_heads(ref, values, run, rows, g, place):
    flat = values.T
    for j in range(GROUP):
        slab, half = divmod(GROUP * g + j, 2)
        z = flat[j * rows : (j + 1) * rows, :]
        if half != place:
            z = pltpu.roll(z, HEAD, 1)
        where = (slice(run * rows, (run + 1) * rows), slice(slab * SLAB, (slab + 1) * SLAB))
        if half == 0:
            ref[where] = jnp.where(lane_half(z.shape) == 0, z, 0.0)
        else:
            ref[where] = jnp.where(lane_half(z.shape) == 1, z, ref[where])


def key_block(own_ref, other_ref, slot, rows, slab):
    at = pl.ds(pl.multiple_of(slot * rows, rows), rows)
    cols = slice(slab * SLAB, (slab + 1) * SLAB)
    return jnp.concatenate([own_ref[at, cols], other_ref[at, cols]], 0)


def key_places(block, core, rows, width):
    i = lax.broadcasted_iota(jnp.int32, (2 * rows, width), 0)
    mine = i + core * rows
    others = i - core * rows
    return block * (2 * rows) + jnp.where(i < rows, mine, others)


def forward_kernel(
    blocks, table, q_ref, own_ref, other_ref, rows_ref, mixed_ref, mixed_b_ref, log_ref, acc_ref, sum_ref, max_ref
):
    rows = q_ref.shape[0] // 2
    width = GROUP * rows
    core = table[blocks]
    for run in range(2):
        first, mid0, mid1, last = [table[blocks + 1 + 4 * run + i] for i in range(4)]
        start = rows_ref[2 * run : 2 * run + 1, :]
        stop = rows_ref[2 * run + 1 : 2 * run + 2, :]
        queries = [head_rows(q_ref, run, rows, g, K_PLACE[g][1]) for g in range(HALF_GROUPS)]
        acc_ref[...] = jnp.zeros_like(acc_ref)
        sum_ref[...] = jnp.zeros_like(sum_ref)
        max_ref[...] = jnp.full_like(max_ref, masked_score)

        def step(b, carry, masked):
            at_rows = pl.ds(pl.multiple_of(table[b] * rows, rows), rows)
            if masked:
                at = key_places(b, core, rows, width)
                ok = (at >= start) & (at <= stop)
            scores = []
            for g in range(HALF_GROUPS):
                cols = slice(K_PLACE[g][0] * SLAB, (K_PLACE[g][0] + 1) * SLAB)
                keys = jnp.concatenate([own_ref[at_rows, cols], other_ref[at_rows, cols]], 0)
                s = dot(keys, queries[g], 1, 1)
                if masked:
                    s = jnp.where(ok, s, masked_score)
                scores.append(s)
            for g in range(HALF_GROUPS):
                s = scores[g]
                cols = slice(V_PLACE[g][0] * SLAB, (V_PLACE[g][0] + 1) * SLAB)
                values = jnp.concatenate([own_ref[at_rows, cols], other_ref[at_rows, cols]], 0)
                before = max_ref[8 * g : 8 * g + 1, :]
                high = jnp.maximum(before, jnp.max(s, 0, keepdims=True))
                keep = jnp.exp(before - high)
                p = jnp.exp(s - high)
                max_ref[8 * g : 8 * g + 1, :] = high
                sum_ref[8 * g : 8 * g + 1, :] = sum_ref[8 * g : 8 * g + 1, :] * keep + jnp.sum(p, 0, keepdims=True)
                rows_g = slice(g * SLAB, (g + 1) * SLAB)
                acc_ref[rows_g, :] = acc_ref[rows_g, :] * keep + dot(values, p.astype(bf16), 0, 0)
            return carry

        lax.fori_loop(first, mid0, functools.partial(step, masked=True), 0)
        lax.fori_loop(mid0, mid1, functools.partial(step, masked=False), 0)
        lax.fori_loop(mid1, last, functools.partial(step, masked=True), 0)
        for g in range(HALF_GROUPS):
            total = sum_ref[8 * g : 8 * g + 1, :]
            log_ref[run * HALF_GROUPS + g : run * HALF_GROUPS + g + 1, :] = max_ref[8 * g : 8 * g + 1, :] + jnp.log(total)
            put_heads(mixed_ref, acc_ref[g * SLAB : (g + 1) * SLAB, :] * (1.0 / total), run, rows, g, V_PLACE[g][1])
    mixed_b_ref[...] = mixed_ref[...].astype(bf16)


def wide_rows(ref, run, rows, places, base):
    parts = []
    for g in range(HALF_GROUPS):
        slab, half = places[g]
        z = head_rows(ref, run, rows, g, half)
        zero = jnp.zeros_like(z)
        parts.append(jnp.concatenate([z, zero] if slab == base else [zero, z], 1))
    return jnp.concatenate(parts, 0)


def backward_kernel(blocks,
    table, q_ref, own_ref, other_ref, rows_ref, mixed_ref, log_ref, grad_ref, cos_ref, sin_ref,
    dq_ref, down_ref, dother_out, dq_buf, raw_buf, dother_ref, q_buf, g_buf):
    rows = q_ref.shape[0] // 2
    width = GROUP * rows
    core = table[blocks]
    down_ref[...] = jnp.zeros_like(down_ref)
    dother_ref[...] = jnp.zeros_like(dother_ref)
    for run in range(2):
        first, mid0, mid1, last = [table[blocks + 1 + 4 * run + i] for i in range(4)]
        start = rows_ref[2 * run : 2 * run + 1, :]
        stop = rows_ref[2 * run + 1 : 2 * run + 2, :]
        q_buf[...] = wide_rows(q_ref, run, rows, K_PLACE, 0)
        g_buf[...] = wide_rows(grad_ref, run, rows, V_PLACE, 1)
        logs, deltas = [], []
        for g in range(HALF_GROUPS):
            logs.append(log_ref[run * HALF_GROUPS + g : run * HALF_GROUPS + g + 1, :])
            parts = []
            for j in range(GROUP):
                slab, half = divmod(GROUP * g + j, 2)
                where = (slice(run * rows, (run + 1) * rows), slice(slab * SLAB, (slab + 1) * SLAB))
                z = grad_ref[where].astype(f32) * mixed_ref[where]
                z = jnp.where(lane_half(z.shape) == half, z, 0.0)
                parts.append(jnp.sum(z.T, 0, keepdims=True))
            deltas.append(jnp.concatenate(parts, 1))
        log_all = jnp.concatenate(logs, 1)
        delta_all = jnp.concatenate(deltas, 1)
        dq_buf[...] = jnp.zeros_like(dq_buf)

        def step(b, carry, masked):
            at_rows = pl.ds(pl.multiple_of(table[b] * rows, rows), rows)
            keys = jnp.concatenate([own_ref[at_rows, : 2 * SLAB], other_ref[at_rows, : 2 * SLAB]], 0)
            vals = jnp.concatenate([own_ref[at_rows, SLAB:], other_ref[at_rows, SLAB:]], 0)
            if masked:
                at = key_places(b, core, rows, width)
                ok = (at >= start) & (at <= stop)
            ps, dss = [], []
            for g in range(HALF_GROUPS):
                rg = slice(g * width, (g + 1) * width)
                s = dot(keys, q_buf[rg, :], 1, 1)
                p = jnp.exp(s - log_all[:, rg])
                if masked:
                    p = jnp.where(ok, p, 0.0)
                dp = dot(vals, g_buf[rg, :], 1, 1)
                ps.append(p.astype(bf16))
                dss.append((p * (dp - delta_all[:, rg])).astype(bf16))
            ds = jnp.concatenate(dss, 1)
            p = jnp.concatenate(ps, 1)
            dq_buf[...] += dot(keys, ds, 0, 0)
            dk = dot(ds, q_buf[...])
            dv = dot(p, g_buf[...])
            for i, val in ((0, dk[:, :SLAB]), (1, dk[:, SLAB:] + dv[:, :SLAB]), (2, dv[:, SLAB:])):
                cols = slice(i * SLAB, (i + 1) * SLAB)
                down_ref[at_rows, cols] += val[:rows]
                dother_ref[at_rows, cols] += val[rows:]
            return carry

        lax.fori_loop(first, mid0, functools.partial(step, masked=True), 0)
        lax.fori_loop(mid0, mid1, functools.partial(step, masked=False), 0)
        lax.fori_loop(mid1, last, functools.partial(step, masked=True), 0)
        for g in range(HALF_GROUPS):
            slab, half = K_PLACE[g]
            put_heads(raw_buf, dq_buf[slab * SLAB : (slab + 1) * SLAB, g * width : (g + 1) * width], run, rows, g, half)
    dother_out[...] = dother_ref[...].astype(bf16)
    cosine, sine = cos_ref[...], sin_ref[...]
    for s in range(Q_WIDE // SLAB):
        z = raw_buf[:, s * SLAB : (s + 1) * SLAB] * HEAD ** (-0.5)
        dq_ref[:, s * SLAB : (s + 1) * SLAB] = (z * cosine - turn(z) * sine).astype(bf16)


def put_weights(ring_ref, block_refs, whole_ref, sems, first, columns):
    copies = []
    for k, ref in enumerate(block_refs):
        block = ref.shape[0]
        at = 0 if len(block_refs) == 1 else pl.multiple_of(ring_ref[1 + k] * block, block)
        copy = pltpu.make_async_copy(
            ref.at[:, pl.ds(first, columns)], whole_ref.at[pl.ds(at, block), :], sems.at[k]
        )
        copy.start()
        copies.append(copy)
    return copies


def feed_kernel(ring_ref, own_ref, other_ref, gain_ref, cot_ref, *rest, unit_tile):
    *block_refs, normed_ref, active_ref, grads_ref, part_ref, part_other_ref, wide_ref, sems = rest
    core_ref = ring_ref
    copies = put_weights(ring_ref, block_refs, wide_ref, sems, 0, wide_ref.shape[1])
    rows = own_ref.shape[0]
    units = active_ref.shape[1]
    gain = gain_ref[1:2, :]
    own_at = pl.multiple_of(core_ref[0] * rows, rows)
    other_at = pl.multiple_of((1 - core_ref[0]) * rows, rows)
    for ref, at in ((own_ref, own_at), (other_ref, other_at)):
        x = ref[...]
        scale_rows = lax.rsqrt(jnp.mean(x * x, -1, keepdims=True) + epsilon)
        normed_ref[pl.ds(at, rows), :] = (x * scale_rows * gain).astype(bf16)
    for copy in copies:
        copy.wait()

    @pl.loop(0, units // unit_tile)
    def unit_step(t):
        at = pl.multiple_of(t * unit_tile, unit_tile)
        cols = pl.ds(at, unit_tile)
        up_cols = pl.ds(pl.multiple_of(units + at, unit_tile), unit_tile)
        gate = dot(normed_ref[...], wide_ref[:, cols])
        up = dot(normed_ref[...], wide_ref[:, up_cols])
        grad_active = dot(cot_ref[...], wide_ref[:, pl.ds(pl.multiple_of(2 * units + at, unit_tile), unit_tile)])
        sig = jax.nn.sigmoid(gate)
        silu = gate * sig
        active_ref[:, cols] = (silu * up).astype(bf16)
        grads_ref[:, cols] = (grad_active * up * (sig * (1.0 + gate * (1.0 - sig)))).astype(bf16)
        grads_ref[:, up_cols] = (grad_active * silu).astype(bf16)

    model = normed_ref.shape[1]
    tile = model // 3

    @pl.loop(0, 3)
    def model_step(t):
        at = pl.ds(pl.multiple_of(t * tile, tile), tile)
        wide = wide_ref[at, : 2 * units]
        part_ref[:, at] = dot(grads_ref[pl.ds(own_at, rows), :], wide, 1, 1)
        part_other_ref[:, at] = dot(grads_ref[pl.ds(other_at, rows), :], wide, 1, 1).astype(bf16)


def feed_weights_kernel(n, count, place_ref, normed_ref, active_ref, grads_ref, cot_ref, *outs):
    weight_refs = outs[:count]
    *block_refs, out_ref, out_other_ref, buf, down_ref, sems = outs[count:]
    units = active_ref.shape[1]
    copies = put_weights(place_ref, weight_refs, down_ref, sems, 2 * units, units)
    rows = out_ref.shape[0]
    units = active_ref.shape[1]
    model = normed_ref.shape[1]
    tile = buf.shape[1]
    own_at = pl.multiple_of(place_ref[0] * rows, rows)
    other_at = pl.multiple_of((1 - place_ref[0]) * rows, rows)

    def put(values, at):
        if len(block_refs) == 1:
            block_refs[0][:, at] = values.astype(bf16)
            return
        buf[...] = values.astype(bf16)
        block = model // n
        for k in range(n):
            block_refs[k][:, at] = buf[pl.ds(pl.multiple_of(place_ref[1 + k] * block, block), block), :]

    @pl.loop(0, units // tile)
    def weight_step(t):
        for i in range(3):
            cols = pl.ds(pl.multiple_of(t * tile, tile), tile)
            at = pl.ds(pl.multiple_of(i * units + t * tile, tile), tile)
            if i < 2:
                put(dot(normed_ref[...], grads_ref[:, at], 0, 0), at)
            else:
                put(dot(cot_ref[...], active_ref[:, cols], 0, 0), at)

    wide_tile = model // 3
    for copy in copies:
        copy.wait()

    @pl.loop(0, 3)
    def out_step(t):
        at = pl.ds(pl.multiple_of(t * wide_tile, wide_tile), wide_tile)
        down = down_ref[at, :]
        out_ref[:, at] = dot(active_ref[pl.ds(own_at, rows), :], down, 1, 1)
        out_other_ref[:, at] = dot(active_ref[pl.ds(other_at, rows), :], down, 1, 1).astype(bf16)


def hidden_grad_kernel(
    core_ref, hidden_ref, mine_ref, came_ref, gains_ref, cot_ref, w_ref, grad_ref, attn_ref, mixed_ref, gain_ref
):
    rows = hidden_ref.shape[0]
    hidden = hidden_ref[...]
    grad_normed = mine_ref[...].astype(f32) + came_ref[...].astype(f32)
    scale_rows = lax.rsqrt(jnp.mean(hidden * hidden, -1, keepdims=True) + epsilon)
    unit = hidden * scale_rows
    gain_ref[...] = jnp.sum(grad_normed * unit, 0, keepdims=True)
    grad_unit = grad_normed * gains_ref[1:2, :]
    inner = jnp.mean(grad_unit * unit, -1, keepdims=True)
    cot = cot_ref[pl.ds(pl.multiple_of(core_ref[0] * rows, rows), rows), :].astype(f32)
    grad = cot + scale_rows * (grad_unit - unit * inner)
    grad_ref[...] = grad
    attn_ref[...] = grad.astype(bf16)
    mixed_ref[:, :HALF_Q] = dot(attn_ref[...], w_ref[:, PACK:]).astype(bf16)
    mixed_ref[:, HALF_Q:] = jnp.zeros((rows, HEAD), bf16)


def last_kernel(
    dkv_ref, dq_ref, cos_ref, sin_ref, w_ref, normed_ref, x_ref, grad_attn_ref, mixed_ref, gain_two_ref, *rest
):
    *came_refs, part_ref, dw_ref, lin_ref = rest
    cosine, sine = cos_ref[...], sin_ref[...]
    half = lane_half(cosine.shape)
    for s in range(3):
        cols = slice(s * SLAB, (s + 1) * SLAB)
        z = dkv_ref[:, cols]
        for ref in came_refs:
            z = z + ref[:, cols].astype(f32)
        turned = z * cosine - turn(z) * sine
        lin_ref[:, cols] = (turned if s == 0 else jnp.where(half == 0, turned, z) if s == 1 else z).astype(bf16)
    lin_ref[:, 3 * SLAB :] = dq_ref[...]
    x = x_ref[...].astype(f32)
    scale_rows = lax.rsqrt(jnp.mean(x * x, -1, keepdims=True) + epsilon)
    model = normed_ref.shape[1]
    tile = model // 3
    last = PACK - SLAB

    @pl.loop(0, 3)
    def model_step(t):
        at = pl.ds(pl.multiple_of(t * tile, tile), tile)
        part = dot(lin_ref[...], w_ref[at, :PACK], 1, 1)
        part_ref[:, at] = part.astype(bf16)
        unit = x_ref[:, at].astype(f32) * scale_rows
        gain_one = jnp.sum(part * unit, 0, keepdims=True)
        gain_one = jnp.broadcast_to(gain_one, (SLAB, tile)).T
        gain_two = jnp.broadcast_to(gain_two_ref[:, at], (SLAB, tile)).T
        dw = dot(normed_ref[:, at], lin_ref[...], 0, 0)
        dw_ref[at, :last] = dw[:, :last].astype(bf16)
        lane = lax.broadcasted_iota(jnp.int32, (tile, SLAB), 1)
        gains = jnp.where(lane < HEAD + HEAD // 2, gain_one, gain_two)
        dw_ref[at, last:PACK] = jnp.where(lane < HEAD, dw[:, last:], gains).astype(bf16)
        dw_ref[at, PACK:] = dot(grad_attn_ref[:, at], mixed_ref[:, :HALF_Q], 0, 0).astype(bf16)


def finish_kernel(x_ref, kept_ref, came_ref, query_ref, key_ref, value_ref, out_ref, gain_ref):
    first = x_ref[0] == 0
    kept, came = kept_ref[...].astype(f32), came_ref[...].astype(f32)
    k_end, v_end, q_end = HALF_KV, 2 * HALF_KV, 2 * HALF_KV + HALF_Q
    for half in range(2):
        z = jnp.where(first, kept, came) if half == 0 else jnp.where(first, came, kept)
        key_ref[:, half * HALF_KV : (half + 1) * HALF_KV] = z[:, :k_end]
        value_ref[:, half * HALF_KV : (half + 1) * HALF_KV] = z[:, k_end:v_end]
        query_ref[:, half * HALF_Q : (half + 1) * HALF_Q] = z[:, v_end:q_end]
        out_ref[:, half * HALF_Q : (half + 1) * HALF_Q] = z[:, PACK:]
    gain_ref[...] = kept[:, q_end : q_end + 1] + came[:, q_end : q_end + 1]


def as_dealt(array, pieces):
    rows = array.shape[0]
    rest = array.shape[1:]
    axes = (0, 2, 1, 3) + tuple(4 + i for i in range(len(rest)))
    split = array.reshape((2, 2, pieces // 2, rows // (2 * pieces)) + rest)
    return jnp.transpose(split, axes).reshape((rows,) + rest)


def norm_backward(grad_normed, unit_rows, scale_rows, gain):
    grad_unit = grad_normed * gain
    grad_gain = jnp.sum(grad_normed * unit_rows, 0)
    grad_rows = scale_rows * (
        grad_unit - unit_rows * jnp.mean(grad_unit * unit_rows, -1, keepdims=True)
    )
    return grad_rows, grad_gain


def on_device(n, args):
    (inputs, cotangent, segments, pair_order, gain_attn, w_query, w_key, w_value, w_out, gain_mlp,
     w_gate, w_up, w_down) = args
    local_rows, model = inputs.shape
    pieces = PIECES
    own_rows = local_rows // 2
    run_rows = own_rows // 2
    part_rows = gain_attn.shape[0]
    ctx_rows = gain_mlp.shape[0]
    pair_rows = ctx_rows // 2
    units = w_gate.shape[1]
    blocks = 2 * n
    ctx_index = lax.axis_index("ctx")
    wa_index = lax.axis_index("wa")
    x_index, core_index = wa_index // 2, wa_index % 2

    def both_halves(array, width):
        return array[:, :width], array[:, width:]

    q_halves = both_halves(w_query, HALF_Q)
    k_halves = both_halves(w_key, HALF_KV)
    v_halves = both_halves(w_value, HALF_KV)
    gain_two_part = lax.dynamic_slice_in_dim(gain_mlp, wa_index * part_rows, part_rows)
    gain_cols = jnp.concatenate(
        [jnp.broadcast_to(g[:, None], (part_rows, HEAD // 2)) for g in (gain_attn, gain_two_part)], 1
    )
    out_halves = both_halves(w_out.T, HALF_Q)
    halves = [
        jnp.concatenate([k_halves[i], v_halves[i], q_halves[i], gain_cols, out_halves[i]], 1)
        for i in range(2)
    ]

    half_ring = n // 2

    def gather_rows(halves, wide_block, prepared):
        mine = jnp.where(x_index == 0, halves[0], halves[1])
        theirs = jnp.where(x_index == 0, halves[1], halves[0])
        first_rows = ctx_rows // 2
        early = ring_send(wide_block[:first_rows], wide_block[:first_rows], n)
        came, prepared = lax.optimization_barrier((x_swap(theirs), prepared))
        low = jnp.where(x_index == 0, mine, came)
        high = jnp.where(x_index == 0, came, mine)
        pair = jnp.stack([low, high])
        other, early = lax.optimization_barrier((core_swap(pair), early))
        zero = jnp.where(core_index == 0, pair, other)
        one = jnp.where(core_index == 0, other, pair)
        quad = jnp.stack([zero, one], 1).reshape(ctx_rows, -1)
        sent = lax.dynamic_slice_in_dim(quad, core_index * pair_rows, pair_rows, 0)
        held = ring_gather(sent, n)
        late = ring_send(wide_block[first_rows:], wide_block[first_rows:], n)
        wide = {
            0: wide_block,
            n - 1: jnp.concatenate([early[0], late[0]], 0),
            1: jnp.concatenate([early[1], late[1]], 0),
        }
        for step in range(2, half_ring - 2):
            wide = ring_gather_step(wide, step, n)
        held, wide = lax.optimization_barrier((held, wide))
        ordered = jnp.zeros((n,) + sent.shape, bf16)
        for k in range(n):
            ordered = lax.dynamic_update_index_in_dim(ordered, held[k], ring_id(ctx_index, k, n), 0)
        held = ordered
        opposite = core_swap(held)
        whole = jnp.where(
            core_index == 0,
            jnp.concatenate([held, opposite], 1),
            jnp.concatenate([opposite, held], 1),
        )
        return whole.reshape(n * ctx_rows, -1), wide, prepared

    at = jnp.stack([ctx_index, core_index]).astype(jnp.int32)
    table, ring, rows_info, cosine, sine, x_own, run_cotangent = pl.pallas_call(
        functools.partial(prepare_kernel, n),
        out_shape=(
            jax.ShapeDtypeStruct((blocks + 9,), jnp.int32),
            jax.ShapeDtypeStruct((n + 1,), jnp.int32),
            jax.ShapeDtypeStruct((4, GROUP * run_rows), jnp.int32),
            jax.ShapeDtypeStruct((own_rows, SLAB), f32),
            jax.ShapeDtypeStruct((own_rows, SLAB), f32),
            jax.ShapeDtypeStruct((own_rows, model), bf16),
            jax.ShapeDtypeStruct((local_rows, model), bf16),
        ),
        in_specs=[smem()] * 2 + [vmem()] * 3,
        out_specs=(smem(),) * 2 + (vmem(),) * 5,
        compiler_params=params(),
        cost_estimate=cost(6),
    )(at, pair_order, segments.reshape(-1, local_rows // PIECES), inputs, cotangent)

    wide_block = jnp.concatenate([w_gate, w_up, w_down.T], 1)
    prepared = (table, ring, rows_info, cosine, sine, x_own, run_cotangent)
    w_all, wide, prepared = gather_rows(halves, wide_block, prepared)
    table, ring, rows_info, cosine, sine, x_own, run_cotangent = prepared
    w_out_t = w_all[:, PACK:]
    normed, queries, kv_own, gains = pl.pallas_call(
        project_kernel,
        out_shape=(
            jax.ShapeDtypeStruct((own_rows, model), bf16),
            jax.ShapeDtypeStruct((own_rows, Q_WIDE), bf16),
            jax.ShapeDtypeStruct((own_rows, 2 * HALF_KV), bf16),
            jax.ShapeDtypeStruct((2, model), f32),
        ),
        in_specs=[vmem()] * 4,
        out_specs=(vmem(),) * 4,
        compiler_params=params(),
        cost_estimate=cost(5),
    )(x_own, w_all, cosine, sine)

    kv_found = ring_gather(kv_own, n)
    kv_core = jnp.concatenate([kv_found[k] for k in range(n)], 0)
    kv_other = core_swap(kv_core)
    wide, kv_core, kv_other = lax.optimization_barrier((wide, kv_core, kv_other))
    wide = ring_gather_step(wide, half_ring - 2, n)

    mixed, mixed_b, log_total = pl.pallas_call(
        functools.partial(forward_kernel, blocks),
        out_shape=(
            jax.ShapeDtypeStruct((own_rows, Q_WIDE), f32),
            jax.ShapeDtypeStruct((own_rows, Q_WIDE), bf16),
            jax.ShapeDtypeStruct((8, GROUP * run_rows), f32),
        ),
        in_specs=[smem()] + [vmem()] * 4,
        out_specs=(vmem(),) * 3,
        scratch_shapes=[
            pltpu.VMEM((HALF_GROUPS * SLAB, GROUP * run_rows), f32),
            pltpu.VMEM((8 * HALF_GROUPS, GROUP * run_rows), f32),
            pltpu.VMEM((8 * HALF_GROUPS, GROUP * run_rows), f32),
        ],
        compiler_params=params(14 + n // 2),
        cost_estimate=cost(16),
    )(table, queries, kv_core, kv_other, rows_info)

    wide, mixed_b = lax.optimization_barrier((wide, mixed_b))
    wide = ring_gather_step(wide, half_ring - 1, n)
    attn_part = rounded(dot(mixed_b[:, :HALF_Q], w_all[:, PACK:], 1, 1))
    attn_came = x_swap(attn_part)
    wide, attn_came = lax.optimization_barrier((wide, attn_came))
    wide = ring_gather_step(wide, half_ring, n)
    x_f = x_own.astype(f32)
    hidden_own = x_f + (attn_part.astype(f32) + attn_came.astype(f32))
    hidden_other = core_swap(hidden_own)
    wide, hidden_other = lax.optimization_barrier((wide, hidden_other))
    wide = [wide[k] for k in range(n)]
    whole_tiles = ctx_rows % 16 == 0
    if not whole_tiles:
        wide_full = jnp.zeros((n,) + wide_block.shape, bf16)
        for k in range(n):
            wide_full = lax.dynamic_update_index_in_dim(wide_full, wide[k], ring_id(ctx_index, k, n), 0)
        wide = [wide_full.reshape(model, 3 * units)]

    def join(own, other):
        return jnp.where(
            core_index == 0, jnp.concatenate([own, other], 0), jnp.concatenate([other, own], 0)
        )

    normed_two, active, grads_wide, grad_two_own, grad_two_other = pl.pallas_call(
        functools.partial(feed_kernel, unit_tile=min(256, units)),
        out_shape=(
            jax.ShapeDtypeStruct((local_rows, model), bf16),
            jax.ShapeDtypeStruct((local_rows, units), bf16),
            jax.ShapeDtypeStruct((local_rows, 2 * units), bf16),
            jax.ShapeDtypeStruct((own_rows, model), f32),
            jax.ShapeDtypeStruct((own_rows, model), bf16),
        ),
        in_specs=[smem()] + [vmem()] * 4 + [pl.BlockSpec(memory_space=pl.ANY)] * len(wide),
        out_specs=(vmem(),) * 5,
        scratch_shapes=[
            pltpu.VMEM((model, 3 * units), bf16),
            pltpu.SemaphoreType.DMA((len(wide),)),
        ],
        compiler_params=params(),
        cost_estimate=cost(12),
    )(ring, hidden_own, hidden_other, gains, run_cotangent, *wide)
    shapes = (
        (jax.ShapeDtypeStruct((ctx_rows, 3 * units), bf16),) * n
        if whole_tiles
        else (jax.ShapeDtypeStruct((model, 3 * units), bf16),)
    )
    unit_tile = min(256, units)
    *d_terms, mlp_own, mlp_other = pl.pallas_call(
        functools.partial(feed_weights_kernel, n, len(wide)),
        out_shape=shapes
        + (
            jax.ShapeDtypeStruct((own_rows, model), f32),
            jax.ShapeDtypeStruct((own_rows, model), bf16),
        ),
        in_specs=[smem()] + [vmem()] * 4 + [pl.BlockSpec(memory_space=pl.ANY)] * len(wide),
        out_specs=(vmem(),) * (len(shapes) + 2),
        scratch_shapes=[
            pltpu.VMEM((model, unit_tile), bf16),
            pltpu.VMEM((model, units), bf16),
            pltpu.SemaphoreType.DMA((len(wide),)),
        ],
        compiler_params=params(),
        cost_estimate=cost(9),
    )(ring, normed_two, active, grads_wide, run_cotangent, *wide)
    if not whole_tiles:
        d_blocks = d_terms[0].reshape(n, ctx_rows, 3 * units)
        d_terms = [
            lax.dynamic_index_in_dim(d_blocks, ring_id(ctx_index, k, n), 0, keepdims=False) for k in range(n)
        ]
    def chip_sum(own, other):
        return rounded(own + core_swap(other).astype(f32))

    grad_two = chip_sum(grad_two_own, grad_two_other)
    grad_two_came, d_terms, mlp_own = lax.optimization_barrier((x_swap(grad_two), d_terms, mlp_own))
    d_came = None
    for step in range(1, half_ring - 2):
        d_came = ring_scatter_step(d_terms, d_came, step, n)
    output_chip = chip_sum(mlp_own, mlp_other)
    grad_hidden, grad_attn, grad_mixed, grad_gain_two = pl.pallas_call(
        hidden_grad_kernel,
        out_shape=(
            jax.ShapeDtypeStruct((own_rows, model), f32),
            jax.ShapeDtypeStruct((own_rows, model), bf16),
            jax.ShapeDtypeStruct((own_rows, Q_WIDE), bf16),
            jax.ShapeDtypeStruct((1, model), f32),
        ),
        in_specs=[smem()] + [vmem()] * 6,
        out_specs=(vmem(),) * 4,
        compiler_params=params(),
        cost_estimate=cost(5),
    )(ring, hidden_own, grad_two, grad_two_came, gains, run_cotangent, w_all)
    d_came, grad_mixed, output_chip = lax.optimization_barrier((d_came, grad_mixed, output_chip))
    d_came = ring_scatter_step(d_terms, d_came, half_ring - 2, n)

    dq_lin, dkv_core, dkv_other = pl.pallas_call(
        functools.partial(backward_kernel, blocks),
        out_shape=(
            jax.ShapeDtypeStruct((own_rows, Q_WIDE), bf16),
            jax.ShapeDtypeStruct(kv_core.shape, f32),
            jax.ShapeDtypeStruct(kv_core.shape, bf16),
        ),
        in_specs=[smem()] + [vmem()] * 9,
        out_specs=(vmem(),) * 3,
        scratch_shapes=[
            pltpu.VMEM((2 * SLAB, HEADS // 2 * run_rows), f32),
            pltpu.VMEM((own_rows, Q_WIDE), f32),
            pltpu.VMEM(kv_core.shape, f32),
            pltpu.VMEM((HEADS // 2 * run_rows, 2 * SLAB), bf16),
            pltpu.VMEM((HEADS // 2 * run_rows, 2 * SLAB), bf16),
        ],
        compiler_params=params(12 + 2 * n),
        cost_estimate=cost(24),
    )(table, queries, kv_core, kv_other, rows_info, mixed, log_total, grad_mixed, cosine, sine)

    def scatter_rows(part, crossing):
        cols = part.shape[1]
        split = part.reshape(n, 2, pair_rows, cols)
        mine = lax.dynamic_index_in_dim(split, core_index, 1, keepdims=False)
        theirs = lax.dynamic_index_in_dim(split, 1 - core_index, 1, keepdims=False)
        chip = mine.astype(f32) + core_swap(theirs).astype(f32)
        terms = [lax.dynamic_index_in_dim(chip, ring_id(ctx_index, k, n), 0, keepdims=False) for k in range(n)]
        came, (crossed,) = ring_scatter(terms, n, {2: x_swap(crossing)})
        total = terms[0] + came[0].astype(f32) + came[1].astype(f32)
        total_b = total.astype(bf16)
        opposite = core_swap(total_b)
        rows = jnp.where(
            core_index == 0,
            jnp.concatenate([total_b, opposite], 0),
            jnp.concatenate([opposite, total_b], 0),
        )
        quad = rows.reshape(2, 2, part_rows, cols)
        kept = lax.dynamic_index_in_dim(
            lax.dynamic_index_in_dim(quad, x_index, 0, keepdims=False), core_index, 0, keepdims=False
        )
        sent = lax.dynamic_index_in_dim(
            lax.dynamic_index_in_dim(quad, 1 - x_index, 0, keepdims=False), core_index, 0, keepdims=False
        )
        came = x_swap(sent)
        return rows, kept, came, crossed

    dkv_other, d_came, output_came = lax.optimization_barrier((dkv_other, d_came, x_swap(output_chip)))
    d_step = ring_scatter_step(d_terms, d_came, half_ring - 1, n)
    dkv = dkv_core + core_swap(dkv_other).astype(f32)
    dkv = dkv.reshape(n, own_rows, 2 * HALF_KV)
    dkv_own, (dkv_came, (d_came,)) = dkv[0], ring_scatter(dkv, n, {half_ring - 1: d_step})
    d_came = ring_scatter_step(d_terms, d_came, half_ring, n)
    output_own = (hidden_own + (output_chip.astype(f32) + output_came.astype(f32))).astype(bf16)
    output = as_dealt(join(output_own, core_swap(output_own)), pieces)
    normed_part, d_in = pl.pallas_call(
        last_kernel,
        out_shape=(
            jax.ShapeDtypeStruct((own_rows, model), bf16),
            jax.ShapeDtypeStruct((model, PACK + HALF_Q), bf16),
        ),
        in_specs=[vmem()] * (10 + len(dkv_came)),
        out_specs=(vmem(),) * 2,
        scratch_shapes=[pltpu.VMEM((own_rows, PACK), bf16)],
        compiler_params=params(56),
        cost_estimate=cost(5),
    )(dkv_own, dq_lin, cosine, sine, w_all, normed, x_own, grad_attn, mixed_b, grad_gain_two, *dkv_came)
    d_in, d_came = lax.optimization_barrier((d_in, d_came))
    in_rows, kept, came, normed_came = scatter_rows(d_in, normed_part)
    d_mlp = d_terms[0].astype(f32) + d_came[0].astype(f32) + d_came[1].astype(f32)
    grad_w_gate = d_mlp[:, :units]
    grad_w_up = d_mlp[:, units : 2 * units]
    grad_w_down = d_mlp[:, 2 * units :].T

    grad_w_query, grad_w_key, grad_w_value, grad_w_out, grad_gain = pl.pallas_call(
        finish_kernel,
        out_shape=(
            jax.ShapeDtypeStruct((part_rows, 2 * HALF_Q), f32),
            jax.ShapeDtypeStruct((part_rows, 2 * HALF_KV), f32),
            jax.ShapeDtypeStruct((part_rows, 2 * HALF_KV), f32),
            jax.ShapeDtypeStruct((part_rows, 2 * HALF_Q), f32),
            jax.ShapeDtypeStruct((part_rows, 1), f32),
        ),
        in_specs=[smem(), vmem(), vmem()],
        out_specs=(vmem(),) * 5,
        compiler_params=params(),
        cost_estimate=cost(2),
    )(x_index.reshape(1).astype(jnp.int32), kept, came)
    grad_w_out = grad_w_out.T
    grad_gain_attn = grad_gain[:, 0]

    grad_normed = normed_part.astype(f32) + normed_came.astype(f32)
    scale_one = lax.rsqrt(jnp.mean(x_f * x_f, -1, keepdims=True) + epsilon)
    input_rows, unused_gain = norm_backward(grad_normed, x_f * scale_one, scale_one, gains[:1])
    grad_inputs_own = (grad_hidden + input_rows).astype(bf16)
    grad_inputs = as_dealt(join(grad_inputs_own, core_swap(grad_inputs_own)), pieces)
    grad_gain_mlp = in_rows[:, PACK - 1].astype(f32)
    return (
        output,
        grad_inputs,
        grad_gain_attn,
        grad_w_query,
        grad_w_key,
        grad_w_value,
        grad_w_out,
        grad_gain_mlp,
        grad_w_gate,
        grad_w_up,
        grad_w_down,
    )


def solution(mesh):
    n = mesh.shape["ctx"]

    def body(*args):
        return on_device(n, args)

    return jax.shard_map(
        body,
        mesh=mesh,
        in_specs=(
            P("ctx", None),
            P("ctx", None),
            P(),
            P(),
            P(("ctx", "wa")),
            P(("ctx", "wa"), None),
            P(("ctx", "wa"), None),
            P(("ctx", "wa"), None),
            P(None, ("ctx", "wa")),
            P("ctx"),
            P("ctx", "wa"),
            P("ctx", "wa"),
            P("wa", "ctx"),
        ),
        out_specs=(
            P("ctx", None),
            P("ctx", None),
            P(("ctx", "wa")),
            P(("ctx", "wa"), None),
            P(("ctx", "wa"), None),
            P(("ctx", "wa"), None),
            P(None, ("ctx", "wa")),
            P("ctx"),
            P("ctx", "wa"),
            P("ctx", "wa"),
            P("wa", "ctx"),
        ),
        check_vma=False,
    )
```

```python
import functools
import math

import jax
import jax.numpy as jnp
from jax import lax
from jax.experimental import pallas as pl
from jax.experimental.pallas import tpu as pltpu
from jax.sharding import PartitionSpec as P

HEADS = 18
KV_HEADS = 6
HEAD = 64
GROUP = HEADS // KV_HEADS
HALF_Q = HEADS * HEAD // 2
HALF_KV = KV_HEADS * HEAD // 2
HALF_GROUPS = KV_HEADS // 2
SLAB = 128
PACK = 2 * HALF_KV + HALF_Q + HEAD
Q_WIDE = HALF_Q + HEAD

epsilon = 1e-05
rope_base = 10000.0
masked_score = -1e30
DOCS = 16
PIECES = 4
f32 = jnp.float32
bf16 = jnp.bfloat16
MIB = 1024 * 1024

K_PLACE = [divmod(g, 2) for g in range(HALF_GROUPS)]
V_PLACE = [divmod(HALF_GROUPS + g, 2) for g in range(HALF_GROUPS)]


def vmem():
    return pl.BlockSpec(memory_space=pltpu.VMEM)


def smem():
    return pl.BlockSpec(memory_space=pltpu.SMEM)


def params(mib=26):
    return pltpu.CompilerParams(vmem_limit_bytes=min(mib, 58) * MIB)


def cost(micros):
    return pl.CostEstimate(flops=int(micros * 1e9), bytes_accessed=0, transcendentals=0)


def dot(a, b, ca=1, cb=0):
    return lax.dot_general(a, b, (((ca,), (cb,)), ((), ())), preferred_element_type=f32)


def ctx_parts(n):
    slow = min(4, n)
    return slow, n // slow


def ctx_swap(block, n, k):
    return lax.ppermute(block, "ctx", [(i, i ^ k) for i in range(n)])


def wa_swap(block, k):
    return lax.ppermute(block, "wa", [(i, i ^ k) for i in range(4)])


def core_swap(block):
    return wa_swap(block, 1)


def x_swap(block):
    return wa_swap(block, 2)


def ring_order(n):
    slow, fast = ctx_parts(n)
    order = []
    for r in range(fast):
        line = [z * fast + r for z in range(slow)]
        order += line if r % 2 == 0 else line[::-1]
    return order


def ring_id(ctx, offset, n):
    slow, fast = ctx_parts(n)

    def along(r, z):
        return jnp.where(r % 2 == 0, z, slow - 1 - z)

    place = (ctx % fast) * slow + along(ctx % fast, ctx // fast)
    place = (place + offset) % n
    r = place // slow
    return along(r, place % slow) * fast + r


def ring_send(forward, backward, n):
    order = ring_order(n)
    pairs = [(order[p], order[(p + 1) % n]) for p in range(n)]
    return (
        lax.ppermute(forward, "ctx", pairs),
        lax.ppermute(backward, "ctx", [(b, a) for a, b in pairs]),
    )


def ring_gather_step(found, step, n):
    half_ring = n // 2
    f, b = found[(1 - step) % n], found[step - 1]
    if step == half_ring:
        half = f.shape[0] // 2
        parts = ring_send(f[:half], b[half:], n)
        return found | {half_ring: jnp.concatenate(parts, 0)}
    f, b = ring_send(f, b, n)
    return found | {n - step: f, step: b}


def ring_scatter_step(terms, came, step, n):
    half_ring = n // 2
    far = terms[half_ring]
    half = far.shape[0] // 2
    if step == 1:
        return ring_send(far[:half].astype(bf16), far[half:].astype(bf16), n)
    d = half_ring - step + 1
    f, b = terms[d].astype(f32), terms[n - d].astype(f32)
    came_f, came_b = came[0].astype(f32), came[1].astype(f32)
    if step == 2:
        rest = jnp.zeros_like(far[half:], f32)
        came_f = jnp.concatenate([came_f, rest], 0)
        came_b = jnp.concatenate([jnp.zeros_like(far[:half], f32), came_b], 0)
    return ring_send((f + came_f).astype(bf16), (b + came_b).astype(bf16), n)


def ring_gather(block, n):
    found = {0: block}
    for step in range(1, n // 2 + 1):
        found = ring_gather_step(found, step, n)
    return found


def ring_scatter(terms, n, beside=None):
    came = None
    beside = dict(beside or {})
    for step in range(1, n // 2 + 1):
        came = ring_scatter_step(terms, came, step, n)
        if step in beside:
            came, beside[step] = lax.optimization_barrier((came, beside[step]))
    return came, list(beside.values())


def rounded(array):
    return lax.optimization_barrier(array.astype(bf16))


def lane_half(shape):
    lane = lax.broadcasted_iota(jnp.int32, shape, 1)
    return lane // HEAD


def turn(z):
    lane = lax.broadcasted_iota(jnp.int32, z.shape, 1)
    return jnp.where(
        lane % HEAD < HEAD // 2,
        pltpu.roll(z, SLAB - HEAD // 2, 1),
        pltpu.roll(z, HEAD // 2, 1),
    )


def prepare_kernel(
    n, at_ref, pairs_ref, segments_ref, x_ref, cot_ref, table_ref, ring_ref, rows_ref, cos_ref, sin_ref, own_ref, cots_ref
):
    ctx, core = at_ref[0], at_ref[1]
    own_rows = own_ref.shape[0]
    run_rows = own_rows // 2
    piece = run_rows // 2
    blocks = 2 * n
    lower = pairs_ref[ctx]
    for c in range(2):
        for run in range(2):
            for p in range(2):
                to = c * own_rows + run * run_rows + p * piece
                source = (2 * c + p) * 2 * piece + run * piece
                cots_ref[to : to + piece, :] = cot_ref[source : source + piece, :]
    for run in range(2):
        for p in range(2):
            to = run * run_rows + p * piece
            source = pl.multiple_of((2 * core + p) * 2 * piece + run * piece, piece)
            own_ref[to : to + piece, :] = x_ref[pl.ds(source, piece), :]
    ring_ref[0] = core
    for k in range(n):
        ring_ref[1 + k] = ring_id(ctx, k, n)
    for k in range(n):
        low = pairs_ref[ring_ref[1 + k]]
        table_ref[low] = 2 * k
        table_ref[blocks - 1 - low] = 2 * k + 1
    counts = []
    every = segments_ref[...]
    for d in range(DOCS):
        here = (every == d + 1).astype(f32)
        counts.append(jnp.sum(here, 0, keepdims=True))
    count = jnp.sum(jnp.concatenate(counts, 0), 1, keepdims=True)
    docs = lax.broadcasted_iota(jnp.int32, (DOCS, run_rows), 0) + 1
    lane = lax.broadcasted_iota(jnp.int32, (1, run_rows), 1)
    first_piece = segments_ref[pl.ds(ctx * PIECES + 2 * core, 1), :]
    second_piece = segments_ref[pl.ds(ctx * PIECES + 2 * core + 1, 1), :]
    runs = (
        jnp.where(lane < piece, first_piece, pltpu.roll(second_piece, piece, 1)),
        jnp.where(lane < piece, pltpu.roll(first_piece, piece, 1), second_piece),
    )
    table_ref[blocks] = core
    for run in range(2):
        block = lower if run == 0 else blocks - 1 - lower
        position = block * (2 * run_rows) + core * run_rows + lane
        earlier = jnp.where(docs < runs[run], count, 0.0)
        start = jnp.sum(earlier, 0, keepdims=True)
        start = jnp.where(runs[run] > 0, start, position.astype(f32))
        first = jnp.min(start).astype(jnp.int32) // (2 * run_rows)
        latest = (jnp.max(start).astype(jnp.int32) + 2 * run_rows - 1) // (2 * run_rows)
        whole_from = jnp.minimum(jnp.maximum(latest, first), block + 1)
        whole_to = jnp.maximum(block, whole_from)
        for i, value in enumerate((first, whole_from, whole_to, block + 1)):
            table_ref[blocks + 1 + 4 * run + i] = value
        start = start.astype(jnp.int32)
        rows_ref[2 * run : 2 * run + 1, :] = jnp.concatenate([start] * GROUP, 1)
        rows_ref[2 * run + 1 : 2 * run + 2, :] = jnp.concatenate([position] * GROUP, 1)
    lanes = lax.broadcasted_iota(jnp.int32, (run_rows, SLAB), 1)
    row = lax.broadcasted_iota(jnp.int32, (run_rows, SLAB), 0)
    frequency = jnp.exp(-math.log(rope_base) * 2.0 * (lanes % (HEAD // 2)).astype(f32) / HEAD)
    for run in range(2):
        block = lower if run == 0 else blocks - 1 - lower
        angle = (block * (2 * run_rows) + core * run_rows + row).astype(f32) * frequency
        at = slice(run * run_rows, (run + 1) * run_rows)
        cos_ref[at, :] = jnp.cos(angle)
        sine = jnp.sin(angle)
        sin_ref[at, :] = jnp.where(lanes % HEAD < HEAD // 2, -sine, sine)


def project_kernel(x_ref, w_ref, cos_ref, sin_ref, normed_ref, q_ref, kv_ref, gains_ref):
    tail = w_ref[:, PACK - SLAB : PACK].astype(f32).T
    gains_ref[0:1, :] = tail[SLAB - HEAD : SLAB - HEAD + 1, :]
    gains_ref[1:2, :] = tail[SLAB - 1 :, :]
    gain_ref = gains_ref.at[0:1, :]
    x = x_ref[...].astype(f32)
    scale_rows = lax.rsqrt(jnp.mean(x * x, -1, keepdims=True) + epsilon)
    normed = (x * scale_rows * gain_ref[...]).astype(bf16)
    normed_ref[...] = normed
    cosine, sine = cos_ref[...], sin_ref[...]
    half = lane_half(cosine.shape)
    for s in range(PACK // SLAB):
        z = dot(normed, w_ref[:, s * SLAB : (s + 1) * SLAB])
        if s == 2:
            kv_ref[:, 2 * SLAB : 3 * SLAB] = z.astype(bf16)
            continue
        turned = z * cosine + turn(z) * sine
        if s == 0:
            kv_ref[:, :SLAB] = turned.astype(bf16)
        elif s == 1:
            kv_ref[:, SLAB : 2 * SLAB] = jnp.where(half == 0, turned, z).astype(bf16)
        else:
            scaled = turned * HEAD ** (-0.5)
            if s == PACK // SLAB - 1:
                scaled = jnp.where(half == 0, scaled, 0.0)
            q_ref[:, (s - 3) * SLAB : (s - 2) * SLAB] = scaled.astype(bf16)


def head_rows(ref, run, rows, g, place):
    parts = []
    for j in range(GROUP):
        slab, half = divmod(GROUP * g + j, 2)
        z = ref[run * rows : (run + 1) * rows, slab * SLAB : (slab + 1) * SLAB].astype(f32)
        if half != place:
            z = pltpu.roll(z, HEAD, 1)
        parts.append(jnp.where(lane_half(z.shape) == place, z, 0.0).astype(bf16))
    return jnp.concatenate(parts, 0)


def put_heads(ref, values, run, rows, g, place):
    flat = values.T
    for j in range(GROUP):
        slab, half = divmod(GROUP * g + j, 2)
        z = flat[j * rows : (j + 1) * rows, :]
        if half != place:
            z = pltpu.roll(z, HEAD, 1)
        where = (slice(run * rows, (run + 1) * rows), slice(slab * SLAB, (slab + 1) * SLAB))
        if half == 0:
            ref[where] = jnp.where(lane_half(z.shape) == 0, z, 0.0)
        else:
            ref[where] = jnp.where(lane_half(z.shape) == 1, z, ref[where])


def key_block(own_ref, other_ref, slot, rows, slab):
    at = pl.ds(pl.multiple_of(slot * rows, rows), rows)
    cols = slice(slab * SLAB, (slab + 1) * SLAB)
    return jnp.concatenate([own_ref[at, cols], other_ref[at, cols]], 0)


def key_places(block, core, rows, width):
    i = lax.broadcasted_iota(jnp.int32, (2 * rows, width), 0)
    mine = i + core * rows
    others = i - core * rows
    return block * (2 * rows) + jnp.where(i < rows, mine, others)


def forward_kernel(
    blocks, table, q_ref, own_ref, other_ref, rows_ref, mixed_ref, mixed_b_ref, log_ref, acc_ref, sum_ref, max_ref
):
    rows = q_ref.shape[0] // 2
    width = GROUP * rows
    core = table[blocks]
    for run in range(2):
        first, mid0, mid1, last = [table[blocks + 1 + 4 * run + i] for i in range(4)]
        start = rows_ref[2 * run : 2 * run + 1, :]
        stop = rows_ref[2 * run + 1 : 2 * run + 2, :]
        queries = [head_rows(q_ref, run, rows, g, K_PLACE[g][1]) for g in range(HALF_GROUPS)]
        acc_ref[...] = jnp.zeros_like(acc_ref)
        sum_ref[...] = jnp.zeros_like(sum_ref)
        max_ref[...] = jnp.full_like(max_ref, masked_score)

        def step(b, carry, masked):
            at_rows = pl.ds(pl.multiple_of(table[b] * rows, rows), rows)
            if masked:
                at = key_places(b, core, rows, width)
                ok = (at >= start) & (at <= stop)
            scores = []
            for g in range(HALF_GROUPS):
                cols = slice(K_PLACE[g][0] * SLAB, (K_PLACE[g][0] + 1) * SLAB)
                keys = jnp.concatenate([own_ref[at_rows, cols], other_ref[at_rows, cols]], 0)
                s = dot(keys, queries[g], 1, 1)
                if masked:
                    s = jnp.where(ok, s, masked_score)
                scores.append(s)
            for g in range(HALF_GROUPS):
                s = scores[g]
                cols = slice(V_PLACE[g][0] * SLAB, (V_PLACE[g][0] + 1) * SLAB)
                values = jnp.concatenate([own_ref[at_rows, cols], other_ref[at_rows, cols]], 0)
                before = max_ref[8 * g : 8 * g + 1, :]
                high = jnp.maximum(before, jnp.max(s, 0, keepdims=True))
                keep = jnp.exp(before - high)
                p = jnp.exp(s - high)
                max_ref[8 * g : 8 * g + 1, :] = high
                sum_ref[8 * g : 8 * g + 1, :] = sum_ref[8 * g : 8 * g + 1, :] * keep + jnp.sum(p, 0, keepdims=True)
                rows_g = slice(g * SLAB, (g + 1) * SLAB)
                acc_ref[rows_g, :] = acc_ref[rows_g, :] * keep + dot(values, p.astype(bf16), 0, 0)
            return carry

        lax.fori_loop(first, mid0, functools.partial(step, masked=True), 0)
        lax.fori_loop(mid0, mid1, functools.partial(step, masked=False), 0)
        lax.fori_loop(mid1, last, functools.partial(step, masked=True), 0)
        for g in range(HALF_GROUPS):
            total = sum_ref[8 * g : 8 * g + 1, :]
            log_ref[run * HALF_GROUPS + g : run * HALF_GROUPS + g + 1, :] = max_ref[8 * g : 8 * g + 1, :] + jnp.log(total)
            put_heads(mixed_ref, acc_ref[g * SLAB : (g + 1) * SLAB, :] * (1.0 / total), run, rows, g, V_PLACE[g][1])
    mixed_b_ref[...] = mixed_ref[...].astype(bf16)


def wide_rows(ref, run, rows, places, base):
    parts = []
    for g in range(HALF_GROUPS):
        slab, half = places[g]
        z = head_rows(ref, run, rows, g, half)
        zero = jnp.zeros_like(z)
        parts.append(jnp.concatenate([z, zero] if slab == base else [zero, z], 1))
    return jnp.concatenate(parts, 0)


def backward_kernel(blocks,
    table, q_ref, own_ref, other_ref, rows_ref, mixed_ref, log_ref, grad_ref, cos_ref, sin_ref,
    dq_ref, down_ref, dother_out, dq_buf, raw_buf, dother_ref, q_buf, g_buf):
    rows = q_ref.shape[0] // 2
    width = GROUP * rows
    core = table[blocks]
    down_ref[...] = jnp.zeros_like(down_ref)
    dother_ref[...] = jnp.zeros_like(dother_ref)
    for run in range(2):
        first, mid0, mid1, last = [table[blocks + 1 + 4 * run + i] for i in range(4)]
        start = rows_ref[2 * run : 2 * run + 1, :]
        stop = rows_ref[2 * run + 1 : 2 * run + 2, :]
        q_buf[...] = wide_rows(q_ref, run, rows, K_PLACE, 0)
        g_buf[...] = wide_rows(grad_ref, run, rows, V_PLACE, 1)
        logs, deltas = [], []
        for g in range(HALF_GROUPS):
            logs.append(log_ref[run * HALF_GROUPS + g : run * HALF_GROUPS + g + 1, :])
            parts = []
            for j in range(GROUP):
                slab, half = divmod(GROUP * g + j, 2)
                where = (slice(run * rows, (run + 1) * rows), slice(slab * SLAB, (slab + 1) * SLAB))
                z = grad_ref[where].astype(f32) * mixed_ref[where]
                z = jnp.where(lane_half(z.shape) == half, z, 0.0)
                parts.append(jnp.sum(z.T, 0, keepdims=True))
            deltas.append(jnp.concatenate(parts, 1))
        log_all = jnp.concatenate(logs, 1)
        delta_all = jnp.concatenate(deltas, 1)
        dq_buf[...] = jnp.zeros_like(dq_buf)

        def step(b, carry, masked):
            at_rows = pl.ds(pl.multiple_of(table[b] * rows, rows), rows)
            keys = jnp.concatenate([own_ref[at_rows, : 2 * SLAB], other_ref[at_rows, : 2 * SLAB]], 0)
            vals = jnp.concatenate([own_ref[at_rows, SLAB:], other_ref[at_rows, SLAB:]], 0)
            if masked:
                at = key_places(b, core, rows, width)
                ok = (at >= start) & (at <= stop)
            ps, dss = [], []
            for g in range(HALF_GROUPS):
                rg = slice(g * width, (g + 1) * width)
                s = dot(keys, q_buf[rg, :], 1, 1)
                p = jnp.exp(s - log_all[:, rg])
                if masked:
                    p = jnp.where(ok, p, 0.0)
                dp = dot(vals, g_buf[rg, :], 1, 1)
                ps.append(p.astype(bf16))
                dss.append((p * (dp - delta_all[:, rg])).astype(bf16))
            ds = jnp.concatenate(dss, 1)
            p = jnp.concatenate(ps, 1)
            dq_buf[...] += dot(keys, ds, 0, 0)
            dk = dot(ds, q_buf[...])
            dv = dot(p, g_buf[...])
            for i, val in ((0, dk[:, :SLAB]), (1, dk[:, SLAB:] + dv[:, :SLAB]), (2, dv[:, SLAB:])):
                cols = slice(i * SLAB, (i + 1) * SLAB)
                down_ref[at_rows, cols] += val[:rows]
                dother_ref[at_rows, cols] += val[rows:]
            return carry

        lax.fori_loop(first, mid0, functools.partial(step, masked=True), 0)
        lax.fori_loop(mid0, mid1, functools.partial(step, masked=False), 0)
        lax.fori_loop(mid1, last, functools.partial(step, masked=True), 0)
        for g in range(HALF_GROUPS):
            slab, half = K_PLACE[g]
            put_heads(raw_buf, dq_buf[slab * SLAB : (slab + 1) * SLAB, g * width : (g + 1) * width], run, rows, g, half)
    dother_out[...] = dother_ref[...].astype(bf16)
    cosine, sine = cos_ref[...], sin_ref[...]
    for s in range(Q_WIDE // SLAB):
        z = raw_buf[:, s * SLAB : (s + 1) * SLAB] * HEAD ** (-0.5)
        dq_ref[:, s * SLAB : (s + 1) * SLAB] = (z * cosine - turn(z) * sine).astype(bf16)


def put_weights(ring_ref, block_refs, whole_ref, sems, first, columns):
    copies = []
    for k, ref in enumerate(block_refs):
        block = ref.shape[0]
        at = 0 if len(block_refs) == 1 else pl.multiple_of(ring_ref[1 + k] * block, block)
        copy = pltpu.make_async_copy(
            ref.at[:, pl.ds(first, columns)], whole_ref.at[pl.ds(at, block), :], sems.at[k]
        )
        copy.start()
        copies.append(copy)
    return copies


def feed_kernel(ring_ref, own_ref, other_ref, gain_ref, cot_ref, *rest, unit_tile):
    *block_refs, normed_ref, active_ref, grads_ref, part_ref, part_other_ref, wide_ref, sems = rest
    core_ref = ring_ref
    copies = put_weights(ring_ref, block_refs, wide_ref, sems, 0, wide_ref.shape[1])
    rows = own_ref.shape[0]
    units = active_ref.shape[1]
    gain = gain_ref[1:2, :]
    own_at = pl.multiple_of(core_ref[0] * rows, rows)
    other_at = pl.multiple_of((1 - core_ref[0]) * rows, rows)
    for ref, at in ((own_ref, own_at), (other_ref, other_at)):
        x = ref[...]
        scale_rows = lax.rsqrt(jnp.mean(x * x, -1, keepdims=True) + epsilon)
        normed_ref[pl.ds(at, rows), :] = (x * scale_rows * gain).astype(bf16)
    for copy in copies:
        copy.wait()

    @pl.loop(0, units // unit_tile)
    def unit_step(t):
        at = pl.multiple_of(t * unit_tile, unit_tile)
        cols = pl.ds(at, unit_tile)
        up_cols = pl.ds(pl.multiple_of(units + at, unit_tile), unit_tile)
        gate = dot(normed_ref[...], wide_ref[:, cols])
        up = dot(normed_ref[...], wide_ref[:, up_cols])
        grad_active = dot(cot_ref[...], wide_ref[:, pl.ds(pl.multiple_of(2 * units + at, unit_tile), unit_tile)])
        sig = jax.nn.sigmoid(gate)
        silu = gate * sig
        active_ref[:, cols] = (silu * up).astype(bf16)
        grads_ref[:, cols] = (grad_active * up * (sig * (1.0 + gate * (1.0 - sig)))).astype(bf16)
        grads_ref[:, up_cols] = (grad_active * silu).astype(bf16)

    model = normed_ref.shape[1]
    tile = model // 3

    @pl.loop(0, 3)
    def model_step(t):
        at = pl.ds(pl.multiple_of(t * tile, tile), tile)
        wide = wide_ref[at, : 2 * units]
        part_ref[:, at] = dot(grads_ref[pl.ds(own_at, rows), :], wide, 1, 1)
        part_other_ref[:, at] = dot(grads_ref[pl.ds(other_at, rows), :], wide, 1, 1).astype(bf16)


def feed_weights_kernel(n, count, place_ref, normed_ref, active_ref, grads_ref, cot_ref, *outs):
    weight_refs = outs[:count]
    *block_refs, out_ref, out_other_ref, buf, down_ref, sems = outs[count:]
    units = active_ref.shape[1]
    copies = put_weights(place_ref, weight_refs, down_ref, sems, 2 * units, units)
    rows = out_ref.shape[0]
    units = active_ref.shape[1]
    model = normed_ref.shape[1]
    tile = buf.shape[1]
    own_at = pl.multiple_of(place_ref[0] * rows, rows)
    other_at = pl.multiple_of((1 - place_ref[0]) * rows, rows)

    def put(values, at):
        if len(block_refs) == 1:
            block_refs[0][:, at] = values.astype(bf16)
            return
        buf[...] = values.astype(bf16)
        block = model // n
        for k in range(n):
            block_refs[k][:, at] = buf[pl.ds(pl.multiple_of(place_ref[1 + k] * block, block), block), :]

    @pl.loop(0, units // tile)
    def weight_step(t):
        for i in range(3):
            cols = pl.ds(pl.multiple_of(t * tile, tile), tile)
            at = pl.ds(pl.multiple_of(i * units + t * tile, tile), tile)
            if i < 2:
                put(dot(normed_ref[...], grads_ref[:, at], 0, 0), at)
            else:
                put(dot(cot_ref[...], active_ref[:, cols], 0, 0), at)

    wide_tile = model // 3
    for copy in copies:
        copy.wait()

    @pl.loop(0, 3)
    def out_step(t):
        at = pl.ds(pl.multiple_of(t * wide_tile, wide_tile), wide_tile)
        down = down_ref[at, :]
        out_ref[:, at] = dot(active_ref[pl.ds(own_at, rows), :], down, 1, 1)
        out_other_ref[:, at] = dot(active_ref[pl.ds(other_at, rows), :], down, 1, 1).astype(bf16)


def hidden_grad_kernel(
    core_ref, hidden_ref, mine_ref, came_ref, gains_ref, cot_ref, w_ref, grad_ref, attn_ref, mixed_ref, gain_ref
):
    rows = hidden_ref.shape[0]
    hidden = hidden_ref[...]
    grad_normed = mine_ref[...].astype(f32) + came_ref[...].astype(f32)
    scale_rows = lax.rsqrt(jnp.mean(hidden * hidden, -1, keepdims=True) + epsilon)
    unit = hidden * scale_rows
    gain_ref[...] = jnp.sum(grad_normed * unit, 0, keepdims=True)
    grad_unit = grad_normed * gains_ref[1:2, :]
    inner = jnp.mean(grad_unit * unit, -1, keepdims=True)
    cot = cot_ref[pl.ds(pl.multiple_of(core_ref[0] * rows, rows), rows), :].astype(f32)
    grad = cot + scale_rows * (grad_unit - unit * inner)
    grad_ref[...] = grad
    attn_ref[...] = grad.astype(bf16)
    mixed_ref[:, :HALF_Q] = dot(attn_ref[...], w_ref[:, PACK:]).astype(bf16)
    mixed_ref[:, HALF_Q:] = jnp.zeros((rows, HEAD), bf16)


def last_kernel(
    dkv_ref, dq_ref, cos_ref, sin_ref, w_ref, normed_ref, x_ref, grad_attn_ref, mixed_ref, gain_two_ref, *rest
):
    *came_refs, part_ref, dw_ref, lin_ref = rest
    cosine, sine = cos_ref[...], sin_ref[...]
    half = lane_half(cosine.shape)
    for s in range(3):
        cols = slice(s * SLAB, (s + 1) * SLAB)
        z = dkv_ref[:, cols]
        for ref in came_refs:
            z = z + ref[:, cols].astype(f32)
        turned = z * cosine - turn(z) * sine
        lin_ref[:, cols] = (turned if s == 0 else jnp.where(half == 0, turned, z) if s == 1 else z).astype(bf16)
    lin_ref[:, 3 * SLAB :] = dq_ref[...]
    x = x_ref[...].astype(f32)
    scale_rows = lax.rsqrt(jnp.mean(x * x, -1, keepdims=True) + epsilon)
    model = normed_ref.shape[1]
    tile = model // 3
    last = PACK - SLAB

    @pl.loop(0, 3)
    def model_step(t):
        at = pl.ds(pl.multiple_of(t * tile, tile), tile)
        part = dot(lin_ref[...], w_ref[at, :PACK], 1, 1)
        part_ref[:, at] = part.astype(bf16)
        unit = x_ref[:, at].astype(f32) * scale_rows
        gain_one = jnp.sum(part * unit, 0, keepdims=True)
        gain_one = jnp.broadcast_to(gain_one, (SLAB, tile)).T
        gain_two = jnp.broadcast_to(gain_two_ref[:, at], (SLAB, tile)).T
        dw = dot(normed_ref[:, at], lin_ref[...], 0, 0)
        dw_ref[at, :last] = dw[:, :last].astype(bf16)
        lane = lax.broadcasted_iota(jnp.int32, (tile, SLAB), 1)
        gains = jnp.where(lane < HEAD + HEAD // 2, gain_one, gain_two)
        dw_ref[at, last:PACK] = jnp.where(lane < HEAD, dw[:, last:], gains).astype(bf16)
        dw_ref[at, PACK:] = dot(grad_attn_ref[:, at], mixed_ref[:, :HALF_Q], 0, 0).astype(bf16)


def finish_kernel(x_ref, kept_ref, came_ref, query_ref, key_ref, value_ref, out_ref, gain_ref):
    first = x_ref[0] == 0
    kept, came = kept_ref[...].astype(f32), came_ref[...].astype(f32)
    k_end, v_end, q_end = HALF_KV, 2 * HALF_KV, 2 * HALF_KV + HALF_Q
    for half in range(2):
        z = jnp.where(first, kept, came) if half == 0 else jnp.where(first, came, kept)
        key_ref[:, half * HALF_KV : (half + 1) * HALF_KV] = z[:, :k_end]
        value_ref[:, half * HALF_KV : (half + 1) * HALF_KV] = z[:, k_end:v_end]
        query_ref[:, half * HALF_Q : (half + 1) * HALF_Q] = z[:, v_end:q_end]
        out_ref[:, half * HALF_Q : (half + 1) * HALF_Q] = z[:, PACK:]
    gain_ref[...] = kept[:, q_end : q_end + 1] + came[:, q_end : q_end + 1]


def as_dealt(array, pieces):
    rows = array.shape[0]
    rest = array.shape[1:]
    axes = (0, 2, 1, 3) + tuple(4 + i for i in range(len(rest)))
    split = array.reshape((2, 2, pieces // 2, rows // (2 * pieces)) + rest)
    return jnp.transpose(split, axes).reshape((rows,) + rest)


def norm_backward(grad_normed, unit_rows, scale_rows, gain):
    grad_unit = grad_normed * gain
    grad_gain = jnp.sum(grad_normed * unit_rows, 0)
    grad_rows = scale_rows * (
        grad_unit - unit_rows * jnp.mean(grad_unit * unit_rows, -1, keepdims=True)
    )
    return grad_rows, grad_gain


def on_device(n, args):
    (inputs, cotangent, segments, pair_order, gain_attn, w_query, w_key, w_value, w_out, gain_mlp,
     w_gate, w_up, w_down) = args
    local_rows, model = inputs.shape
    pieces = PIECES
    own_rows = local_rows // 2
    run_rows = own_rows // 2
    part_rows = gain_attn.shape[0]
    ctx_rows = gain_mlp.shape[0]
    pair_rows = ctx_rows // 2
    units = w_gate.shape[1]
    blocks = 2 * n
    ctx_index = lax.axis_index("ctx")
    wa_index = lax.axis_index("wa")
    x_index, core_index = wa_index // 2, wa_index % 2

    def both_halves(array, width):
        return array[:, :width], array[:, width:]

    q_halves = both_halves(w_query, HALF_Q)
    k_halves = both_halves(w_key, HALF_KV)
    v_halves = both_halves(w_value, HALF_KV)
    gain_two_part = lax.dynamic_slice_in_dim(gain_mlp, wa_index * part_rows, part_rows)
    gain_cols = jnp.concatenate(
        [jnp.broadcast_to(g[:, None], (part_rows, HEAD // 2)) for g in (gain_attn, gain_two_part)], 1
    )
    out_halves = both_halves(w_out.T, HALF_Q)
    halves = [
        jnp.concatenate([k_halves[i], v_halves[i], q_halves[i], gain_cols, out_halves[i]], 1)
        for i in range(2)
    ]

    half_ring = n // 2

    def gather_rows(halves, wide_block, prepared):
        mine = jnp.where(x_index == 0, halves[0], halves[1])
        theirs = jnp.where(x_index == 0, halves[1], halves[0])
        first_rows = 2 * ctx_rows // 3
        early = ring_send(wide_block[:first_rows], wide_block[:first_rows], n)
        came, prepared = lax.optimization_barrier((x_swap(theirs), prepared))
        low = jnp.where(x_index == 0, mine, came)
        high = jnp.where(x_index == 0, came, mine)
        pair = jnp.stack([low, high])
        other, early = lax.optimization_barrier((core_swap(pair), early))
        zero = jnp.where(core_index == 0, pair, other)
        one = jnp.where(core_index == 0, other, pair)
        quad = jnp.stack([zero, one], 1).reshape(ctx_rows, -1)
        sent = lax.dynamic_slice_in_dim(quad, core_index * pair_rows, pair_rows, 0)
        held = ring_gather(sent, n)
        late = ring_send(wide_block[first_rows:], wide_block[first_rows:], n)
        wide = {
            0: wide_block,
            n - 1: jnp.concatenate([early[0], late[0]], 0),
            1: jnp.concatenate([early[1], late[1]], 0),
        }
        for step in range(2, half_ring - 2):
            wide = ring_gather_step(wide, step, n)
        held, wide = lax.optimization_barrier((held, wide))
        ordered = jnp.zeros((n,) + sent.shape, bf16)
        for k in range(n):
            ordered = lax.dynamic_update_index_in_dim(ordered, held[k], ring_id(ctx_index, k, n), 0)
        held = ordered
        opposite = core_swap(held)
        whole = jnp.where(
            core_index == 0,
            jnp.concatenate([held, opposite], 1),
            jnp.concatenate([opposite, held], 1),
        )
        return whole.reshape(n * ctx_rows, -1), wide, prepared

    at = jnp.stack([ctx_index, core_index]).astype(jnp.int32)
    table, ring, rows_info, cosine, sine, x_own, run_cotangent = pl.pallas_call(
        functools.partial(prepare_kernel, n),
        out_shape=(
            jax.ShapeDtypeStruct((blocks + 9,), jnp.int32),
            jax.ShapeDtypeStruct((n + 1,), jnp.int32),
            jax.ShapeDtypeStruct((4, GROUP * run_rows), jnp.int32),
            jax.ShapeDtypeStruct((own_rows, SLAB), f32),
            jax.ShapeDtypeStruct((own_rows, SLAB), f32),
            jax.ShapeDtypeStruct((own_rows, model), bf16),
            jax.ShapeDtypeStruct((local_rows, model), bf16),
        ),
        in_specs=[smem()] * 2 + [vmem()] * 3,
        out_specs=(smem(),) * 2 + (vmem(),) * 5,
        compiler_params=params(),
        cost_estimate=cost(6),
    )(at, pair_order, segments.reshape(-1, local_rows // PIECES), inputs, cotangent)

    wide_block = jnp.concatenate([w_gate, w_up, w_down.T], 1)
    prepared = (table, ring, rows_info, cosine, sine, x_own, run_cotangent)
    w_all, wide, prepared = gather_rows(halves, wide_block, prepared)
    table, ring, rows_info, cosine, sine, x_own, run_cotangent = prepared
    w_out_t = w_all[:, PACK:]
    normed, queries, kv_own, gains = pl.pallas_call(
        project_kernel,
        out_shape=(
            jax.ShapeDtypeStruct((own_rows, model), bf16),
            jax.ShapeDtypeStruct((own_rows, Q_WIDE), bf16),
            jax.ShapeDtypeStruct((own_rows, 2 * HALF_KV), bf16),
            jax.ShapeDtypeStruct((2, model), f32),
        ),
        in_specs=[vmem()] * 4,
        out_specs=(vmem(),) * 4,
        compiler_params=params(),
        cost_estimate=cost(5),
    )(x_own, w_all, cosine, sine)

    kv_found = ring_gather(kv_own, n)
    kv_core = jnp.concatenate([kv_found[k] for k in range(n)], 0)
    kv_other = core_swap(kv_core)
    wide, kv_core, kv_other = lax.optimization_barrier((wide, kv_core, kv_other))
    wide = ring_gather_step(wide, half_ring - 2, n)

    mixed, mixed_b, log_total = pl.pallas_call(
        functools.partial(forward_kernel, blocks),
        out_shape=(
            jax.ShapeDtypeStruct((own_rows, Q_WIDE), f32),
            jax.ShapeDtypeStruct((own_rows, Q_WIDE), bf16),
            jax.ShapeDtypeStruct((8, GROUP * run_rows), f32),
        ),
        in_specs=[smem()] + [vmem()] * 4,
        out_specs=(vmem(),) * 3,
        scratch_shapes=[
            pltpu.VMEM((HALF_GROUPS * SLAB, GROUP * run_rows), f32),
            pltpu.VMEM((8 * HALF_GROUPS, GROUP * run_rows), f32),
            pltpu.VMEM((8 * HALF_GROUPS, GROUP * run_rows), f32),
        ],
        compiler_params=params(14 + n // 2),
        cost_estimate=cost(16),
    )(table, queries, kv_core, kv_other, rows_info)

    wide, mixed_b = lax.optimization_barrier((wide, mixed_b))
    wide = ring_gather_step(wide, half_ring - 1, n)
    attn_part = rounded(dot(mixed_b[:, :HALF_Q], w_all[:, PACK:], 1, 1))
    attn_came = x_swap(attn_part)
    wide, attn_came = lax.optimization_barrier((wide, attn_came))
    wide = ring_gather_step(wide, half_ring, n)
    x_f = x_own.astype(f32)
    hidden_own = x_f + (attn_part.astype(f32) + attn_came.astype(f32))
    hidden_other = core_swap(hidden_own)
    wide, hidden_other = lax.optimization_barrier((wide, hidden_other))
    wide = [wide[k] for k in range(n)]
    whole_tiles = ctx_rows % 16 == 0
    if not whole_tiles:
        wide_full = jnp.zeros((n,) + wide_block.shape, bf16)
        for k in range(n):
            wide_full = lax.dynamic_update_index_in_dim(wide_full, wide[k], ring_id(ctx_index, k, n), 0)
        wide = [wide_full.reshape(model, 3 * units)]

    def join(own, other):
        return jnp.where(
            core_index == 0, jnp.concatenate([own, other], 0), jnp.concatenate([other, own], 0)
        )

    normed_two, active, grads_wide, grad_two_own, grad_two_other = pl.pallas_call(
        functools.partial(feed_kernel, unit_tile=min(256, units)),
        out_shape=(
            jax.ShapeDtypeStruct((local_rows, model), bf16),
            jax.ShapeDtypeStruct((local_rows, units), bf16),
            jax.ShapeDtypeStruct((local_rows, 2 * units), bf16),
            jax.ShapeDtypeStruct((own_rows, model), f32),
            jax.ShapeDtypeStruct((own_rows, model), bf16),
        ),
        in_specs=[smem()] + [vmem()] * 4 + [pl.BlockSpec(memory_space=pl.ANY)] * len(wide),
        out_specs=(vmem(),) * 5,
        scratch_shapes=[
            pltpu.VMEM((model, 3 * units), bf16),
            pltpu.SemaphoreType.DMA((len(wide),)),
        ],
        compiler_params=params(),
        cost_estimate=cost(12),
    )(ring, hidden_own, hidden_other, gains, run_cotangent, *wide)
    shapes = (
        (jax.ShapeDtypeStruct((ctx_rows, 3 * units), bf16),) * n
        if whole_tiles
        else (jax.ShapeDtypeStruct((model, 3 * units), bf16),)
    )
    unit_tile = min(256, units)
    *d_terms, mlp_own, mlp_other = pl.pallas_call(
        functools.partial(feed_weights_kernel, n, len(wide)),
        out_shape=shapes
        + (
            jax.ShapeDtypeStruct((own_rows, model), f32),
            jax.ShapeDtypeStruct((own_rows, model), bf16),
        ),
        in_specs=[smem()] + [vmem()] * 4 + [pl.BlockSpec(memory_space=pl.ANY)] * len(wide),
        out_specs=(vmem(),) * (len(shapes) + 2),
        scratch_shapes=[
            pltpu.VMEM((model, unit_tile), bf16),
            pltpu.VMEM((model, units), bf16),
            pltpu.SemaphoreType.DMA((len(wide),)),
        ],
        compiler_params=params(),
        cost_estimate=cost(9),
    )(ring, normed_two, active, grads_wide, run_cotangent, *wide)
    if not whole_tiles:
        d_blocks = d_terms[0].reshape(n, ctx_rows, 3 * units)
        d_terms = [
            lax.dynamic_index_in_dim(d_blocks, ring_id(ctx_index, k, n), 0, keepdims=False) for k in range(n)
        ]
    def chip_sum(own, other):
        return rounded(own + core_swap(other).astype(f32))

    grad_two = chip_sum(grad_two_own, grad_two_other)
    grad_two_came, d_terms, mlp_own = lax.optimization_barrier((x_swap(grad_two), d_terms, mlp_own))
    d_came = None
    for step in range(1, half_ring - 2):
        d_came = ring_scatter_step(d_terms, d_came, step, n)
    output_chip = chip_sum(mlp_own, mlp_other)
    grad_hidden, grad_attn, grad_mixed, grad_gain_two = pl.pallas_call(
        hidden_grad_kernel,
        out_shape=(
            jax.ShapeDtypeStruct((own_rows, model), f32),
            jax.ShapeDtypeStruct((own_rows, model), bf16),
            jax.ShapeDtypeStruct((own_rows, Q_WIDE), bf16),
            jax.ShapeDtypeStruct((1, model), f32),
        ),
        in_specs=[smem()] + [vmem()] * 6,
        out_specs=(vmem(),) * 4,
        compiler_params=params(),
        cost_estimate=cost(5),
    )(ring, hidden_own, grad_two, grad_two_came, gains, run_cotangent, w_all)
    d_came, grad_mixed, output_chip = lax.optimization_barrier((d_came, grad_mixed, output_chip))
    d_came = ring_scatter_step(d_terms, d_came, half_ring - 2, n)

    dq_lin, dkv_core, dkv_other = pl.pallas_call(
        functools.partial(backward_kernel, blocks),
        out_shape=(
            jax.ShapeDtypeStruct((own_rows, Q_WIDE), bf16),
            jax.ShapeDtypeStruct(kv_core.shape, f32),
            jax.ShapeDtypeStruct(kv_core.shape, bf16),
        ),
        in_specs=[smem()] + [vmem()] * 9,
        out_specs=(vmem(),) * 3,
        scratch_shapes=[
            pltpu.VMEM((2 * SLAB, HEADS // 2 * run_rows), f32),
            pltpu.VMEM((own_rows, Q_WIDE), f32),
            pltpu.VMEM(kv_core.shape, f32),
            pltpu.VMEM((HEADS // 2 * run_rows, 2 * SLAB), bf16),
            pltpu.VMEM((HEADS // 2 * run_rows, 2 * SLAB), bf16),
        ],
        compiler_params=params(12 + 2 * n),
        cost_estimate=cost(24),
    )(table, queries, kv_core, kv_other, rows_info, mixed, log_total, grad_mixed, cosine, sine)

    def scatter_rows(part, crossing):
        cols = part.shape[1]
        split = part.reshape(n, 2, pair_rows, cols)
        mine = lax.dynamic_index_in_dim(split, core_index, 1, keepdims=False)
        theirs = lax.dynamic_index_in_dim(split, 1 - core_index, 1, keepdims=False)
        chip = mine.astype(f32) + core_swap(theirs).astype(f32)
        terms = [lax.dynamic_index_in_dim(chip, ring_id(ctx_index, k, n), 0, keepdims=False) for k in range(n)]
        came, (crossed,) = ring_scatter(terms, n, {2: x_swap(crossing)})
        total = terms[0] + came[0].astype(f32) + came[1].astype(f32)
        total_b = total.astype(bf16)
        opposite = core_swap(total_b)
        rows = jnp.where(
            core_index == 0,
            jnp.concatenate([total_b, opposite], 0),
            jnp.concatenate([opposite, total_b], 0),
        )
        quad = rows.reshape(2, 2, part_rows, cols)
        kept = lax.dynamic_index_in_dim(
            lax.dynamic_index_in_dim(quad, x_index, 0, keepdims=False), core_index, 0, keepdims=False
        )
        sent = lax.dynamic_index_in_dim(
            lax.dynamic_index_in_dim(quad, 1 - x_index, 0, keepdims=False), core_index, 0, keepdims=False
        )
        came = x_swap(sent)
        return rows, kept, came, crossed

    dkv_other, d_came, output_came = lax.optimization_barrier((dkv_other, d_came, x_swap(output_chip)))
    d_step = ring_scatter_step(d_terms, d_came, half_ring - 1, n)
    dkv = dkv_core + core_swap(dkv_other).astype(f32)
    dkv = dkv.reshape(n, own_rows, 2 * HALF_KV)
    dkv_own, (dkv_came, (d_came,)) = dkv[0], ring_scatter(dkv, n, {half_ring - 1: d_step})
    d_came = ring_scatter_step(d_terms, d_came, half_ring, n)
    output_own = (hidden_own + (output_chip.astype(f32) + output_came.astype(f32))).astype(bf16)
    output = as_dealt(join(output_own, core_swap(output_own)), pieces)
    normed_part, d_in = pl.pallas_call(
        last_kernel,
        out_shape=(
            jax.ShapeDtypeStruct((own_rows, model), bf16),
            jax.ShapeDtypeStruct((model, PACK + HALF_Q), bf16),
        ),
        in_specs=[vmem()] * (10 + len(dkv_came)),
        out_specs=(vmem(),) * 2,
        scratch_shapes=[pltpu.VMEM((own_rows, PACK), bf16)],
        compiler_params=params(56),
        cost_estimate=cost(5),
    )(dkv_own, dq_lin, cosine, sine, w_all, normed, x_own, grad_attn, mixed_b, grad_gain_two, *dkv_came)
    d_in, d_came = lax.optimization_barrier((d_in, d_came))
    in_rows, kept, came, normed_came = scatter_rows(d_in, normed_part)
    d_mlp = d_terms[0].astype(f32) + d_came[0].astype(f32) + d_came[1].astype(f32)
    grad_w_gate = d_mlp[:, :units]
    grad_w_up = d_mlp[:, units : 2 * units]
    grad_w_down = d_mlp[:, 2 * units :].T

    grad_w_query, grad_w_key, grad_w_value, grad_w_out, grad_gain = pl.pallas_call(
        finish_kernel,
        out_shape=(
            jax.ShapeDtypeStruct((part_rows, 2 * HALF_Q), f32),
            jax.ShapeDtypeStruct((part_rows, 2 * HALF_KV), f32),
            jax.ShapeDtypeStruct((part_rows, 2 * HALF_KV), f32),
            jax.ShapeDtypeStruct((part_rows, 2 * HALF_Q), f32),
            jax.ShapeDtypeStruct((part_rows, 1), f32),
        ),
        in_specs=[smem(), vmem(), vmem()],
        out_specs=(vmem(),) * 5,
        compiler_params=params(),
        cost_estimate=cost(2),
    )(x_index.reshape(1).astype(jnp.int32), kept, came)
    grad_w_out = grad_w_out.T
    grad_gain_attn = grad_gain[:, 0]

    grad_normed = normed_part.astype(f32) + normed_came.astype(f32)
    scale_one = lax.rsqrt(jnp.mean(x_f * x_f, -1, keepdims=True) + epsilon)
    input_rows, unused_gain = norm_backward(grad_normed, x_f * scale_one, scale_one, gains[:1])
    grad_inputs_own = (grad_hidden + input_rows).astype(bf16)
    grad_inputs = as_dealt(join(grad_inputs_own, core_swap(grad_inputs_own)), pieces)
    grad_gain_mlp = in_rows[:, PACK - 1].astype(f32)
    return (
        output,
        grad_inputs,
        grad_gain_attn,
        grad_w_query,
        grad_w_key,
        grad_w_value,
        grad_w_out,
        grad_gain_mlp,
        grad_w_gate,
        grad_w_up,
        grad_w_down,
    )


def solution(mesh):
    n = mesh.shape["ctx"]

    def body(*args):
        return on_device(n, args)

    return jax.shard_map(
        body,
        mesh=mesh,
        in_specs=(
            P("ctx", None),
            P("ctx", None),
            P(),
            P(),
            P(("ctx", "wa")),
            P(("ctx", "wa"), None),
            P(("ctx", "wa"), None),
            P(("ctx", "wa"), None),
            P(None, ("ctx", "wa")),
            P("ctx"),
            P("ctx", "wa"),
            P("ctx", "wa"),
            P("wa", "ctx"),
        ),
        out_specs=(
            P("ctx", None),
            P("ctx", None),
            P(("ctx", "wa")),
            P(("ctx", "wa"), None),
            P(("ctx", "wa"), None),
            P(("ctx", "wa"), None),
            P(None, ("ctx", "wa")),
            P("ctx"),
            P("ctx", "wa"),
            P("ctx", "wa"),
            P("wa", "ctx"),
        ),
        check_vma=False,
    )
```
